512 devices in a mesh: row: 16 (over x_hi, y), col: 32 (over x_lo, z, core).
Axes of the slice: x: 4 (x_hi: 2, x_lo: 2; x = x_hi * 2 + x_lo), y: 8, z: 8, core: 2. Of those that a mesh axis runs over, the one named last changes fastest.
Arguments:
- orbitals: bfloat16 [64, 96, 64, 128], P('col', None, 'row'), may hold values from -6 to 6
- potential: float32 [96, 64, 128], P('row'), may hold values from -1 to 1
- proj_points: int32 [128, 128], P('row'), may hold values from 0 to 49151
- projector: float32 [128, 128], P('row'), may hold values from -4 to 4
- strength: float32 [128], P('row'), may hold values from 0.5 to 2
- ritz_panel: bfloat16 [64, 64], P('row', 'col'), may hold values from -0.75 to 0.75
- panel_rows: int32 [64], replicated, may hold values from 0 to 63, each once
Outputs:
- rotated: float32 [64, 96, 64, 128], P('col', 'row')
The draws below stay inside these ranges and needn't reach their ends.
Inputs may be any that keep to these rules, and one draw needn't show every extreme that they name: `proj_points`: flat indices into the 6 x 64 x 128 cells of the slab of that atom, first dimension slowest. `panel_rows`: each state appears once.
All inputs are finite; a program needn't handle non-finite values.
Results may differ from the reference program's by a relative error of at most 0.0029.
Values may be sent and summed in bfloat16 or wider, within the bound.
No kernel may reach another device: no remote copies, remote signals or barrier semaphores. Data moves between devices by JAX's collectives and lax.ppermute only.
A program may use at most 128 MiB of HBM per device.

```python
import math
import jax
import jax.numpy as jnp
from jax import lax

SLAB = 6
GY = 64
GZ = 128
DEG = 3
ATOM_DEV = 8
NPP = 128
BLOCK = 64
GX = 96
ATOMS = 128


def with_ends(result, own_key, low, largest):
    dims = result.shape
    place = [jax.random.randint(jax.random.fold_in(own_key, axis), (), 0, dims[axis]) for axis in range(len(dims))]
    result = result.at[tuple(place)].set(low)
    longest = dims.index(max(dims))
    place[longest] = (place[longest] + 1) % dims[longest]
    return result.at[tuple(place)].set(largest)


def level_of(key, shape, pieces, least, largest):
    level = 1.0
    for axis_at, shards_of in pieces:
        draws = jax.random.uniform(jax.random.fold_in(jax.random.fold_in(key, 6), axis_at), (shards_of,), jnp.float32, least / len(pieces), largest / len(pieces))
        level = level * jnp.repeat(jnp.exp(draws), shape[axis_at] // shards_of).reshape((-1,) + (1,) * (len(shape) - 1 - axis_at))
    return level


def centred(own_key, dims, width, reach, shards=(), kind=jnp.bfloat16):
    gain = level_of(own_key, dims, shards, -0.22, 0.18) if shards else 1.0
    array = jax.random.normal(own_key, dims, jnp.float32) * width * gain
    return jnp.minimum(jnp.maximum(array, -reach), reach).astype(kind)


def setup_inputs(seed: int = 0) -> dict:
    seeds = jax.random.split(jax.random.key(seed), 8)
    return {
        "orbitals": centred(seeds[0], (BLOCK, GX, GY, GZ), 1.0, 6.0, ((0, 32), (2, 16))),
        "potential": jnp.clip(jax.random.uniform(seeds[1], (GX, GY, GZ), jnp.float32, -1.0, 1.0) * level_of(seeds[1], (GX, GY, GZ), ((0, 16),), -0.4, 0.0), -1.0, 1.0),
        "proj_points": with_ends(jax.random.randint(seeds[2], (ATOMS, NPP), 0, SLAB * GY * GZ), jax.random.fold_in(seeds[2], 1), 0, (SLAB * GY * GZ) - 1).astype(jnp.int32),
        "projector": centred(seeds[3], (ATOMS, NPP), 0.3, 4.0, ((0, 16),), jnp.float32),
        "strength": jnp.clip(jnp.exp(math.log(2.0) - 1.3862944 * jax.random.uniform(seeds[4], (ATOMS,), jnp.float32) ** level_of(seeds[4], (ATOMS,), ((0, 16),), -0.2, 0.2)), 0.5, 2.0),
        "ritz_panel": centred(seeds[5], (BLOCK, BLOCK), BLOCK ** -0.5, 0.75, ((0, 16), (1, 32))),
        "panel_rows": jax.random.permutation(seeds[6], BLOCK).astype(jnp.int32),
    }


STENCIL = (-5369.0 / 1800.0, 12.0 / 7.0, -15.0 / 56.0, 10.0 / 189.0, -1.0 / 112.0, 2.0 / 1925.0, -1.0 / 16632.0)
CENTER = 7.0
HALF_WIDTH = 5.0


def laplace(states, across):
    summed = (3.0 * STENCIL[0]) * states
    for offset in range(1, 7):
        forward, backward = across(offset)
        summed = summed + STENCIL[offset] * (forward + backward)
    for offset in range(1, 7):
        summed = summed + STENCIL[offset] * (jnp.roll(states, -offset, axis=2) + jnp.roll(states, offset, axis=2))
    for offset in range(1, 7):
        summed = summed + STENCIL[offset] * (jnp.roll(states, -offset, axis=3) + jnp.roll(states, offset, axis=3))
    return summed


def nonlocal_term(states, points, projector, strength):
    state_count = states.shape[0]
    flattened = states.reshape(state_count, -1)
    sampled = flattened[:, points]
    weights = jnp.sum(sampled * projector, axis=2) * strength
    spread = weights[:, :, None] * projector
    placed = jnp.zeros_like(flattened).at[:, points.reshape(-1)].add(spread.reshape(state_count, -1))
    return placed.reshape(states.shape)


def chebyshev(states, make_across, potential, points, projector, strength):
    def apply_ham(states_now):
        return -0.5 * laplace(states_now, make_across(states_now)) + potential * states_now + nonlocal_term(states_now, points, projector, strength)

    previous = states
    current = (apply_ham(states) - CENTER * states) / HALF_WIDTH
    for degree_step in range(DEG - 1):
        following = 2.0 * (apply_ham(current) - CENTER * current) / HALF_WIDTH - previous
        previous, current = current, following
    return current


def rolled(states_now):
    return lambda offset: (jnp.roll(states_now, -offset, axis=1), jnp.roll(states_now, offset, axis=1))


def reference(orbitals, potential, proj_points, projector, strength, ritz_panel, panel_rows):
    planes = SLAB * GY * GZ
    offsets = (jnp.arange(ATOMS, dtype=jnp.int32) // ATOM_DEV) * planes
    global_points = (proj_points + offsets[:, None]).astype(jnp.int32)

    def one_state(single):
        start = single.astype(jnp.float32)[None]
        return chebyshev(start, rolled, potential, global_points, projector, strength)[0].astype(jnp.bfloat16)

    filtered = lax.map(one_state, orbitals)
    coeffs = jnp.zeros((BLOCK, BLOCK), jnp.bfloat16).at[panel_rows].set(ritz_panel)
    return jnp.einsum("ij,ixyz->jxyz", coeffs.astype(jnp.float32), filtered.astype(jnp.float32), precision=lax.Precision.HIGHEST)
```

```python
import functools

import jax
import jax.numpy as jnp
import numpy as np
from jax import lax
from jax.experimental import pallas as pl
from jax.experimental.pallas import tpu as pltpu
from jax.sharding import PartitionSpec as P

F32 = jnp.float32
BF16 = jnp.bfloat16

STENCIL = (
    -5369.0 / 1800.0,
    12.0 / 7.0,
    -15.0 / 56.0,
    10.0 / 189.0,
    -1.0 / 112.0,
    2.0 / 1925.0,
    -1.0 / 16632.0,
)
CENTER = 7.0
HALF_WIDTH = 5.0

ROWS, COLS = 16, 32
SLAB, GY, GZ = 6, 64, 128
GX = ROWS * SLAB
YPART = GY // ROWS
WIDE = 3 * SLAB
ATOM_DEV = 8
SLAB_ROWS = SLAB * GY
SENT = 2 * WIDE + 1

SIDE = tuple(-0.5 * c for c in STENCIL)
DIAGONAL = -0.5 * 3.0 * STENCIL[0] - CENTER

VMEM = pl.BlockSpec(memory_space=pltpu.VMEM)
PARAMS = pltpu.CompilerParams(vmem_limit_bytes=40 * 1024 * 1024)


def circulant(size):
    whole = np.zeros((size, size), np.float32)
    for offset in range(1, 7):
        for i in range(size):
            whole[i, (i + offset) % size] += SIDE[offset]
            whole[i, (i - offset) % size] += SIDE[offset]
    high = whole.astype(jnp.bfloat16)
    low = (whole - high.astype(np.float32)).astype(jnp.bfloat16)
    return high, low


def stencil_matrices():
    high, low = circulant(GZ)
    along_z = np.block([[high, low], [high, low]])
    high, low = circulant(GY)
    along_y = np.block([[high, high], [low, low]])
    return jnp.asarray(along_z), jnp.asarray(along_y)


def call(kernel, outs, scratch=(), flops=0, bytes_accessed=0, specs=None):
    return pl.pallas_call(
        kernel,
        out_shape=outs,
        in_specs=specs,
        out_specs=jax.tree.map(lambda _: VMEM, outs),
        scratch_shapes=list(scratch),
        compiler_params=PARAMS,
        cost_estimate=pl.CostEstimate(
            flops=flops, bytes_accessed=bytes_accessed, transcendentals=0
        ),
    )


def pack_kernel(orbitals, panel, out):
    row = lax.axis_index("row")
    place = lax.broadcasted_iota(jnp.int32, (YPART, GZ), 1)
    stored = lax.broadcasted_iota(jnp.int32, (YPART, GZ), 0)
    here = jnp.where(place == stored + YPART * row, 1.0, 0.0)
    values = panel[...].astype(F32)
    first = jnp.sum(here * values[:, 0:1], axis=0, keepdims=True)
    second = jnp.sum(here * values[:, 1:2], axis=0, keepdims=True)
    line = lax.broadcasted_iota(jnp.int32, (YPART, GZ), 0)
    tile = jnp.where(line == 0, first, jnp.where(line == 1, second, 0.0)).astype(BF16)
    for target in range(ROWS):
        begin = (SLAB * target - SLAB) % GX
        for state in range(2):
            base = state * WIDE
            head = min(WIDE, GX - begin)
            out[target, base : base + head] = orbitals[state, begin : begin + head]
            if head < WIDE:
                out[target, base + head : base + WIDE] = orbitals[state, : WIDE - head]
        out[target, 2 * WIDE] = tile


def project_kernel(points, projector, strength, dense, gains):
    for atom in range(ATOM_DEV):
        at = points[atom : atom + 1, :]
        value = projector[atom : atom + 1, :]
        grid_row = lax.shift_right_logical(at, 7)
        lane = at & (GZ - 1)
        rows = jnp.where(
            lax.broadcasted_iota(jnp.int32, (SLAB_ROWS, GZ), 0) == grid_row, 1.0, 0.0
        ).astype(BF16)
        at_lane = lax.broadcasted_iota(jnp.int32, (GZ, GZ), 0) == lane
        high = value.astype(BF16).astype(F32)
        rest = value - high
        middle = rest.astype(BF16).astype(F32)
        low = rest - middle
        lanes = [jnp.where(at_lane, part, 0.0).astype(BF16) for part in (high, middle, low)]
        dense[atom] = lax.dot_general(
            jnp.concatenate([rows] * 3, axis=1),
            jnp.concatenate(lanes, axis=1),
            (((1,), (1,)), ((), ())),
            preferred_element_type=F32,
        )
        gains[atom : atom + 1, :] = jnp.full((1, GZ), strength[atom], F32)


def inside(planes, scale, potential, dense, gains, along_z, along_y, wide_z, summed_z, emit):
    partial = [[None] * ATOM_DEV for _ in range(2)]
    for p in range(SLAB):
        for state in range(2):
            value = planes(state, p)
            high = value.astype(BF16)
            low = (value - high.astype(F32)).astype(BF16)
            start = (state * SLAB + p) * GY
            wide_z[start : start + GY, 0:GZ] = high
            wide_z[start : start + GY, GZ : 2 * GZ] = low
        own = [planes(state, p) for state in range(2)]
        for atom in range(ATOM_DEV):
            weight = dense[atom, p * GY : (p + 1) * GY, :]
            for state in range(2):
                term = jnp.sum((weight * own[state]).reshape(GY // 8, 8, GZ), axis=0)
                before = partial[state][atom]
                partial[state][atom] = term if before is None else before + term
    summed_z[...] = jnp.dot(wide_z[...], along_z[...], preferred_element_type=F32)
    weights = []
    for state in range(2):
        lines = [jnp.sum(term, axis=0, keepdims=True) for term in partial[state]]
        total = jnp.sum(jnp.concatenate(lines, axis=0), axis=1, keepdims=True)
        weights.append(total * gains[...])
    for p in range(SLAB):
        both = jnp.concatenate(
            [
                jnp.concatenate(
                    [
                        wide_z[start : start + GY, 0:GZ],
                        wide_z[start : start + GY, GZ : 2 * GZ],
                    ],
                    axis=0,
                )
                for start in (p * GY, (SLAB + p) * GY)
            ],
            axis=1,
        )
        turned = jnp.dot(along_y[...], both, preferred_element_type=F32)
        turned = turned[:GY] + turned[GY:]
        level = DIAGONAL + potential[p]
        for state in range(2):
            start = (state * SLAB + p) * GY
            total = level * planes(state, p) + turned[:, state * GZ : (state + 1) * GZ]
            total = total + (
                summed_z[start : start + GY, 0:GZ] + summed_z[start : start + GY, GZ : 2 * GZ]
            )
            for atom in range(ATOM_DEV):
                total = (
                    total
                    + weights[state][atom : atom + 1, :] * dense[atom, p * GY : (p + 1) * GY, :]
                )
            for offset in range(1, 7):
                terms = [planes(state, q) for q in (p - offset, p + offset) if 0 <= q < SLAB]
                if terms:
                    total = total + SIDE[offset] * functools.reduce(jnp.add, terms)
            emit(state, p, scale * total)


def beside(below, above, state, p):
    total = None
    for offset in range(1, 7):
        if p - offset < 0:
            plane = below(state, SLAB + p - offset)
        else:
            plane = None
        if p + offset >= SLAB:
            other = above(state, p + offset - SLAB)
            plane = other if plane is None else plane + other
        if plane is not None:
            total = SIDE[offset] * plane if total is None else total + SIDE[offset] * plane
    return total


def first_kernel(
    received, potential, dense, gains, along_z, along_y,
    start_out, next_out, sent_out, panel_out, slabs, wide_z, summed_z,
):
    panel = jnp.zeros((YPART, GZ), F32)
    for source in range(ROWS):
        for state in range(2):
            slabs[state, :, source * YPART : (source + 1) * YPART, :] = received[
                source, state * WIDE : (state + 1) * WIDE
            ].astype(F32)
        panel = panel + received[source, 2 * WIDE].astype(F32)
    panel_out[0:YPART, :] = panel
    panel_out[YPART:8, :] = jnp.zeros((8 - YPART, GZ), F32)
    for state in range(2):
        start_out[state] = slabs[state, SLAB : 2 * SLAB]
    scale = 1.0 / HALF_WIDTH

    def emit(state, p, value):
        value = value + scale * beside(
            lambda s, q: slabs[s, q], lambda s, q: slabs[s, 2 * SLAB + q], state, p
        )
        next_out[state, p] = value
        sent_out[state, p] = value.astype(BF16)

    inside(
        lambda state, p: slabs[state, SLAB + p],
        scale, potential, dense, gains, along_z, along_y, wide_z, summed_z, emit,
    )


def inside_kernel(
    current, previous, potential, dense, gains, along_z, along_y, out, wide_z, summed_z
):
    def emit(state, p, value):
        out[state, p] = value - previous[state, p]

    inside(
        lambda state, p: current[state, p],
        2.0 / HALF_WIDTH, potential, dense, gains, along_z, along_y, wide_z, summed_z, emit,
    )


def joined(partial, below, above, state, p):
    return partial[state, p] + (2.0 / HALF_WIDTH) * beside(
        lambda s, q: below[s, q].astype(F32), lambda s, q: above[s, q].astype(F32), state, p
    )


def join_kernel(partial, below, above, next_out, sent_out):
    for p in range(SLAB):
        for state in range(2):
            value = joined(partial, below, above, state, p)
            next_out[state, p] = value
            sent_out[state, p] = value.astype(BF16)


def lane_below(half):
    return lax.broadcasted_iota(jnp.int32, (8, GZ), 1) < half


def last_kernel(partial, below, above, panel, out, slab):
    for p in range(SLAB):
        for state in range(2):
            slab[state, p * GY : (p + 1) * GY, :] = joined(partial, below, above, state, p)
    left = lane_below(GZ // 2)
    for target in range(COLS):
        tiles = [slab[state, 8 * target : 8 * target + 8, :] for state in range(2)]
        shared = 8 * (COLS + target // 2)
        first, second = (slab[state, shared : shared + 8, :] for state in range(2))
        if target % 2 == 0:
            tiles.append(jnp.where(left, first, pltpu.roll(second, GZ // 2, 1)))
        else:
            tiles.append(jnp.where(left, pltpu.roll(first, GZ // 2, 1), second))
        tiles.append(panel[...])
        out[target] = jnp.concatenate(tiles, axis=0).astype(BF16)


def rotate_kernel(received, panel_rows, out):
    left = lane_below(GZ // 2)
    columns = [[], []]
    turned = [[], []]
    for source in range(COLS):
        chunk = received[source].astype(F32)
        for state in range(2):
            shared = chunk[16:24]
            if state == 1:
                shared = pltpu.roll(shared, GZ // 2, 1)
            columns[state].append(
                jnp.concatenate([chunk[8 * state : 8 * state + 8], shared], axis=1)
            )
            turned[state].append(
                jnp.broadcast_to(chunk[24 + state : 25 + state, :64], (8, 64))
            )
    states = jnp.concatenate(columns[0] + columns[1], axis=0).astype(BF16)
    wanted = jnp.concatenate(turned[0] + turned[1], axis=0).astype(BF16)
    size = 16 * COLS
    order = lax.broadcasted_iota(jnp.int32, (size, 64), 0)
    half = 8 * COLS
    state_of = jnp.where(order < half, (order >> 3) * 2, ((order - half) >> 3) * 2 + 1)
    stored = jnp.where(panel_rows[...] == state_of, 1.0, 0.0).astype(BF16)
    spread = lax.dot_general(
        wanted, stored, (((1,), (1,)), ((), ())), preferred_element_type=F32
    )
    same = (
        lax.broadcasted_iota(jnp.int32, (size, size), 0) & 7
    ) == (lax.broadcasted_iota(jnp.int32, (size, size), 1) & 7)
    spread = jnp.where(same, spread, 0.0).astype(BF16)
    rotated = jnp.dot(spread, states, preferred_element_type=F32)
    for target in range(COLS):
        pair = [rotated[start : start + 8] for start in (8 * target, half + 8 * target)]
        shared = jnp.where(left, pair[0][:, GZ:], pltpu.roll(pair[1][:, GZ:], GZ // 2, 1))
        out[target] = jnp.concatenate([pair[0][:, :GZ], pair[1][:, :GZ], shared], axis=0).astype(
            BF16
        )


def place_kernel(received, out):
    left = lane_below(GZ // 2)
    for pair in range(COLS // 2):
        chunks = [received[2 * pair + k].astype(F32) for k in range(2)]
        for k in range(2):
            at = 8 * (2 * pair + k)
            for state in range(2):
                out[state, at : at + 8, :] = chunks[k][8 * state : 8 * state + 8]
        even, odd = (chunk[16:24] for chunk in chunks)
        at = 8 * (COLS + pair)
        out[0, at : at + 8, :] = jnp.where(left, even, pltpu.roll(odd, GZ // 2, 1))
        out[1, at : at + 8, :] = jnp.where(left, pltpu.roll(even, GZ // 2, 1), odd)


def per_device(orbitals, potential, proj_points, projector, strength, ritz_panel, panel_rows):
    shape = jax.ShapeDtypeStruct
    slab_f32 = shape((2, SLAB, GY, GZ), F32)
    slab_bf16 = shape((2, SLAB, GY, GZ), BF16)
    along_z, along_y = stencil_matrices()
    work = [
        pltpu.VMEM((2 * SLAB_ROWS, 2 * GZ), BF16),
        pltpu.VMEM((2 * SLAB_ROWS, 2 * GZ), F32),
    ]

    packed = call(pack_kernel, shape((ROWS, SENT, YPART, GZ), BF16), specs=[VMEM] * 2)(
        orbitals, ritz_panel
    )
    regrouped = lax.all_to_all(packed, "row", split_axis=0, concat_axis=0, tiled=True)
    dense, gains = call(
        project_kernel,
        (shape((ATOM_DEV, SLAB_ROWS, GZ), F32), shape((8, GZ), F32)),
        specs=[VMEM, VMEM, pl.BlockSpec(memory_space=pltpu.SMEM)],
        flops=1_000_000_000,
        bytes_accessed=1_600_000,
    )(proj_points, projector, strength)

    fixed = (potential, dense, gains, along_z, along_y)
    start, current, sent, panel = call(
        first_kernel,
        (slab_f32, slab_f32, slab_bf16, shape((8, GZ), F32)),
        scratch=[pltpu.VMEM((2, WIDE, GY, GZ), F32)] + work,
        specs=[VMEM] * 6,
    )(regrouped, *fixed)

    up = [(i, (i + 1) % ROWS) for i in range(ROWS)]
    down = [((i + 1) % ROWS, i) for i in range(ROWS)]
    previous = start
    for step in range(2):
        below = lax.ppermute(sent, "row", up)
        above = lax.ppermute(sent, "row", down)
        partial = call(
            inside_kernel,
            slab_f32,
            scratch=work,
            specs=[VMEM] * 7,
            flops=2_000_000_000,
            bytes_accessed=3_000_000,
        )(current, previous, *fixed)
        if step == 0:
            previous = current
            current, sent = call(join_kernel, (slab_f32, slab_bf16), specs=[VMEM] * 3)(
                partial, below, above
            )
    layered = call(
        last_kernel,
        shape((COLS, 32, GZ), BF16),
        scratch=[pltpu.VMEM((2, SLAB_ROWS, GZ), F32)],
        specs=[VMEM] * 4,
    )(partial, below, above, panel)
    columns = lax.all_to_all(layered, "col", split_axis=0, concat_axis=0, tiled=True)
    turned = call(rotate_kernel, shape((COLS, 24, GZ), BF16), specs=[VMEM] * 2)(
        columns, panel_rows.reshape(1, -1)
    )
    result = lax.all_to_all(turned, "col", split_axis=0, concat_axis=0, tiled=True)
    whole = call(place_kernel, shape((2, SLAB_ROWS, GZ), F32), specs=[VMEM])(result)
    return whole.reshape(2, SLAB, GY, GZ)


def solution(mesh):
    placed = (
        P("col", None, "row", None),
        P("row", None, None),
        P("row", None),
        P("row", None),
        P("row"),
        P("row", "col"),
        P(),
    )
    return jax.shard_map(
        per_device,
        mesh=mesh,
        in_specs=placed,
        out_specs=P("col", "row", None, None),
        check_vma=False,
    )
```

```python
import functools

import jax
import jax.numpy as jnp
import numpy as np
from jax import lax
from jax.experimental import pallas as pl
from jax.experimental.pallas import tpu as pltpu
from jax.sharding import PartitionSpec as P

F32 = jnp.float32
BF16 = jnp.bfloat16

STENCIL = (
    -5369.0 / 1800.0,
    12.0 / 7.0,
    -15.0 / 56.0,
    10.0 / 189.0,
    -1.0 / 112.0,
    2.0 / 1925.0,
    -1.0 / 16632.0,
)
CENTER = 7.0
HALF_WIDTH = 5.0

ROWS, COLS = 16, 32
SLAB, GY, GZ = 6, 64, 128
GX = ROWS * SLAB
YPART = GY // ROWS
WIDE = 5 * SLAB
REACH = (WIDE - SLAB) // 2
ATOM_DEV = 8
SLAB_ROWS = SLAB * GY
SENT = 2 * WIDE + 1
NEXT_ROWS = SLAB_ROWS + 6 * ATOM_DEV

SIDE = tuple(-0.5 * c for c in STENCIL)
DIAGONAL = -0.5 * 3.0 * STENCIL[0] - CENTER

VMEM = pl.BlockSpec(memory_space=pltpu.VMEM)
PARAMS = pltpu.CompilerParams(vmem_limit_bytes=40 * 1024 * 1024)


def circulant(size):
    whole = np.zeros((size, size), np.float32)
    for offset in range(1, 7):
        for i in range(size):
            whole[i, (i + offset) % size] += SIDE[offset]
            whole[i, (i - offset) % size] += SIDE[offset]
    high = whole.astype(jnp.bfloat16)
    low = (whole - high.astype(np.float32)).astype(jnp.bfloat16)
    return high, low


def stencil_matrices():
    high, low = circulant(GZ)
    along_z = np.block([[high, low], [high, low]])
    high, low = circulant(GY)
    along_y = np.block([[high, high], [low, low]])
    return jnp.asarray(along_z), jnp.asarray(along_y)


def call(kernel, outs, scratch=(), flops=0, bytes_accessed=0, specs=None):
    return pl.pallas_call(
        kernel,
        out_shape=outs,
        in_specs=specs,
        out_specs=jax.tree.map(lambda _: VMEM, outs),
        scratch_shapes=list(scratch),
        compiler_params=PARAMS,
        cost_estimate=pl.CostEstimate(
            flops=flops, bytes_accessed=bytes_accessed, transcendentals=0
        ),
    )


def pack_pieces():
    pieces = []
    for target in range(ROWS):
        begin = (SLAB * target - REACH) % GX
        head = min(WIDE, GX - begin)
        for state in range(2):
            pieces.append((target, state, begin, state * WIDE, head))
            if head < WIDE:
                pieces.append((target, state, 0, state * WIDE + head, WIDE - head))
    return pieces


def pack_kernel(orbitals, panel, out, sems):
    copies = []
    for i, (target, state, begin, at, count) in enumerate(pack_pieces()):
        copies.append(
            pltpu.make_async_copy(
                orbitals.at[state, pl.ds(begin, count)],
                out.at[target, pl.ds(at, count)],
                sems.at[i],
            )
        )
        copies[-1].start()
    row = lax.axis_index("row")
    place = lax.broadcasted_iota(jnp.int32, (2, GZ), 1)
    values = panel[...].astype(F32)
    tile = jnp.zeros((2, GZ), F32)
    for k in range(YPART):
        tile = jnp.where(place == YPART * row + k, values[:, k : k + 1], tile)
    tile = jnp.concatenate([tile, jnp.zeros((YPART - 2, GZ), F32)], axis=0).astype(BF16)
    for target in range(ROWS):
        out[target, 2 * WIDE] = tile
    for copy in copies:
        copy.wait()


def three_parts(value):
    high = value.astype(BF16).astype(F32)
    rest = value - high
    middle = rest.astype(BF16).astype(F32)
    return high, middle, rest - middle


def next_kernel(potential, points, projector, strength, out):
    for p in range(SLAB):
        out[p * GY : (p + 1) * GY, :] = potential[p].astype(BF16)
    gains = jnp.concatenate(
        [jnp.full((1, GZ), strength[atom], F32) for atom in range(ATOM_DEV)], axis=0
    )
    lane = lax.broadcasted_iota(jnp.int32, (ATOM_DEV, GZ), 1)
    high, middle, low = three_parts(gains)
    gains = jnp.where(lane == 0, high, jnp.where(lane == 1, middle, low))
    at = points[...]
    tail = [
        lax.shift_right_logical(at, 8).astype(F32),
        (at & 255).astype(F32),
        *three_parts(projector[...]),
        gains,
    ]
    out[SLAB_ROWS:NEXT_ROWS, :] = jnp.concatenate(tail, axis=0).astype(BF16)


def densify(grid_row, lane, parts, store):
    for atom in range(ATOM_DEV):
        rows = jnp.where(
            lax.broadcasted_iota(jnp.int32, (SLAB_ROWS, GZ), 0) == grid_row[atom : atom + 1, :],
            1.0,
            0.0,
        ).astype(BF16)
        at_lane = lax.broadcasted_iota(jnp.int32, (GZ, GZ), 0) == lane[atom : atom + 1, :]
        lanes = [
            jnp.where(at_lane, part[atom : atom + 1, :], 0.0).astype(BF16) for part in parts
        ]
        store(
            atom,
            lax.dot_general(
                jnp.concatenate([rows] * 3, axis=1),
                jnp.concatenate(lanes, axis=1),
                (((1,), (1,)), ((), ())),
                preferred_element_type=F32,
            ),
        )


def project_kernel(points, projector, strength, dense, gains):
    at = points[...]

    def store(atom, value):
        dense[atom] = value

    densify(lax.shift_right_logical(at, 7), at & (GZ - 1), three_parts(projector[...]), store)
    for atom in range(ATOM_DEV):
        gains[atom : atom + 1, :] = jnp.full((1, GZ), strength[atom], F32)


def project_next_kernel(below, above, dense, gains):
    for side, received in enumerate((below, above)):
        tail = received[SLAB_ROWS:NEXT_ROWS, :].astype(F32)
        pieces = [tail[ATOM_DEV * i : ATOM_DEV * (i + 1)] for i in range(6)]
        top, bottom = (piece.astype(jnp.int32) for piece in pieces[:2])

        def store(atom, value):
            dense[side, atom] = value

        densify(
            top * 2 + lax.shift_right_logical(bottom, 7), bottom & (GZ - 1), pieces[2:5], store
        )
        gain = pieces[5]
        gain = gain[:, 0:1] + (gain[:, 1:2] + gain[:, 2:3])
        gains[side] = jnp.broadcast_to(gain, (ATOM_DEV, GZ))


def apply(planes, slabs, reach, scale, along_z, along_y, wide_z, summed_z, emit):
    count = SLAB * len(slabs)
    weights = []
    for s, (_, dense, gains) in enumerate(slabs):
        partial = [[None] * ATOM_DEV for _ in range(2)]
        for p in range(SLAB):
            own = [planes(state, SLAB * s + p) for state in range(2)]
            for state in range(2):
                high = own[state].astype(BF16)
                low = (own[state] - high.astype(F32)).astype(BF16)
                start = (state * count + SLAB * s + p) * GY
                wide_z[start : start + GY, 0:GZ] = high
                wide_z[start : start + GY, GZ : 2 * GZ] = low
            for atom in range(ATOM_DEV):
                weight = dense[atom, p * GY : (p + 1) * GY, :]
                for state in range(2):
                    term = jnp.sum((weight * own[state]).reshape(GY // 8, 8, GZ), axis=0)
                    before = partial[state][atom]
                    partial[state][atom] = term if before is None else before + term
        lines = []
        for state in range(2):
            sums = [jnp.sum(term, axis=0, keepdims=True) for term in partial[state]]
            total = jnp.sum(jnp.concatenate(sums, axis=0), axis=1, keepdims=True)
            lines.append(total * gains)
        weights.append(lines)
    height = 2 * count * GY
    summed_z[0:height, :] = jnp.dot(
        wide_z[0:height, :], along_z[...], preferred_element_type=F32
    )
    for s, (potential, dense, _) in enumerate(slabs):
        for q in range(SLAB):
            p = SLAB * s + q
            both = jnp.concatenate(
                [
                    jnp.concatenate(
                        [
                            wide_z[start : start + GY, 0:GZ],
                            wide_z[start : start + GY, GZ : 2 * GZ],
                        ],
                        axis=0,
                    )
                    for start in (p * GY, (count + p) * GY)
                ],
                axis=1,
            )
            turned = jnp.dot(along_y[...], both, preferred_element_type=F32)
            turned = turned[:GY] + turned[GY:]
            level = DIAGONAL + potential(q)
            for state in range(2):
                start = (state * count + p) * GY
                total = level * planes(state, p) + turned[:, state * GZ : (state + 1) * GZ]
                total = total + (
                    summed_z[start : start + GY, 0:GZ]
                    + summed_z[start : start + GY, GZ : 2 * GZ]
                )
                for atom in range(ATOM_DEV):
                    total = (
                        total
                        + weights[s][state][atom : atom + 1, :]
                        * dense[atom, q * GY : (q + 1) * GY, :]
                    )
                for offset in range(1, 7):
                    terms = [
                        planes(state, k)
                        for k in (p - offset, p + offset)
                        if -reach <= k < count + reach
                    ]
                    if terms:
                        total = total + SIDE[offset] * functools.reduce(jnp.add, terms)
                emit(state, p, scale * total)


def beside(below, above, state, p):
    total = None
    for offset in range(1, 7):
        if p - offset < 0:
            plane = below(state, SLAB + p - offset)
        else:
            plane = None
        if p + offset >= SLAB:
            other = above(state, p + offset - SLAB)
            plane = other if plane is None else plane + other
        if plane is not None:
            total = SIDE[offset] * plane if total is None else total + SIDE[offset] * plane
    return total


def first_kernel(
    received, below, above, next_dense, next_gains, potential, dense, gains, along_z, along_y,
    previous_out, current_out, sent_out, panel_out, start, first, wide_z, summed_z,
):
    panel = jnp.zeros((YPART, GZ), F32)
    for source in range(ROWS):
        for state in range(2):
            start[state, :, source * YPART : (source + 1) * YPART, :] = received[
                source, state * WIDE : (state + 1) * WIDE
            ].astype(F32)
        panel = panel + received[source, 2 * WIDE].astype(F32)
    panel_out[0:YPART, :] = panel
    panel_out[YPART:8, :] = jnp.zeros((8 - YPART, GZ), F32)

    own = (lambda q: potential[q], dense, gains[...])
    slabs = [
        (lambda q: below[q * GY : (q + 1) * GY, :].astype(F32), next_dense.at[0], next_gains[0]),
        own,
        (lambda q: above[q * GY : (q + 1) * GY, :].astype(F32), next_dense.at[1], next_gains[1]),
    ]

    def emit_first(state, p, value):
        first[state, p] = value
        if SLAB <= p < 2 * SLAB:
            previous_out[state, p - SLAB] = value

    apply(
        lambda state, p: start[state, SLAB + p],
        slabs, SLAB, 1.0 / HALF_WIDTH, along_z, along_y, wide_z, summed_z, emit_first,
    )

    def emit_second(state, p, value):
        value = value - start[state, REACH + p]
        current_out[state, p] = value
        sent_out[state, p] = value.astype(BF16)

    apply(
        lambda state, p: first[state, SLAB + p],
        [own], SLAB, 2.0 / HALF_WIDTH, along_z, along_y, wide_z, summed_z, emit_second,
    )


def inside_kernel(
    current, previous, potential, dense, gains, along_z, along_y, out, wide_z, summed_z
):
    def emit(state, p, value):
        out[state, p] = value - previous[state, p]

    apply(
        lambda state, p: current[state, p],
        [(lambda q: potential[q], dense, gains[...])],
        0, 2.0 / HALF_WIDTH, along_z, along_y, wide_z, summed_z, emit,
    )


def joined(partial, below, above, state, p):
    return partial[state, p] + (2.0 / HALF_WIDTH) * beside(
        lambda s, q: below[s, q].astype(F32), lambda s, q: above[s, q].astype(F32), state, p
    )


def lane_below(half):
    return lax.broadcasted_iota(jnp.int32, (8, GZ), 1) < half


def last_kernel(partial, below, above, panel, out, slab):
    for p in range(SLAB):
        for state in range(2):
            slab[state, p * GY : (p + 1) * GY, :] = joined(partial, below, above, state, p)
    left = lane_below(GZ // 2)
    for target in range(COLS):
        tiles = [slab[state, 8 * target : 8 * target + 8, :] for state in range(2)]
        shared = 8 * (COLS + target // 2)
        first, second = (slab[state, shared : shared + 8, :] for state in range(2))
        if target % 2 == 0:
            tiles.append(jnp.where(left, first, pltpu.roll(second, GZ // 2, 1)))
        else:
            tiles.append(jnp.where(left, pltpu.roll(first, GZ // 2, 1), second))
        tiles.append(panel[...])
        out[target] = jnp.concatenate(tiles, axis=0).astype(BF16)


def rotate_kernel(received, panel_rows, out):
    left = lane_below(GZ // 2)
    columns = [[], []]
    turned = [[], []]
    for source in range(COLS):
        chunk = received[source].astype(F32)
        for state in range(2):
            shared = chunk[16:24]
            if state == 1:
                shared = pltpu.roll(shared, GZ // 2, 1)
            columns[state].append(
                jnp.concatenate([chunk[8 * state : 8 * state + 8], shared], axis=1)
            )
            turned[state].append(
                jnp.broadcast_to(chunk[24 + state : 25 + state, :64], (8, 64))
            )
    states = jnp.concatenate(columns[0] + columns[1], axis=0).astype(BF16)
    wanted = jnp.concatenate(turned[0] + turned[1], axis=0).astype(BF16)
    size = 16 * COLS
    order = lax.broadcasted_iota(jnp.int32, (size, 64), 0)
    half = 8 * COLS
    state_of = jnp.where(order < half, (order >> 3) * 2, ((order - half) >> 3) * 2 + 1)
    stored = jnp.where(panel_rows[...] == state_of, 1.0, 0.0).astype(BF16)
    spread = lax.dot_general(
        wanted, stored, (((1,), (1,)), ((), ())), preferred_element_type=F32
    )
    same = (
        lax.broadcasted_iota(jnp.int32, (size, size), 0) & 7
    ) == (lax.broadcasted_iota(jnp.int32, (size, size), 1) & 7)
    spread = jnp.where(same, spread, 0.0).astype(BF16)
    rotated = jnp.dot(spread, states, preferred_element_type=F32)
    for target in range(COLS):
        pair = [rotated[start : start + 8] for start in (8 * target, half + 8 * target)]
        shared = jnp.where(left, pair[0][:, GZ:], pltpu.roll(pair[1][:, GZ:], GZ // 2, 1))
        out[target] = jnp.concatenate([pair[0][:, :GZ], pair[1][:, :GZ], shared], axis=0).astype(
            BF16
        )


def place_kernel(received, out):
    left = lane_below(GZ // 2)
    for pair in range(COLS // 2):
        chunks = [received[2 * pair + k].astype(F32) for k in range(2)]
        for k in range(2):
            at = 8 * (2 * pair + k)
            for state in range(2):
                out[state, at : at + 8, :] = chunks[k][8 * state : 8 * state + 8]
        even, odd = (chunk[16:24] for chunk in chunks)
        at = 8 * (COLS + pair)
        out[0, at : at + 8, :] = jnp.where(left, even, pltpu.roll(odd, GZ // 2, 1))
        out[1, at : at + 8, :] = jnp.where(left, pltpu.roll(even, GZ // 2, 1), odd)


def per_device(orbitals, potential, proj_points, projector, strength, ritz_panel, panel_rows):
    shape = jax.ShapeDtypeStruct
    slab_f32 = shape((2, SLAB, GY, GZ), F32)
    slab_bf16 = shape((2, SLAB, GY, GZ), BF16)
    along_z, along_y = stencil_matrices()
    smem = pl.BlockSpec(memory_space=pltpu.SMEM)
    up = [(i, (i + 1) % ROWS) for i in range(ROWS)]
    down = [((i + 1) % ROWS, i) for i in range(ROWS)]

    def work(slabs):
        height = 2 * slabs * SLAB_ROWS
        return [pltpu.VMEM((height, 2 * GZ), BF16), pltpu.VMEM((height, 2 * GZ), F32)]

    def beside_of(array):
        return lax.ppermute(array, "row", up), lax.ppermute(array, "row", down)

    packed = call(
        pack_kernel,
        shape((ROWS, SENT, YPART, GZ), BF16),
        scratch=[pltpu.SemaphoreType.DMA((len(pack_pieces()),))],
        specs=[pl.BlockSpec(memory_space=pl.ANY), VMEM],
    )(orbitals, ritz_panel.T)
    regrouped = lax.all_to_all(packed, "row", split_axis=0, concat_axis=0, tiled=True)
    given = call(
        next_kernel,
        shape((NEXT_ROWS, GZ), BF16),
        specs=[VMEM] * 3 + [smem],
        flops=1_000_000,
        bytes_accessed=300_000,
    )(potential, proj_points, projector, strength)
    next_below, next_above = beside_of(given)
    dense, gains = call(
        project_kernel,
        (shape((ATOM_DEV, SLAB_ROWS, GZ), F32), shape((ATOM_DEV, GZ), F32)),
        specs=[VMEM, VMEM, smem],
        flops=1_000_000_000,
        bytes_accessed=1_600_000,
    )(proj_points, projector, strength)
    next_dense, next_gains = call(
        project_next_kernel,
        (shape((2, ATOM_DEV, SLAB_ROWS, GZ), F32), shape((2, ATOM_DEV, GZ), F32)),
        specs=[VMEM] * 2,
        flops=2_000_000_000,
        bytes_accessed=3_200_000,
    )(next_below, next_above)

    fixed = (potential, dense, gains, along_z, along_y)
    previous, current, sent, panel = call(
        first_kernel,
        (slab_f32, slab_f32, slab_bf16, shape((8, GZ), F32)),
        scratch=[pltpu.VMEM((2, WIDE, GY, GZ), F32), pltpu.VMEM((2, 3 * SLAB, GY, GZ), F32)]
        + work(3),
        specs=[VMEM] * 10,
    )(regrouped, next_below, next_above, next_dense, next_gains, *fixed)
    below, above = beside_of(sent)
    partial = call(
        inside_kernel,
        slab_f32,
        scratch=work(1),
        specs=[VMEM] * 7,
        flops=2_000_000_000,
        bytes_accessed=3_000_000,
    )(current, previous, *fixed)
    layered = call(
        last_kernel,
        shape((COLS, 32, GZ), BF16),
        scratch=[pltpu.VMEM((2, SLAB_ROWS, GZ), F32)],
        specs=[VMEM] * 4,
    )(partial, below, above, panel)
    columns = lax.all_to_all(layered, "col", split_axis=0, concat_axis=0, tiled=True)
    turned = call(rotate_kernel, shape((COLS, 24, GZ), BF16), specs=[VMEM] * 2)(
        columns, panel_rows.reshape(1, -1)
    )
    result = lax.all_to_all(turned, "col", split_axis=0, concat_axis=0, tiled=True)
    whole = call(place_kernel, shape((2, SLAB_ROWS, GZ), F32), specs=[VMEM])(result)
    return whole.reshape(2, SLAB, GY, GZ)


def solution(mesh):
    placed = (
        P("col", None, "row", None),
        P("row", None, None),
        P("row", None),
        P("row", None),
        P("row"),
        P("row", "col"),
        P(),
    )
    return jax.shard_map(
        per_device,
        mesh=mesh,
        in_specs=placed,
        out_specs=P("col", "row", None, None),
        check_vma=False,
    )
```

```python
import functools

import jax
import jax.numpy as jnp
import numpy as np
from jax import lax
from jax.experimental import pallas as pl
from jax.experimental.pallas import tpu as pltpu
from jax.sharding import PartitionSpec as P

F32 = jnp.float32
BF16 = jnp.bfloat16

STENCIL = (
    -5369.0 / 1800.0,
    12.0 / 7.0,
    -15.0 / 56.0,
    10.0 / 189.0,
    -1.0 / 112.0,
    2.0 / 1925.0,
    -1.0 / 16632.0,
)
CENTER = 7.0
HALF_WIDTH = 5.0

ROWS, COLS = 16, 32
SLAB, GY, GZ = 6, 64, 128
GX = ROWS * SLAB
YPART = GY // ROWS
WIDE = 3 * SLAB
ATOM_DEV = 8
SLAB_ROWS = SLAB * GY
SENT = 2 * WIDE + 1
HALF = ROWS // 2
PIECE = SLAB_ROWS // COLS // 4
OTHER_ROWS = SLAB_ROWS + 3 * ATOM_DEV

SIDE = tuple(-0.5 * c for c in STENCIL)
DIAGONAL = -0.5 * 3.0 * STENCIL[0] - CENTER

VMEM = pl.BlockSpec(memory_space=pltpu.VMEM)
PARAMS = pltpu.CompilerParams(vmem_limit_bytes=40 * 1024 * 1024)


def circulant(size):
    whole = np.zeros((size, size), np.float32)
    for offset in range(1, 7):
        for i in range(size):
            whole[i, (i + offset) % size] += SIDE[offset]
            whole[i, (i - offset) % size] += SIDE[offset]
    high = whole.astype(jnp.bfloat16)
    low = (whole - high.astype(np.float32)).astype(jnp.bfloat16)
    return high, low


def stencil_matrices():
    high, low = circulant(GZ)
    along_z = np.block([[high, low], [high, low]])
    high, low = circulant(GY)
    along_y = np.block([[high, high], [low, low]])
    return jnp.asarray(along_z), jnp.asarray(along_y)


def call(kernel, outs, scratch=(), flops=0, bytes_accessed=0, specs=None):
    return pl.pallas_call(
        kernel,
        out_shape=outs,
        in_specs=specs,
        out_specs=jax.tree.map(lambda _: VMEM, outs),
        scratch_shapes=list(scratch),
        compiler_params=PARAMS,
        cost_estimate=pl.CostEstimate(
            flops=flops, bytes_accessed=bytes_accessed, transcendentals=0
        ),
    )


def pack_kernel(orbitals, panel, out):
    row = lax.axis_index("row")
    place = lax.broadcasted_iota(jnp.int32, (2, GZ), 1)
    values = panel[...].astype(F32)
    tile = jnp.zeros((2, GZ), F32)
    for k in range(YPART):
        tile = jnp.where(place == YPART * row + k, values[:, k : k + 1], tile)
    tile = jnp.concatenate([tile, jnp.zeros((YPART - 2, GZ), F32)], axis=0).astype(BF16)
    for target in range(ROWS):
        state = target // HALF
        for index, slab in enumerate((target, target ^ HALF)):
            begin = (SLAB * slab - SLAB) % GX
            base = index * WIDE
            head = min(WIDE, GX - begin)
            out[target, base : base + head] = orbitals[state, begin : begin + head]
            if head < WIDE:
                out[target, base + head : base + WIDE] = orbitals[state, : WIDE - head]
        out[target, 2 * WIDE] = tile


def other_kernel(potential, points, projector, strength, out):
    for p in range(SLAB):
        out[p * GY : (p + 1) * GY, :] = potential[p]
    out[SLAB_ROWS : SLAB_ROWS + 8, :] = points[...].astype(F32)
    out[SLAB_ROWS + 8 : SLAB_ROWS + 16, :] = projector[...]
    for atom in range(ATOM_DEV):
        at = SLAB_ROWS + 16 + atom
        out[at : at + 1, :] = jnp.full((1, GZ), strength[atom], F32)


def densify(points, projector, dense):
    grid_row, lane = lax.shift_right_logical(points, 7), points & (GZ - 1)
    high = projector.astype(BF16).astype(F32)
    parts = (high, projector - high)
    for atom in range(ATOM_DEV):
        rows = jnp.where(
            lax.broadcasted_iota(jnp.int32, (SLAB_ROWS, GZ), 0) == grid_row[atom : atom + 1, :],
            1.0,
            0.0,
        ).astype(BF16)
        at_lane = lax.broadcasted_iota(jnp.int32, (GZ, GZ), 0) == lane[atom : atom + 1, :]
        lanes = [
            jnp.where(at_lane, part[atom : atom + 1, :], 0.0).astype(BF16) for part in parts
        ]
        dense[atom] = lax.dot_general(
            jnp.concatenate([rows] * 2, axis=1),
            jnp.concatenate(lanes, axis=1),
            (((1,), (1,)), ((), ())),
            preferred_element_type=F32,
        )


def project_kernel(points, projector, strength, dense, gains):
    densify(points[...], projector[...], dense)
    for atom in range(ATOM_DEV):
        gains[atom : atom + 1, :] = jnp.full((1, GZ), strength[atom], F32)


def project_other_kernel(given, dense, gains):
    points = given[SLAB_ROWS : SLAB_ROWS + 8, :].astype(jnp.int32)
    densify(points, given[SLAB_ROWS + 8 : SLAB_ROWS + 16, :], dense)
    gains[...] = given[SLAB_ROWS + 16 : SLAB_ROWS + 24, :]


def apply(planes, reach, scale, potentials, denses, gains, along_z, along_y, wide_z, summed_z, emit):
    weights = []
    for slab in range(2):
        partial = [None] * ATOM_DEV
        for p in range(SLAB):
            value = planes(slab, p)
            high = value.astype(BF16)
            low = (value - high.astype(F32)).astype(BF16)
            start = (slab * SLAB + p) * GY
            wide_z[start : start + GY, 0:GZ] = high
            wide_z[start : start + GY, GZ : 2 * GZ] = low
            for atom in range(ATOM_DEV):
                weight = denses[slab][atom, p * GY : (p + 1) * GY, :]
                term = jnp.sum((weight * value).reshape(GY // 8, 8, GZ), axis=0)
                partial[atom] = term if p == 0 else partial[atom] + term
        lines = [jnp.sum(term, axis=0, keepdims=True) for term in partial]
        total = jnp.sum(jnp.concatenate(lines, axis=0), axis=1, keepdims=True)
        weights.append(total * gains[slab][...])
    summed_z[...] = jnp.dot(wide_z[...], along_z[...], preferred_element_type=F32)
    for p in range(SLAB):
        both = jnp.concatenate(
            [
                jnp.concatenate(
                    [
                        wide_z[start : start + GY, 0:GZ],
                        wide_z[start : start + GY, GZ : 2 * GZ],
                    ],
                    axis=0,
                )
                for start in (p * GY, (SLAB + p) * GY)
            ],
            axis=1,
        )
        turned = jnp.dot(along_y[...], both, preferred_element_type=F32)
        turned = turned[:GY] + turned[GY:]
        for slab in range(2):
            start = (slab * SLAB + p) * GY
            level = DIAGONAL + potentials[slab](p)
            total = level * planes(slab, p) + turned[:, slab * GZ : (slab + 1) * GZ]
            total = total + (
                summed_z[start : start + GY, 0:GZ] + summed_z[start : start + GY, GZ : 2 * GZ]
            )
            for atom in range(ATOM_DEV):
                total = (
                    total
                    + weights[slab][atom : atom + 1, :]
                    * denses[slab][atom, p * GY : (p + 1) * GY, :]
                )
            for offset in range(1, 7):
                terms = [
                    planes(slab, k)
                    for k in (p - offset, p + offset)
                    if -reach <= k < SLAB + reach
                ]
                if terms:
                    total = total + SIDE[offset] * functools.reduce(jnp.add, terms)
            emit(slab, p, scale * total)


def potentials_of(own, other):
    return (lambda p: own[p]), (lambda p: other[p * GY : (p + 1) * GY, :])


def first_kernel(
    received, potential, other, dense, gains, other_dense, other_gains, along_z, along_y,
    start_out, next_out, sent_out, panel_out, slabs, wide_z, summed_z,
):
    panel = jnp.zeros((YPART, GZ), F32)
    for source in range(ROWS):
        for slab in range(2):
            slabs[slab, :, source * YPART : (source + 1) * YPART, :] = received[
                source, slab * WIDE : (slab + 1) * WIDE
            ].astype(F32)
        panel = panel + received[source, 2 * WIDE].astype(F32)
    mine = jnp.where(lax.axis_index("row") < HALF, panel[0:1], panel[1:2])
    panel_out[...] = jnp.broadcast_to(mine, (8, GZ))
    for slab in range(2):
        start_out[slab] = slabs[slab, SLAB : 2 * SLAB]

    def emit(slab, p, value):
        next_out[slab, p] = value
        sent_out[slab, p] = value.astype(BF16)

    apply(
        lambda slab, p: slabs[slab, SLAB + p], SLAB, 1.0 / HALF_WIDTH,
        potentials_of(potential, other), (dense, other_dense), (gains, other_gains),
        along_z, along_y, wide_z, summed_z, emit,
    )


def inside_kernel(
    current, previous, potential, other, dense, gains, other_dense, other_gains, along_z, along_y,
    out, wide_z, summed_z,
):
    def emit(slab, p, value):
        out[slab, p] = value - previous[slab, p]

    apply(
        lambda slab, p: current[slab, p], 0, 2.0 / HALF_WIDTH,
        potentials_of(potential, other), (dense, other_dense), (gains, other_gains),
        along_z, along_y, wide_z, summed_z, emit,
    )


def joining(partial, below, above):
    column = lax.axis_index("row") & (HALF - 1)
    lower = jnp.where(column == 0, 1, 0)
    upper = jnp.where(column == HALF - 1, 1, 0)

    def joined(slab, p):
        total = partial[slab, p]
        lower_slab = lower ^ slab
        upper_slab = upper ^ slab
        for offset in range(1, 7):
            terms = []
            if p - offset < 0:
                terms.append(below[lower_slab, SLAB + p - offset].astype(F32))
            if p + offset >= SLAB:
                terms.append(above[upper_slab, p + offset - SLAB].astype(F32))
            if terms:
                side = (2.0 / HALF_WIDTH) * SIDE[offset]
                total = total + side * functools.reduce(jnp.add, terms)
        return total

    return joined


def join_kernel(partial, below, above, next_out, sent_out):
    joined = joining(partial, below, above)
    for p in range(SLAB):
        for slab in range(2):
            value = joined(slab, p)
            next_out[slab, p] = value
            sent_out[slab, p] = value.astype(BF16)


def last_kernel(partial, below, above, panel, out, slabs):
    joined = joining(partial, below, above)
    for p in range(SLAB):
        for slab in range(2):
            slabs[slab, p * GY : (p + 1) * GY, :] = joined(slab, p)
    upper = lax.axis_index("row") // HALF
    line = lax.broadcasted_iota(jnp.int32, (4, GZ), 0)
    tile = jnp.where(line == 0, panel[0:4], 0.0).astype(BF16)
    for half in range(2):
        slab = upper ^ half
        for col in range(COLS):
            member = half * COLS + col
            for k in range(PIECE):
                at = 4 * (PIECE * col + k)
                out[member, k] = slabs[slab, at : at + 4, :].astype(BF16)
            out[member, PIECE] = tile


def rotate_kernel(received, panel_rows, out, states, wanted, rotated):
    members = 2 * COLS
    size = 4 * members
    for member in range(members):
        at = slice(4 * member, 4 * member + 4)
        for k in range(PIECE):
            states[at, k * GZ : (k + 1) * GZ] = received[member, k].astype(F32)
        tile = received[member, PIECE].astype(F32)
        wanted[at, :] = jnp.broadcast_to(tile[0:1], (4, GZ))
    order = lax.broadcasted_iota(jnp.int32, (size, 64), 0) >> 2
    state_of = 2 * (order & (COLS - 1)) + lax.shift_right_logical(order, 5)
    stored = jnp.where(panel_rows[...] == state_of, 1.0, 0.0).astype(BF16)
    spread = lax.dot_general(
        wanted[:, 0:64].astype(BF16), stored, (((1,), (1,)), ((), ())),
        preferred_element_type=F32,
    )
    same = (
        lax.broadcasted_iota(jnp.int32, (size, size), 0) & 3
    ) == (lax.broadcasted_iota(jnp.int32, (size, size), 1) & 3)
    spread = jnp.where(same, spread, 0.0).astype(BF16)
    rotated[...] = jnp.dot(spread, states[...].astype(BF16), preferred_element_type=F32)
    for col in range(COLS):
        for state in range(2):
            at = 4 * (state * COLS + col)
            for k in range(PIECE):
                out[col, state * PIECE + k] = rotated[
                    at : at + 4, k * GZ : (k + 1) * GZ
                ].astype(BF16)


def place_kernel(received, out):
    for col in range(COLS):
        for state in range(2):
            for k in range(PIECE):
                at = 4 * (PIECE * col + k)
                out[state, at : at + 4, :] = received[col, state * PIECE + k].astype(F32)


def per_device(orbitals, potential, proj_points, projector, strength, ritz_panel, panel_rows):
    shape = jax.ShapeDtypeStruct
    slabs_f32 = shape((2, SLAB, GY, GZ), F32)
    slabs_bf16 = shape((2, SLAB, GY, GZ), BF16)
    dense_gains = (shape((ATOM_DEV, SLAB_ROWS, GZ), F32), shape((ATOM_DEV, GZ), F32))
    along_z, along_y = stencil_matrices()
    smem = pl.BlockSpec(memory_space=pltpu.SMEM)
    work = [
        pltpu.VMEM((2 * SLAB_ROWS, 2 * GZ), BF16),
        pltpu.VMEM((2 * SLAB_ROWS, 2 * GZ), F32),
    ]
    around = [(i, i // HALF * HALF + (i + 1) % HALF) for i in range(ROWS)]

    packed = call(pack_kernel, shape((ROWS, SENT, YPART, GZ), BF16), specs=[VMEM] * 2)(
        orbitals, ritz_panel.T
    )
    regrouped = lax.all_to_all(packed, "row", split_axis=0, concat_axis=0, tiled=True)
    given = call(
        other_kernel,
        shape((OTHER_ROWS, GZ), F32),
        specs=[VMEM] * 3 + [smem],
        flops=1_000_000,
        bytes_accessed=400_000,
    )(potential, proj_points, projector, strength)
    other = lax.ppermute(given, "row", [(i, i ^ HALF) for i in range(ROWS)])
    dense, gains = call(
        project_kernel,
        dense_gains,
        specs=[VMEM, VMEM, smem],
        flops=1_000_000_000,
        bytes_accessed=1_600_000,
    )(proj_points, projector, strength)
    other_dense, other_gains = call(
        project_other_kernel,
        dense_gains,
        specs=[VMEM],
        flops=1_000_000_000,
        bytes_accessed=1_600_000,
    )(other)

    fixed = (potential, other, dense, gains, other_dense, other_gains, along_z, along_y)
    previous, current, sent, panel = call(
        first_kernel,
        (slabs_f32, slabs_f32, slabs_bf16, shape((8, GZ), F32)),
        scratch=[pltpu.VMEM((2, WIDE, GY, GZ), F32)] + work,
        specs=[VMEM] * 9,
    )(regrouped, *fixed)
    for step in range(2):
        below = lax.ppermute(sent, "row", around)
        above = lax.ppermute(sent, "row", [(d, s) for s, d in around])
        partial = call(
            inside_kernel,
            slabs_f32,
            scratch=work,
            specs=[VMEM] * 10,
            flops=2_000_000_000,
            bytes_accessed=3_000_000,
        )(current, previous, *fixed)
        if step == 0:
            previous = current
            current, sent = call(join_kernel, (slabs_f32, slabs_bf16), specs=[VMEM] * 3)(
                partial, below, above
            )
    layered = call(
        last_kernel,
        shape((2 * COLS, PIECE + 1, 4, GZ), BF16),
        scratch=[pltpu.VMEM((2, SLAB_ROWS, GZ), F32)],
        specs=[VMEM] * 4,
    )(partial, below, above, panel)
    both = [
        [(i + HALF * half) * COLS + col for half in range(2) for col in range(COLS)]
        for i in range(HALF)
    ]
    columns = lax.all_to_all(
        layered, ("row", "col"), split_axis=0, concat_axis=0, tiled=True, axis_index_groups=both
    )
    turned = call(
        rotate_kernel,
        shape((COLS, 2 * PIECE, 4, GZ), BF16),
        scratch=[
            pltpu.VMEM((8 * COLS, PIECE * GZ), F32),
            pltpu.VMEM((8 * COLS, GZ), F32),
            pltpu.VMEM((8 * COLS, PIECE * GZ), F32),
        ],
        specs=[VMEM] * 2,
    )(columns, panel_rows.reshape(1, -1))
    result = lax.all_to_all(turned, "col", split_axis=0, concat_axis=0, tiled=True)
    whole = call(place_kernel, shape((2, SLAB_ROWS, GZ), F32), specs=[VMEM])(result)
    return whole.reshape(2, SLAB, GY, GZ)


def solution(mesh):
    placed = (
        P("col", None, "row", None),
        P("row", None, None),
        P("row", None),
        P("row", None),
        P("row"),
        P("row", "col"),
        P(),
    )
    return jax.shard_map(
        per_device,
        mesh=mesh,
        in_specs=placed,
        out_specs=P("col", "row", None, None),
        check_vma=False,
    )
```

```python
import functools

import jax
import jax.numpy as jnp
import numpy as np
from jax import lax
from jax.experimental import pallas as pl
from jax.experimental.pallas import tpu as pltpu
from jax.sharding import PartitionSpec as P

F32 = jnp.float32
BF16 = jnp.bfloat16

STENCIL = (
    -5369.0 / 1800.0,
    12.0 / 7.0,
    -15.0 / 56.0,
    10.0 / 189.0,
    -1.0 / 112.0,
    2.0 / 1925.0,
    -1.0 / 16632.0,
)
CENTER = 7.0
HALF_WIDTH = 5.0

ROWS, COLS = 16, 32
SLAB, GY, GZ = 6, 64, 128
GX = ROWS * SLAB
YPART = GY // ROWS
WIDE = 3 * SLAB
ATOM_DEV = 8
SLAB_ROWS = SLAB * GY
SENT = 2 * WIDE + 1
HALF = ROWS // 2
PIECE = SLAB_ROWS // COLS // 4
OTHER_ROWS = SLAB_ROWS + 3 * ATOM_DEV

SIDE = tuple(-0.5 * c for c in STENCIL)
DIAGONAL = -0.5 * 3.0 * STENCIL[0] - CENTER

VMEM = pl.BlockSpec(memory_space=pltpu.VMEM)
MIB = 1024 * 1024


def circulant(size):
    whole = np.zeros((size, size), np.float32)
    for offset in range(1, 7):
        for i in range(size):
            whole[i, (i + offset) % size] += SIDE[offset]
            whole[i, (i - offset) % size] += SIDE[offset]
    high = whole.astype(jnp.bfloat16)
    low = (whole - high.astype(np.float32)).astype(jnp.bfloat16)
    return high, low


def stencil_matrices():
    high, low = circulant(GZ)
    along_z = np.block([[high, low], [high, low]])
    high, low = circulant(GY)
    along_y = np.block([[high, high], [low, low]])
    return jnp.asarray(along_z), jnp.asarray(along_y)


def call(kernel, outs, scratch=(), flops=0, bytes_accessed=0, specs=None, vmem=12 * MIB):
    return pl.pallas_call(
        kernel,
        out_shape=outs,
        in_specs=specs,
        out_specs=jax.tree.map(lambda _: VMEM, outs),
        scratch_shapes=list(scratch),
        compiler_params=pltpu.CompilerParams(vmem_limit_bytes=vmem),
        cost_estimate=pl.CostEstimate(
            flops=flops, bytes_accessed=bytes_accessed, transcendentals=0
        ),
    )


def pack_kernel(orbitals, panel, out, states, columns, sems):
    copies = [
        pltpu.make_async_copy(source, target, sems.at[i])
        for i, (source, target) in enumerate(
            [
                (panel, columns),
                (orbitals.at[0], states.at[0]),
                (orbitals.at[1], states.at[1]),
            ]
        )
    ]
    for copy in copies:
        copy.start()
    row = lax.axis_index("row")
    place = lax.broadcasted_iota(jnp.int32, (2, GZ), 1)
    copies[0].wait()
    values = columns[...].astype(F32)
    tile = jnp.zeros((2, GZ), F32)
    for k in range(YPART):
        tile = jnp.where(place == YPART * row + k, values[:, k : k + 1], tile)
    tile = jnp.concatenate([tile, jnp.zeros((YPART - 2, GZ), F32)], axis=0).astype(BF16)
    for state in range(2):
        copies[1 + state].wait()
        for target in range(HALF * state, HALF * state + HALF):
            for index, slab in enumerate((target, target ^ HALF)):
                begin = (SLAB * slab - SLAB) % GX
                base = index * WIDE
                head = min(WIDE, GX - begin)
                out[target, base : base + head] = states[state, begin : begin + head]
                if head < WIDE:
                    out[target, base + head : base + WIDE] = states[state, : WIDE - head]
            out[target, 2 * WIDE] = tile


def other_kernel(potential, points, projector, strength, out):
    for p in range(SLAB):
        out[p * GY : (p + 1) * GY, :] = potential[p]
    out[SLAB_ROWS : SLAB_ROWS + 8, :] = points[...].astype(F32)
    out[SLAB_ROWS + 8 : SLAB_ROWS + 16, :] = projector[...]
    for atom in range(ATOM_DEV):
        at = SLAB_ROWS + 16 + atom
        out[at : at + 1, :] = jnp.full((1, GZ), strength[atom], F32)


def densify(points, projector, dense):
    grid_row, lane = lax.shift_right_logical(points, 7), points & (GZ - 1)
    high = projector.astype(BF16).astype(F32)
    parts = (high, projector - high)
    for atom in range(ATOM_DEV):
        rows = jnp.where(
            lax.broadcasted_iota(jnp.int32, (SLAB_ROWS, GZ), 0) == grid_row[atom : atom + 1, :],
            1.0,
            0.0,
        ).astype(BF16)
        at_lane = lax.broadcasted_iota(jnp.int32, (GZ, GZ), 0) == lane[atom : atom + 1, :]
        lanes = [
            jnp.where(at_lane, part[atom : atom + 1, :], 0.0).astype(BF16) for part in parts
        ]
        dense[atom] = lax.dot_general(
            jnp.concatenate([rows] * 2, axis=1),
            jnp.concatenate(lanes, axis=1),
            (((1,), (1,)), ((), ())),
            preferred_element_type=F32,
        )


def project_kernel(points, projector, strength, dense, gains):
    densify(points[...], projector[...], dense)
    for atom in range(ATOM_DEV):
        gains[atom : atom + 1, :] = jnp.full((1, GZ), strength[atom], F32)


def project_other_kernel(given, dense, gains):
    points = given[SLAB_ROWS : SLAB_ROWS + 8, :].astype(jnp.int32)
    densify(points, given[SLAB_ROWS + 8 : SLAB_ROWS + 16, :], dense)
    gains[...] = given[SLAB_ROWS + 16 : SLAB_ROWS + 24, :]


def apply(planes, reach, scale, potentials, denses, gains, along_z, along_y, wide_z, summed_z, emit):
    weights = []
    for slab in range(2):
        partial = [None] * ATOM_DEV
        for p in range(SLAB):
            value = planes(slab, p)
            high = value.astype(BF16)
            low = (value - high.astype(F32)).astype(BF16)
            start = (slab * SLAB + p) * GY
            wide_z[start : start + GY, 0:GZ] = high
            wide_z[start : start + GY, GZ : 2 * GZ] = low
            for atom in range(ATOM_DEV):
                weight = denses[slab][atom, p * GY : (p + 1) * GY, :]
                term = jnp.sum((weight * value).reshape(GY // 8, 8, GZ), axis=0)
                partial[atom] = term if p == 0 else partial[atom] + term
        lines = [jnp.sum(term, axis=0, keepdims=True) for term in partial]
        total = jnp.sum(jnp.concatenate(lines, axis=0), axis=1, keepdims=True)
        weights.append(total * gains[slab][...])
    summed_z[...] = jnp.dot(wide_z[...], along_z[...], preferred_element_type=F32)
    for p in range(SLAB):
        both = jnp.concatenate(
            [
                jnp.concatenate(
                    [
                        wide_z[start : start + GY, 0:GZ],
                        wide_z[start : start + GY, GZ : 2 * GZ],
                    ],
                    axis=0,
                )
                for start in (p * GY, (SLAB + p) * GY)
            ],
            axis=1,
        )
        turned = jnp.dot(along_y[...], both, preferred_element_type=F32)
        turned = turned[:GY] + turned[GY:]
        for slab in range(2):
            start = (slab * SLAB + p) * GY
            level = DIAGONAL + potentials[slab](p)
            total = level * planes(slab, p) + turned[:, slab * GZ : (slab + 1) * GZ]
            total = total + (
                summed_z[start : start + GY, 0:GZ] + summed_z[start : start + GY, GZ : 2 * GZ]
            )
            for atom in range(ATOM_DEV):
                total = (
                    total
                    + weights[slab][atom : atom + 1, :]
                    * denses[slab][atom, p * GY : (p + 1) * GY, :]
                )
            for offset in range(1, 7):
                terms = [
                    planes(slab, k)
                    for k in (p - offset, p + offset)
                    if -reach <= k < SLAB + reach
                ]
                if terms:
                    total = total + SIDE[offset] * functools.reduce(jnp.add, terms)
            emit(slab, p, scale * total)


def potentials_of(own, other):
    return (lambda p: own[p]), (lambda p: other[p * GY : (p + 1) * GY, :])


def first_kernel(
    received, potential, other, dense, gains, other_dense, other_gains, along_z, along_y,
    start_out, next_out, sent_out, panel_out, slabs, wide_z, summed_z,
):
    panel = jnp.zeros((YPART, GZ), F32)
    for source in range(ROWS):
        for slab in range(2):
            slabs[slab, :, source * YPART : (source + 1) * YPART, :] = received[
                source, slab * WIDE : (slab + 1) * WIDE
            ].astype(F32)
        panel = panel + received[source, 2 * WIDE].astype(F32)
    mine = jnp.where(lax.axis_index("row") < HALF, panel[0:1], panel[1:2])
    panel_out[...] = jnp.broadcast_to(mine, (8, GZ))
    for slab in range(2):
        start_out[slab] = slabs[slab, SLAB : 2 * SLAB]

    def emit(slab, p, value):
        next_out[slab, p] = value
        sent_out[slab, p] = value.astype(BF16)

    apply(
        lambda slab, p: slabs[slab, SLAB + p], SLAB, 1.0 / HALF_WIDTH,
        potentials_of(potential, other), (dense, other_dense), (gains, other_gains),
        along_z, along_y, wide_z, summed_z, emit,
    )


def inside_kernel(
    current, previous, potential, other, dense, gains, other_dense, other_gains, along_z, along_y,
    out, wide_z, summed_z,
):
    def emit(slab, p, value):
        out[slab, p] = value - previous[slab, p]

    apply(
        lambda slab, p: current[slab, p], 0, 2.0 / HALF_WIDTH,
        potentials_of(potential, other), (dense, other_dense), (gains, other_gains),
        along_z, along_y, wide_z, summed_z, emit,
    )


def joining(partial, below, above):
    column = lax.axis_index("row") & (HALF - 1)
    lower = jnp.where(column == 0, 1, 0)
    upper = jnp.where(column == HALF - 1, 1, 0)

    def joined(slab, p):
        total = partial[slab, p]
        lower_slab = lower ^ slab
        upper_slab = upper ^ slab
        for offset in range(1, 7):
            terms = []
            if p - offset < 0:
                terms.append(below[lower_slab, SLAB + p - offset].astype(F32))
            if p + offset >= SLAB:
                terms.append(above[upper_slab, p + offset - SLAB].astype(F32))
            if terms:
                side = (2.0 / HALF_WIDTH) * SIDE[offset]
                total = total + side * functools.reduce(jnp.add, terms)
        return total

    return joined


def join_kernel(partial, below, above, next_out, sent_out):
    joined = joining(partial, below, above)
    for p in range(SLAB):
        for slab in range(2):
            value = joined(slab, p)
            next_out[slab, p] = value
            sent_out[slab, p] = value.astype(BF16)


def last_kernel(partial, below, above, panel, out, slabs):
    joined = joining(partial, below, above)
    for p in range(SLAB):
        for slab in range(2):
            slabs[slab, p * GY : (p + 1) * GY, :] = joined(slab, p)
    upper = lax.axis_index("row") // HALF
    line = lax.broadcasted_iota(jnp.int32, (4, GZ), 0)
    tile = jnp.where(line == 0, panel[0:4], 0.0).astype(BF16)
    for half in range(2):
        slab = upper ^ half
        for col in range(COLS):
            member = half * COLS + col
            for k in range(PIECE):
                at = 4 * (PIECE * col + k)
                out[member, k] = slabs[slab, at : at + 4, :].astype(BF16)
            out[member, PIECE] = tile


def rotate_kernel(received, panel_rows, out, states, wanted, rotated):
    members = 2 * COLS
    size = 4 * members
    for member in range(members):
        at = slice(4 * member, 4 * member + 4)
        for k in range(PIECE):
            states[at, k * GZ : (k + 1) * GZ] = received[member, k].astype(F32)
        tile = received[member, PIECE].astype(F32)
        wanted[at, :] = jnp.broadcast_to(tile[0:1], (4, GZ))
    order = lax.broadcasted_iota(jnp.int32, (size, 64), 0) >> 2
    state_of = 2 * (order & (COLS - 1)) + lax.shift_right_logical(order, 5)
    stored = jnp.where(panel_rows[...] == state_of, 1.0, 0.0).astype(BF16)
    spread = lax.dot_general(
        wanted[:, 0:64].astype(BF16), stored, (((1,), (1,)), ((), ())),
        preferred_element_type=F32,
    )
    same = (
        lax.broadcasted_iota(jnp.int32, (size, size), 0) & 3
    ) == (lax.broadcasted_iota(jnp.int32, (size, size), 1) & 3)
    spread = jnp.where(same, spread, 0.0).astype(BF16)
    rotated[...] = jnp.dot(spread, states[...].astype(BF16), preferred_element_type=F32)
    for col in range(COLS):
        for state in range(2):
            at = 4 * (state * COLS + col)
            for k in range(PIECE):
                out[col, state * PIECE + k] = rotated[
                    at : at + 4, k * GZ : (k + 1) * GZ
                ].astype(BF16)


def place_kernel(received, out):
    for col in range(COLS):
        for state in range(2):
            for k in range(PIECE):
                at = 4 * (PIECE * col + k)
                out[state, at : at + 4, :] = received[col, state * PIECE + k].astype(F32)


def per_device(orbitals, potential, proj_points, projector, strength, ritz_panel, panel_rows):
    shape = jax.ShapeDtypeStruct
    slabs_f32 = shape((2, SLAB, GY, GZ), F32)
    slabs_bf16 = shape((2, SLAB, GY, GZ), BF16)
    dense_gains = (shape((ATOM_DEV, SLAB_ROWS, GZ), F32), shape((ATOM_DEV, GZ), F32))
    along_z, along_y = stencil_matrices()
    smem = pl.BlockSpec(memory_space=pltpu.SMEM)
    work = [
        pltpu.VMEM((2 * SLAB_ROWS, 2 * GZ), BF16),
        pltpu.VMEM((2 * SLAB_ROWS, 2 * GZ), F32),
    ]
    around = [(i, i // HALF * HALF + (i + 1) % HALF) for i in range(ROWS)]

    packed = call(
        pack_kernel,
        shape((ROWS, SENT, YPART, GZ), BF16),
        scratch=[
            pltpu.VMEM((2, GX, YPART, GZ), BF16),
            pltpu.VMEM((2, YPART), BF16),
            pltpu.SemaphoreType.DMA((3,)),
        ],
        specs=[pl.BlockSpec(memory_space=pl.ANY)] * 2,
        vmem=60 * MIB,
    )(orbitals, ritz_panel.T)
    regrouped = lax.all_to_all(packed, "row", split_axis=0, concat_axis=0, tiled=True)
    given = call(
        other_kernel,
        shape((OTHER_ROWS, GZ), F32),
        specs=[VMEM] * 3 + [smem],
        flops=1_000_000,
        bytes_accessed=400_000,
    )(potential, proj_points, projector, strength)
    other = lax.ppermute(given, "row", [(i, i ^ HALF) for i in range(ROWS)])
    dense, gains = call(
        project_kernel,
        dense_gains,
        specs=[VMEM, VMEM, smem],
        flops=1_000_000_000,
        bytes_accessed=1_600_000,
    )(proj_points, projector, strength)
    other_dense, other_gains = call(
        project_other_kernel,
        dense_gains,
        specs=[VMEM],
        flops=1_000_000_000,
        bytes_accessed=1_600_000,
    )(other)

    fixed = (potential, other, dense, gains, other_dense, other_gains, along_z, along_y)
    previous, current, sent, panel = call(
        first_kernel,
        (slabs_f32, slabs_f32, slabs_bf16, shape((8, GZ), F32)),
        scratch=[pltpu.VMEM((2, WIDE, GY, GZ), F32)] + work,
        specs=[VMEM] * 9,
    )(regrouped, *fixed)
    for step in range(2):
        below = lax.ppermute(sent, "row", around)
        above = lax.ppermute(sent, "row", [(d, s) for s, d in around])
        partial = call(
            inside_kernel,
            slabs_f32,
            scratch=work,
            specs=[VMEM] * 10,
            flops=2_000_000_000,
            bytes_accessed=3_000_000,
        )(current, previous, *fixed)
        if step == 0:
            previous = current
            current, sent = call(join_kernel, (slabs_f32, slabs_bf16), specs=[VMEM] * 3)(
                partial, below, above
            )
    layered = call(
        last_kernel,
        shape((2 * COLS, PIECE + 1, 4, GZ), BF16),
        scratch=[pltpu.VMEM((2, SLAB_ROWS, GZ), F32)],
        specs=[VMEM] * 4,
    )(partial, below, above, panel)
    both = [
        [(i + HALF * half) * COLS + col for half in range(2) for col in range(COLS)]
        for i in range(HALF)
    ]
    columns = lax.all_to_all(
        layered, ("row", "col"), split_axis=0, concat_axis=0, tiled=True, axis_index_groups=both
    )
    turned = call(
        rotate_kernel,
        shape((COLS, 2 * PIECE, 4, GZ), BF16),
        scratch=[
            pltpu.VMEM((8 * COLS, PIECE * GZ), F32),
            pltpu.VMEM((8 * COLS, GZ), F32),
            pltpu.VMEM((8 * COLS, PIECE * GZ), F32),
        ],
        specs=[VMEM] * 2,
    )(columns, panel_rows.reshape(1, -1))
    result = lax.all_to_all(turned, "col", split_axis=0, concat_axis=0, tiled=True)
    whole = call(place_kernel, shape((2, SLAB_ROWS, GZ), F32), specs=[VMEM])(result)
    return whole.reshape(2, SLAB, GY, GZ)


def solution(mesh):
    placed = (
        P("col", None, "row", None),
        P("row", None, None),
        P("row", None),
        P("row", None),
        P("row"),
        P("row", "col"),
        P(),
    )
    return jax.shard_map(
        per_device,
        mesh=mesh,
        in_specs=placed,
        out_specs=P("col", "row", None, None),
        check_vma=False,
    )
```

```python
import functools

import jax
import jax.numpy as jnp
import numpy as np
from jax import lax
from jax.experimental import pallas as pl
from jax.experimental.pallas import tpu as pltpu
from jax.sharding import PartitionSpec as P

F32 = jnp.float32
BF16 = jnp.bfloat16

STENCIL = (
    -5369.0 / 1800.0,
    12.0 / 7.0,
    -15.0 / 56.0,
    10.0 / 189.0,
    -1.0 / 112.0,
    2.0 / 1925.0,
    -1.0 / 16632.0,
)
CENTER = 7.0
HALF_WIDTH = 5.0

ROWS, COLS = 16, 32
SLAB, GY, GZ = 6, 64, 128
GX = ROWS * SLAB
YPART = GY // ROWS
WIDE = 3 * SLAB
ATOM_DEV = 8
SLAB_ROWS = SLAB * GY
SENT = 2 * WIDE + 1
HALF = ROWS // 2
PIECE = SLAB_ROWS // COLS // 4
OTHER_ROWS = SLAB_ROWS + 3 * ATOM_DEV

SIDE = tuple(-0.5 * c for c in STENCIL)
DIAGONAL = -0.5 * 3.0 * STENCIL[0] - CENTER

VMEM = pl.BlockSpec(memory_space=pltpu.VMEM)
MIB = 1024 * 1024


def circulant(size):
    whole = np.zeros((size, size), np.float32)
    for offset in range(1, 7):
        for i in range(size):
            whole[i, (i + offset) % size] += SIDE[offset]
            whole[i, (i - offset) % size] += SIDE[offset]
    high = whole.astype(jnp.bfloat16)
    low = (whole - high.astype(np.float32)).astype(jnp.bfloat16)
    return high, low


def stencil_matrices():
    high, low = circulant(GZ)
    along_z = np.block([[high, low], [high, low]])
    high, low = circulant(GY)
    along_y = np.block([[high, high], [low, low]])
    return jnp.asarray(along_z), jnp.asarray(along_y)


def call(kernel, outs, scratch=(), flops=0, bytes_accessed=0, specs=None, vmem=12 * MIB):
    return pl.pallas_call(
        kernel,
        out_shape=outs,
        in_specs=specs,
        out_specs=jax.tree.map(lambda _: VMEM, outs),
        scratch_shapes=list(scratch),
        compiler_params=pltpu.CompilerParams(vmem_limit_bytes=vmem),
        cost_estimate=pl.CostEstimate(
            flops=flops, bytes_accessed=bytes_accessed, transcendentals=0
        ),
    )


def pack_kernel(orbitals, panel, out, states, columns, sems):
    copies = [
        pltpu.make_async_copy(source, target, sems.at[i])
        for i, (source, target) in enumerate(
            [
                (panel, columns),
                (orbitals.at[0], states.at[0]),
                (orbitals.at[1], states.at[1]),
            ]
        )
    ]
    for copy in copies:
        copy.start()
    row = lax.axis_index("row")
    place = lax.broadcasted_iota(jnp.int32, (2, GZ), 1)
    copies[0].wait()
    values = columns[...].astype(F32)
    tile = jnp.zeros((2, GZ), F32)
    for k in range(YPART):
        tile = jnp.where(place == YPART * row + k, values[:, k : k + 1], tile)
    tile = jnp.concatenate([tile, jnp.zeros((YPART - 2, GZ), F32)], axis=0).astype(BF16)
    for state in range(2):
        copies[1 + state].wait()
        for target in range(HALF * state, HALF * state + HALF):
            for index, slab in enumerate((target, target ^ HALF)):
                begin = (SLAB * slab - SLAB) % GX
                base = index * WIDE
                head = min(WIDE, GX - begin)
                out[target, base : base + head] = states[state, begin : begin + head]
                if head < WIDE:
                    out[target, base + head : base + WIDE] = states[state, : WIDE - head]
            out[target, 2 * WIDE] = tile


def other_kernel(potential, points, projector, strength, out):
    for p in range(SLAB):
        out[p * GY : (p + 1) * GY, :] = potential[p]
    out[SLAB_ROWS : SLAB_ROWS + 8, :] = points[...].astype(F32)
    out[SLAB_ROWS + 8 : SLAB_ROWS + 16, :] = projector[...]
    for atom in range(ATOM_DEV):
        at = SLAB_ROWS + 16 + atom
        out[at : at + 1, :] = jnp.full((1, GZ), strength[atom], F32)


def densify(points, projector, dense):
    grid_row, lane = lax.shift_right_logical(points, 7), points & (GZ - 1)
    high = projector.astype(BF16).astype(F32)
    parts = (high, projector - high)
    for atom in range(ATOM_DEV):
        rows = jnp.where(
            lax.broadcasted_iota(jnp.int32, (SLAB_ROWS, GZ), 0) == grid_row[atom : atom + 1, :],
            1.0,
            0.0,
        ).astype(BF16)
        at_lane = lax.broadcasted_iota(jnp.int32, (GZ, GZ), 0) == lane[atom : atom + 1, :]
        lanes = [
            jnp.where(at_lane, part[atom : atom + 1, :], 0.0).astype(BF16) for part in parts
        ]
        dense[atom] = lax.dot_general(
            jnp.concatenate([rows] * 2, axis=1),
            jnp.concatenate(lanes, axis=1),
            (((1,), (1,)), ((), ())),
            preferred_element_type=F32,
        )


def project_kernel(points, projector, strength, dense, gains):
    densify(points[...], projector[...], dense)
    for atom in range(ATOM_DEV):
        gains[atom : atom + 1, :] = jnp.full((1, GZ), strength[atom], F32)


def other_projectors(given, dense):
    points = given[SLAB_ROWS : SLAB_ROWS + 8, :].astype(jnp.int32)
    densify(points, given[SLAB_ROWS + 8 : SLAB_ROWS + 16, :], dense)
    return given.at[SLAB_ROWS + 16 : SLAB_ROWS + 24]


def apply(planes, reach, scale, potentials, denses, gains, along_z, along_y, wide_z, summed_z, emit):
    weights = []
    for slab in range(2):
        partial = [None] * ATOM_DEV
        for p in range(SLAB):
            value = planes(slab, p)
            high = value.astype(BF16)
            low = (value - high.astype(F32)).astype(BF16)
            start = (slab * SLAB + p) * GY
            wide_z[start : start + GY, 0:GZ] = high
            wide_z[start : start + GY, GZ : 2 * GZ] = low
            for atom in range(ATOM_DEV):
                weight = denses[slab][atom, p * GY : (p + 1) * GY, :]
                term = jnp.sum((weight * value).reshape(GY // 8, 8, GZ), axis=0)
                partial[atom] = term if p == 0 else partial[atom] + term
        lines = [jnp.sum(term, axis=0, keepdims=True) for term in partial]
        total = jnp.sum(jnp.concatenate(lines, axis=0), axis=1, keepdims=True)
        weights.append(total * gains[slab][...])
    summed_z[...] = jnp.dot(wide_z[...], along_z[...], preferred_element_type=F32)
    for p in range(SLAB):
        both = jnp.concatenate(
            [
                jnp.concatenate(
                    [
                        wide_z[start : start + GY, 0:GZ],
                        wide_z[start : start + GY, GZ : 2 * GZ],
                    ],
                    axis=0,
                )
                for start in (p * GY, (SLAB + p) * GY)
            ],
            axis=1,
        )
        turned = jnp.dot(along_y[...], both, preferred_element_type=F32)
        turned = turned[:GY] + turned[GY:]
        for slab in range(2):
            start = (slab * SLAB + p) * GY
            level = DIAGONAL + potentials[slab](p)
            total = level * planes(slab, p) + turned[:, slab * GZ : (slab + 1) * GZ]
            total = total + (
                summed_z[start : start + GY, 0:GZ] + summed_z[start : start + GY, GZ : 2 * GZ]
            )
            for atom in range(ATOM_DEV):
                total = (
                    total
                    + weights[slab][atom : atom + 1, :]
                    * denses[slab][atom, p * GY : (p + 1) * GY, :]
                )
            for offset in range(1, 7):
                terms = [
                    planes(slab, k)
                    for k in (p - offset, p + offset)
                    if -reach <= k < SLAB + reach
                ]
                if terms:
                    total = total + SIDE[offset] * functools.reduce(jnp.add, terms)
            emit(slab, p, scale * total)


def potentials_of(own, other):
    return (lambda p: own[p]), (lambda p: other[p * GY : (p + 1) * GY, :])


def first_kernel(
    received, potential, other, dense, gains, along_z, along_y,
    start_out, next_out, sent_out, panel_out, slabs, other_dense, wide_z, summed_z,
):
    other_gains = other_projectors(other, other_dense)
    panel = jnp.zeros((YPART, GZ), F32)
    for source in range(ROWS):
        for slab in range(2):
            slabs[slab, :, source * YPART : (source + 1) * YPART, :] = received[
                source, slab * WIDE : (slab + 1) * WIDE
            ].astype(F32)
        panel = panel + received[source, 2 * WIDE].astype(F32)
    mine = jnp.where(lax.axis_index("row") < HALF, panel[0:1], panel[1:2])
    panel_out[...] = jnp.broadcast_to(mine, (8, GZ))
    for slab in range(2):
        start_out[slab] = slabs[slab, SLAB : 2 * SLAB]

    def emit(slab, p, value):
        next_out[slab, p] = value
        sent_out[slab, p] = value.astype(BF16)

    apply(
        lambda slab, p: slabs[slab, SLAB + p], SLAB, 1.0 / HALF_WIDTH,
        potentials_of(potential, other), (dense, other_dense), (gains, other_gains),
        along_z, along_y, wide_z, summed_z, emit,
    )


def inside_kernel(
    current, previous, potential, other, dense, gains, along_z, along_y,
    out, other_dense, wide_z, summed_z,
):
    other_gains = other_projectors(other, other_dense)

    def emit(slab, p, value):
        out[slab, p] = value - previous[slab, p]

    apply(
        lambda slab, p: current[slab, p], 0, 2.0 / HALF_WIDTH,
        potentials_of(potential, other), (dense, other_dense), (gains, other_gains),
        along_z, along_y, wide_z, summed_z, emit,
    )


def joining(partial, below, above):
    column = lax.axis_index("row") & (HALF - 1)
    lower = jnp.where(column == 0, 1, 0)
    upper = jnp.where(column == HALF - 1, 1, 0)

    def joined(slab, p):
        total = partial[slab, p]
        lower_slab = lower ^ slab
        upper_slab = upper ^ slab
        for offset in range(1, 7):
            terms = []
            if p - offset < 0:
                terms.append(below[lower_slab, SLAB + p - offset].astype(F32))
            if p + offset >= SLAB:
                terms.append(above[upper_slab, p + offset - SLAB].astype(F32))
            if terms:
                side = (2.0 / HALF_WIDTH) * SIDE[offset]
                total = total + side * functools.reduce(jnp.add, terms)
        return total

    return joined


def join_kernel(partial, below, above, next_out, sent_out):
    joined = joining(partial, below, above)
    for p in range(SLAB):
        for slab in range(2):
            value = joined(slab, p)
            next_out[slab, p] = value
            sent_out[slab, p] = value.astype(BF16)


def last_kernel(partial, below, above, panel, out, slabs):
    joined = joining(partial, below, above)
    for p in range(SLAB):
        for slab in range(2):
            slabs[slab, p * GY : (p + 1) * GY, :] = joined(slab, p)
    upper = lax.axis_index("row") // HALF
    line = lax.broadcasted_iota(jnp.int32, (4, GZ), 0)
    tile = jnp.where(line == 0, panel[0:4], 0.0).astype(BF16)
    for half in range(2):
        slab = upper ^ half
        for col in range(COLS):
            member = half * COLS + col
            for k in range(PIECE):
                at = 4 * (PIECE * col + k)
                out[member, k] = slabs[slab, at : at + 4, :].astype(BF16)
            out[member, PIECE] = tile


def rotate_kernel(received, panel_rows, out, states, wanted, rotated):
    members = 2 * COLS
    size = 4 * members
    for member in range(members):
        at = slice(4 * member, 4 * member + 4)
        for k in range(PIECE):
            states[at, k * GZ : (k + 1) * GZ] = received[member, k].astype(F32)
        tile = received[member, PIECE].astype(F32)
        wanted[at, :] = jnp.broadcast_to(tile[0:1], (4, GZ))
    order = lax.broadcasted_iota(jnp.int32, (size, 64), 0) >> 2
    state_of = 2 * (order & (COLS - 1)) + lax.shift_right_logical(order, 5)
    stored = jnp.where(panel_rows[...] == state_of, 1.0, 0.0).astype(BF16)
    spread = lax.dot_general(
        wanted[:, 0:64].astype(BF16), stored, (((1,), (1,)), ((), ())),
        preferred_element_type=F32,
    )
    same = (
        lax.broadcasted_iota(jnp.int32, (size, size), 0) & 3
    ) == (lax.broadcasted_iota(jnp.int32, (size, size), 1) & 3)
    spread = jnp.where(same, spread, 0.0).astype(BF16)
    rotated[...] = jnp.dot(spread, states[...].astype(BF16), preferred_element_type=F32)
    for col in range(COLS):
        for state in range(2):
            at = 4 * (state * COLS + col)
            for k in range(PIECE):
                out[col, state * PIECE + k] = rotated[
                    at : at + 4, k * GZ : (k + 1) * GZ
                ].astype(BF16)


def place_kernel(received, out):
    for col in range(COLS):
        for state in range(2):
            for k in range(PIECE):
                at = 4 * (PIECE * col + k)
                out[state, at : at + 4, :] = received[col, state * PIECE + k].astype(F32)


def per_device(orbitals, potential, proj_points, projector, strength, ritz_panel, panel_rows):
    shape = jax.ShapeDtypeStruct
    slabs_f32 = shape((2, SLAB, GY, GZ), F32)
    slabs_bf16 = shape((2, SLAB, GY, GZ), BF16)
    dense_gains = (shape((ATOM_DEV, SLAB_ROWS, GZ), F32), shape((ATOM_DEV, GZ), F32))
    along_z, along_y = stencil_matrices()
    smem = pl.BlockSpec(memory_space=pltpu.SMEM)
    work = [
        pltpu.VMEM((ATOM_DEV, SLAB_ROWS, GZ), F32),
        pltpu.VMEM((2 * SLAB_ROWS, 2 * GZ), BF16),
        pltpu.VMEM((2 * SLAB_ROWS, 2 * GZ), F32),
    ]
    around = [(i, i // HALF * HALF + (i + 1) % HALF) for i in range(ROWS)]

    packed = call(
        pack_kernel,
        shape((ROWS, SENT, YPART, GZ), BF16),
        scratch=[
            pltpu.VMEM((2, GX, YPART, GZ), BF16),
            pltpu.VMEM((2, YPART), BF16),
            pltpu.SemaphoreType.DMA((3,)),
        ],
        specs=[pl.BlockSpec(memory_space=pl.ANY)] * 2,
        vmem=60 * MIB,
    )(orbitals, ritz_panel.T)
    regrouped = lax.all_to_all(packed, "row", split_axis=0, concat_axis=0, tiled=True)
    given = call(
        other_kernel,
        shape((OTHER_ROWS, GZ), F32),
        specs=[VMEM] * 3 + [smem],
        flops=1_000_000,
        bytes_accessed=400_000,
    )(potential, proj_points, projector, strength)
    other = lax.ppermute(given, "row", [(i, i ^ HALF) for i in range(ROWS)])
    dense, gains = call(
        project_kernel,
        dense_gains,
        specs=[VMEM, VMEM, smem],
        flops=1_000_000_000,
        bytes_accessed=1_600_000,
    )(proj_points, projector, strength)
    fixed = (potential, other, dense, gains, along_z, along_y)
    previous, current, sent, panel = call(
        first_kernel,
        (slabs_f32, slabs_f32, slabs_bf16, shape((8, GZ), F32)),
        scratch=[pltpu.VMEM((2, WIDE, GY, GZ), F32)] + work,
        specs=[VMEM] * 7,
    )(regrouped, *fixed)
    for step in range(2):
        below = lax.ppermute(sent, "row", around)
        above = lax.ppermute(sent, "row", [(d, s) for s, d in around])
        partial = call(
            inside_kernel,
            slabs_f32,
            scratch=work,
            specs=[VMEM] * 8,
            flops=2_000_000_000,
            bytes_accessed=3_000_000,
        )(current, previous, *fixed)
        if step == 0:
            previous = current
            current, sent = call(join_kernel, (slabs_f32, slabs_bf16), specs=[VMEM] * 3)(
                partial, below, above
            )
    layered = call(
        last_kernel,
        shape((2 * COLS, PIECE + 1, 4, GZ), BF16),
        scratch=[pltpu.VMEM((2, SLAB_ROWS, GZ), F32)],
        specs=[VMEM] * 4,
    )(partial, below, above, panel)
    both = [
        [(i + HALF * half) * COLS + col for half in range(2) for col in range(COLS)]
        for i in range(HALF)
    ]
    columns = lax.all_to_all(
        layered, ("row", "col"), split_axis=0, concat_axis=0, tiled=True, axis_index_groups=both
    )
    turned = call(
        rotate_kernel,
        shape((COLS, 2 * PIECE, 4, GZ), BF16),
        scratch=[
            pltpu.VMEM((8 * COLS, PIECE * GZ), F32),
            pltpu.VMEM((8 * COLS, GZ), F32),
            pltpu.VMEM((8 * COLS, PIECE * GZ), F32),
        ],
        specs=[VMEM] * 2,
    )(columns, panel_rows.reshape(1, -1))
    result = lax.all_to_all(turned, "col", split_axis=0, concat_axis=0, tiled=True)
    whole = call(place_kernel, shape((2, SLAB_ROWS, GZ), F32), specs=[VMEM])(result)
    return whole.reshape(2, SLAB, GY, GZ)


def solution(mesh):
    placed = (
        P("col", None, "row", None),
        P("row", None, None),
        P("row", None),
        P("row", None),
        P("row"),
        P("row", "col"),
        P(),
    )
    return jax.shard_map(
        per_device,
        mesh=mesh,
        in_specs=placed,
        out_specs=P("col", "row", None, None),
        check_vma=False,
    )
```

```python
import functools

import jax
import jax.numpy as jnp
import numpy as np
from jax import lax
from jax.experimental import pallas as pl
from jax.experimental.pallas import tpu as pltpu
from jax.sharding import PartitionSpec as P

F32 = jnp.float32
BF16 = jnp.bfloat16

STENCIL = (
    -5369.0 / 1800.0,
    12.0 / 7.0,
    -15.0 / 56.0,
    10.0 / 189.0,
    -1.0 / 112.0,
    2.0 / 1925.0,
    -1.0 / 16632.0,
)
CENTER = 7.0
HALF_WIDTH = 5.0

ROWS, COLS = 16, 32
SLAB, GY, GZ = 6, 64, 128
GX = ROWS * SLAB
YPART = GY // ROWS
WIDE = 3 * SLAB
ATOM_DEV = 8
SLAB_ROWS = SLAB * GY
SENT = 2 * WIDE + 1
HALF = ROWS // 2
PIECE = SLAB_ROWS // COLS // 4
OTHER_ROWS = SLAB_ROWS + 3 * ATOM_DEV

SIDE = tuple(-0.5 * c for c in STENCIL)
DIAGONAL = -0.5 * 3.0 * STENCIL[0] - CENTER

VMEM = pl.BlockSpec(memory_space=pltpu.VMEM)
ANY = pl.BlockSpec(memory_space=pl.ANY)
MIB = 1024 * 1024


def circulant(size):
    whole = np.zeros((size, size), np.float32)
    for offset in range(1, 7):
        for i in range(size):
            whole[i, (i + offset) % size] += SIDE[offset]
            whole[i, (i - offset) % size] += SIDE[offset]
    high = whole.astype(jnp.bfloat16)
    low = (whole - high.astype(np.float32)).astype(jnp.bfloat16)
    return high, low


def stencil_matrices():
    high, low = circulant(GZ)
    along_z = np.block([[high, low], [high, low]])
    high, low = circulant(GY)
    along_y = np.block([[high, high], [low, low]])
    return jnp.asarray(along_z), jnp.asarray(along_y)


def call(
    kernel, outs, scratch=(), flops=0, bytes_accessed=0, specs=None, vmem=12 * MIB, out_spec=VMEM
):
    return pl.pallas_call(
        kernel,
        out_shape=outs,
        in_specs=specs,
        out_specs=jax.tree.map(lambda _: out_spec, outs),
        scratch_shapes=list(scratch),
        compiler_params=pltpu.CompilerParams(vmem_limit_bytes=vmem),
        cost_estimate=pl.CostEstimate(
            flops=flops, bytes_accessed=bytes_accessed, transcendentals=0
        ),
    )


def pack_kernel(orbitals, panel, out, states, columns, chunks, sems, out_sems):
    copies = [
        pltpu.make_async_copy(source, target, sems.at[i])
        for i, (source, target) in enumerate(
            [
                (orbitals.at[0], states.at[0]),
                (orbitals.at[1], states.at[1]),
                (panel, columns),
            ]
        )
    ]
    for copy in copies:
        copy.start()
    row = lax.axis_index("row")
    place = lax.broadcasted_iota(jnp.int32, (2, GZ), 1)
    copies[2].wait()
    values = columns[...].astype(F32)
    tile = jnp.zeros((2, GZ), F32)
    for k in range(YPART):
        tile = jnp.where(place == YPART * row + k, values[:, k : k + 1], tile)
    tile = jnp.concatenate([tile, jnp.zeros((YPART - 2, GZ), F32)], axis=0).astype(BF16)
    for target in range(ROWS):
        state = target // HALF
        if target % HALF == 0:
            copies[state].wait()
        for index, slab in enumerate((target, target ^ HALF)):
            begin = (SLAB * slab - SLAB) % GX
            base = index * WIDE
            head = min(WIDE, GX - begin)
            chunks[target, base : base + head] = states[state, begin : begin + head]
            if head < WIDE:
                chunks[target, base + head : base + WIDE] = states[state, : WIDE - head]
        chunks[target, 2 * WIDE] = tile
        copies.append(
            pltpu.make_async_copy(chunks.at[target], out.at[target], out_sems.at[target])
        )
        copies[-1].start()
    for copy in copies[3:]:
        copy.wait()


def other_kernel(potential, points, projector, strength, out):
    for p in range(SLAB):
        out[p * GY : (p + 1) * GY, :] = potential[p]
    out[SLAB_ROWS : SLAB_ROWS + 8, :] = points[...].astype(F32)
    out[SLAB_ROWS + 8 : SLAB_ROWS + 16, :] = projector[...]
    for atom in range(ATOM_DEV):
        at = SLAB_ROWS + 16 + atom
        out[at : at + 1, :] = jnp.full((1, GZ), strength[atom], F32)


def densify(points, projector, dense):
    grid_row, lane = lax.shift_right_logical(points, 7), points & (GZ - 1)
    high = projector.astype(BF16).astype(F32)
    parts = (high, projector - high)
    for atom in range(ATOM_DEV):
        rows = jnp.where(
            lax.broadcasted_iota(jnp.int32, (SLAB_ROWS, GZ), 0) == grid_row[atom : atom + 1, :],
            1.0,
            0.0,
        ).astype(BF16)
        at_lane = lax.broadcasted_iota(jnp.int32, (GZ, GZ), 0) == lane[atom : atom + 1, :]
        lanes = [
            jnp.where(at_lane, part[atom : atom + 1, :], 0.0).astype(BF16) for part in parts
        ]
        dense[atom] = lax.dot_general(
            jnp.concatenate([rows] * 2, axis=1),
            jnp.concatenate(lanes, axis=1),
            (((1,), (1,)), ((), ())),
            preferred_element_type=F32,
        )


def project_kernel(points, projector, strength, dense, gains):
    densify(points[...], projector[...], dense)
    for atom in range(ATOM_DEV):
        gains[atom : atom + 1, :] = jnp.full((1, GZ), strength[atom], F32)


def other_projectors(given, dense):
    points = given[SLAB_ROWS : SLAB_ROWS + 8, :].astype(jnp.int32)
    densify(points, given[SLAB_ROWS + 8 : SLAB_ROWS + 16, :], dense)
    return given.at[SLAB_ROWS + 16 : SLAB_ROWS + 24]


def apply(planes, reach, scale, potentials, denses, gains, along_z, along_y, wide_z, summed_z, emit):
    weights = []
    for slab in range(2):
        partial = [None] * ATOM_DEV
        for p in range(SLAB):
            value = planes(slab, p)
            high = value.astype(BF16)
            low = (value - high.astype(F32)).astype(BF16)
            start = (slab * SLAB + p) * GY
            wide_z[start : start + GY, 0:GZ] = high
            wide_z[start : start + GY, GZ : 2 * GZ] = low
            for atom in range(ATOM_DEV):
                weight = denses[slab][atom, p * GY : (p + 1) * GY, :]
                term = jnp.sum((weight * value).reshape(GY // 8, 8, GZ), axis=0)
                partial[atom] = term if p == 0 else partial[atom] + term
        lines = [jnp.sum(term, axis=0, keepdims=True) for term in partial]
        total = jnp.sum(jnp.concatenate(lines, axis=0), axis=1, keepdims=True)
        weights.append(total * gains[slab][...])
    summed_z[...] = jnp.dot(wide_z[...], along_z[...], preferred_element_type=F32)
    for p in range(SLAB):
        both = jnp.concatenate(
            [
                jnp.concatenate(
                    [
                        wide_z[start : start + GY, 0:GZ],
                        wide_z[start : start + GY, GZ : 2 * GZ],
                    ],
                    axis=0,
                )
                for start in (p * GY, (SLAB + p) * GY)
            ],
            axis=1,
        )
        turned = jnp.dot(along_y[...], both, preferred_element_type=F32)
        turned = turned[:GY] + turned[GY:]
        for slab in range(2):
            start = (slab * SLAB + p) * GY
            level = DIAGONAL + potentials[slab](p)
            total = level * planes(slab, p) + turned[:, slab * GZ : (slab + 1) * GZ]
            total = total + (
                summed_z[start : start + GY, 0:GZ] + summed_z[start : start + GY, GZ : 2 * GZ]
            )
            for atom in range(ATOM_DEV):
                total = (
                    total
                    + weights[slab][atom : atom + 1, :]
                    * denses[slab][atom, p * GY : (p + 1) * GY, :]
                )
            for offset in range(1, 7):
                terms = [
                    planes(slab, k)
                    for k in (p - offset, p + offset)
                    if -reach <= k < SLAB + reach
                ]
                if terms:
                    total = total + SIDE[offset] * functools.reduce(jnp.add, terms)
            emit(slab, p, scale * total)


def potentials_of(own, other):
    return (lambda p: own[p]), (lambda p: other[p * GY : (p + 1) * GY, :])


def first_kernel(
    received, potential, other, dense, gains, along_z, along_y,
    start_out, next_out, sent_out, panel_out, slabs, other_dense, wide_z, summed_z,
):
    other_gains = other_projectors(other, other_dense)
    panel = jnp.zeros((YPART, GZ), F32)
    for source in range(ROWS):
        for slab in range(2):
            slabs[slab, :, source * YPART : (source + 1) * YPART, :] = received[
                source, slab * WIDE : (slab + 1) * WIDE
            ].astype(F32)
        panel = panel + received[source, 2 * WIDE].astype(F32)
    mine = jnp.where(lax.axis_index("row") < HALF, panel[0:1], panel[1:2])
    panel_out[...] = jnp.broadcast_to(mine, (8, GZ))
    for slab in range(2):
        start_out[slab] = slabs[slab, SLAB : 2 * SLAB]

    def emit(slab, p, value):
        next_out[slab, p] = value
        sent_out[slab, p] = value.astype(BF16)

    apply(
        lambda slab, p: slabs[slab, SLAB + p], SLAB, 1.0 / HALF_WIDTH,
        potentials_of(potential, other), (dense, other_dense), (gains, other_gains),
        along_z, along_y, wide_z, summed_z, emit,
    )


def inside_kernel(
    current, previous, potential, other, dense, gains, along_z, along_y,
    out, other_dense, wide_z, summed_z,
):
    other_gains = other_projectors(other, other_dense)

    def emit(slab, p, value):
        out[slab, p] = value - previous[slab, p]

    apply(
        lambda slab, p: current[slab, p], 0, 2.0 / HALF_WIDTH,
        potentials_of(potential, other), (dense, other_dense), (gains, other_gains),
        along_z, along_y, wide_z, summed_z, emit,
    )


def joining(partial, below, above):
    column = lax.axis_index("row") & (HALF - 1)
    lower = jnp.where(column == 0, 1, 0)
    upper = jnp.where(column == HALF - 1, 1, 0)

    def joined(slab, p):
        total = partial[slab, p]
        lower_slab = lower ^ slab
        upper_slab = upper ^ slab
        for offset in range(1, 7):
            terms = []
            if p - offset < 0:
                terms.append(below[lower_slab, SLAB + p - offset].astype(F32))
            if p + offset >= SLAB:
                terms.append(above[upper_slab, p + offset - SLAB].astype(F32))
            if terms:
                side = (2.0 / HALF_WIDTH) * SIDE[offset]
                total = total + side * functools.reduce(jnp.add, terms)
        return total

    return joined


def join_kernel(partial, below, above, next_out, sent_out):
    joined = joining(partial, below, above)
    for p in range(SLAB):
        for slab in range(2):
            value = joined(slab, p)
            next_out[slab, p] = value
            sent_out[slab, p] = value.astype(BF16)


def last_kernel(partial, below, above, panel, out, slabs):
    joined = joining(partial, below, above)
    for p in range(SLAB):
        for slab in range(2):
            slabs[slab, p * GY : (p + 1) * GY, :] = joined(slab, p)
    upper = lax.axis_index("row") // HALF
    line = lax.broadcasted_iota(jnp.int32, (4, GZ), 0)
    tile = jnp.where(line == 0, panel[0:4], 0.0).astype(BF16)
    for half in range(2):
        slab = upper ^ half
        for col in range(COLS):
            member = half * COLS + col
            for k in range(PIECE):
                at = 4 * (PIECE * col + k)
                out[member, k] = slabs[slab, at : at + 4, :].astype(BF16)
            out[member, PIECE] = tile


def rotate_kernel(received, panel_rows, out, states, wanted, rotated):
    members = 2 * COLS
    size = 4 * members
    for member in range(members):
        at = slice(4 * member, 4 * member + 4)
        for k in range(PIECE):
            states[at, k * GZ : (k + 1) * GZ] = received[member, k].astype(F32)
        tile = received[member, PIECE].astype(F32)
        wanted[at, :] = jnp.broadcast_to(tile[0:1], (4, GZ))
    order = lax.broadcasted_iota(jnp.int32, (size, 64), 0) >> 2
    state_of = 2 * (order & (COLS - 1)) + lax.shift_right_logical(order, 5)
    stored = jnp.where(panel_rows[...] == state_of, 1.0, 0.0).astype(BF16)
    spread = lax.dot_general(
        wanted[:, 0:64].astype(BF16), stored, (((1,), (1,)), ((), ())),
        preferred_element_type=F32,
    )
    same = (
        lax.broadcasted_iota(jnp.int32, (size, size), 0) & 3
    ) == (lax.broadcasted_iota(jnp.int32, (size, size), 1) & 3)
    spread = jnp.where(same, spread, 0.0).astype(BF16)
    rotated[...] = jnp.dot(spread, states[...].astype(BF16), preferred_element_type=F32)
    for col in range(COLS):
        for state in range(2):
            at = 4 * (state * COLS + col)
            for k in range(PIECE):
                out[col, state * PIECE + k] = rotated[
                    at : at + 4, k * GZ : (k + 1) * GZ
                ].astype(BF16)


def place_kernel(received, out, whole, sems):
    copies = []
    for col in range(COLS):
        for state in range(2):
            for k in range(PIECE):
                at = 4 * (PIECE * col + k)
                whole[state, at : at + 4, :] = received[col, state * PIECE + k].astype(F32)
        if col % 8 == 7:
            rows = pl.ds(4 * PIECE * (col - 7), 32 * PIECE)
            for state in range(2):
                copies.append(
                    pltpu.make_async_copy(
                        whole.at[state, rows], out.at[state, rows], sems.at[len(copies)]
                    )
                )
                copies[-1].start()
    for copy in copies:
        copy.wait()


def per_device(orbitals, potential, proj_points, projector, strength, ritz_panel, panel_rows):
    shape = jax.ShapeDtypeStruct
    slabs_f32 = shape((2, SLAB, GY, GZ), F32)
    slabs_bf16 = shape((2, SLAB, GY, GZ), BF16)
    dense_gains = (shape((ATOM_DEV, SLAB_ROWS, GZ), F32), shape((ATOM_DEV, GZ), F32))
    along_z, along_y = stencil_matrices()
    smem = pl.BlockSpec(memory_space=pltpu.SMEM)
    work = [
        pltpu.VMEM((ATOM_DEV, SLAB_ROWS, GZ), F32),
        pltpu.VMEM((2 * SLAB_ROWS, 2 * GZ), BF16),
        pltpu.VMEM((2 * SLAB_ROWS, 2 * GZ), F32),
    ]
    around = [(i, i // HALF * HALF + (i + 1) % HALF) for i in range(ROWS)]

    packed = call(
        pack_kernel,
        shape((ROWS, SENT, YPART, GZ), BF16),
        scratch=[
            pltpu.VMEM((2, GX, YPART, GZ), BF16),
            pltpu.VMEM((2, YPART), BF16),
            pltpu.VMEM((ROWS, SENT, YPART, GZ), BF16),
            pltpu.SemaphoreType.DMA((3,)),
            pltpu.SemaphoreType.DMA((ROWS,)),
        ],
        specs=[ANY] * 2,
        vmem=60 * MIB,
        out_spec=ANY,
    )(orbitals, ritz_panel.T)
    regrouped = lax.all_to_all(packed, "row", split_axis=0, concat_axis=0, tiled=True)
    given = call(
        other_kernel,
        shape((OTHER_ROWS, GZ), F32),
        specs=[VMEM] * 3 + [smem],
        flops=1_000_000,
        bytes_accessed=400_000,
    )(potential, proj_points, projector, strength)
    other = lax.ppermute(given, "row", [(i, i ^ HALF) for i in range(ROWS)])
    dense, gains = call(
        project_kernel,
        dense_gains,
        specs=[VMEM, VMEM, smem],
        flops=1_000_000_000,
        bytes_accessed=1_600_000,
    )(proj_points, projector, strength)
    fixed = (potential, other, dense, gains, along_z, along_y)
    previous, current, sent, panel = call(
        first_kernel,
        (slabs_f32, slabs_f32, slabs_bf16, shape((8, GZ), F32)),
        scratch=[pltpu.VMEM((2, WIDE, GY, GZ), F32)] + work,
        specs=[VMEM] * 7,
    )(regrouped, *fixed)
    for step in range(2):
        below = lax.ppermute(sent, "row", around)
        above = lax.ppermute(sent, "row", [(d, s) for s, d in around])
        partial = call(
            inside_kernel,
            slabs_f32,
            scratch=work,
            specs=[VMEM] * 8,
            flops=2_000_000_000,
            bytes_accessed=3_000_000,
        )(current, previous, *fixed)
        if step == 0:
            previous = current
            current, sent = call(join_kernel, (slabs_f32, slabs_bf16), specs=[VMEM] * 3)(
                partial, below, above
            )
    layered = call(
        last_kernel,
        shape((2 * COLS, PIECE + 1, 4, GZ), BF16),
        scratch=[pltpu.VMEM((2, SLAB_ROWS, GZ), F32)],
        specs=[VMEM] * 4,
    )(partial, below, above, panel)
    both = [
        [(i + HALF * half) * COLS + col for half in range(2) for col in range(COLS)]
        for i in range(HALF)
    ]
    columns = lax.all_to_all(
        layered, ("row", "col"), split_axis=0, concat_axis=0, tiled=True, axis_index_groups=both
    )
    turned = call(
        rotate_kernel,
        shape((COLS, 2 * PIECE, 4, GZ), BF16),
        scratch=[
            pltpu.VMEM((8 * COLS, PIECE * GZ), F32),
            pltpu.VMEM((8 * COLS, GZ), F32),
            pltpu.VMEM((8 * COLS, PIECE * GZ), F32),
        ],
        specs=[VMEM] * 2,
    )(columns, panel_rows.reshape(1, -1))
    result = lax.all_to_all(turned, "col", split_axis=0, concat_axis=0, tiled=True)
    whole = call(
        place_kernel,
        shape((2, SLAB_ROWS, GZ), F32),
        scratch=[pltpu.VMEM((2, SLAB_ROWS, GZ), F32), pltpu.SemaphoreType.DMA((COLS // 4,))],
        specs=[VMEM],
        out_spec=ANY,
    )(result)
    return whole.reshape(2, SLAB, GY, GZ)


def solution(mesh):
    placed = (
        P("col", None, "row", None),
        P("row", None, None),
        P("row", None),
        P("row", None),
        P("row"),
        P("row", "col"),
        P(),
    )
    return jax.shard_map(
        per_device,
        mesh=mesh,
        in_specs=placed,
        out_specs=P("col", "row", None, None),
        check_vma=False,
    )
```

```python
import functools

import jax
import jax.numpy as jnp
import numpy as np
from jax import lax
from jax.experimental import pallas as pl
from jax.experimental.pallas import tpu as pltpu
from jax.sharding import PartitionSpec as P

F32 = jnp.float32
BF16 = jnp.bfloat16

STENCIL = (
    -5369.0 / 1800.0,
    12.0 / 7.0,
    -15.0 / 56.0,
    10.0 / 189.0,
    -1.0 / 112.0,
    2.0 / 1925.0,
    -1.0 / 16632.0,
)
CENTER = 7.0
HALF_WIDTH = 5.0

ROWS, COLS = 16, 32
SLAB, GY, GZ = 6, 64, 128
GX = ROWS * SLAB
YPART = GY // ROWS
PAIR = 2 * SLAB
REACH = 3 * SLAB
WIDE = PAIR + 2 * REACH
SENT = WIDE + 1
ATOM_DEV = 8
SLAB_ROWS = SLAB * GY
PIECE = SLAB_ROWS // COLS // 4
OWN_ROWS = SLAB_ROWS + 3 * ATOM_DEV
NEAR_ROWS = SLAB_ROWS + 6 * ATOM_DEV
SLABS = 6
WINDOW = ((False, 0), (False, 1), (True, 0), (True, 1), (False, 2), (False, 3))

SIDE = tuple(-0.5 * c for c in STENCIL)
DIAGONAL = -0.5 * 3.0 * STENCIL[0] - CENTER

VMEM = pl.BlockSpec(memory_space=pltpu.VMEM)
ANY = pl.BlockSpec(memory_space=pl.ANY)
MIB = 1024 * 1024


def circulant(size):
    whole = np.zeros((size, size), np.float32)
    for offset in range(1, 7):
        for i in range(size):
            whole[i, (i + offset) % size] += SIDE[offset]
            whole[i, (i - offset) % size] += SIDE[offset]
    high = whole.astype(jnp.bfloat16)
    low = (whole - high.astype(np.float32)).astype(jnp.bfloat16)
    return high, low


def stencil_matrices():
    high, low = circulant(GZ)
    along_z = np.block([[high, low], [high, low]])
    high, low = circulant(GY)
    along_y = np.block([[high, high], [low, low]])
    return jnp.asarray(along_z), jnp.asarray(along_y)


def call(kernel, outs, scratch=(), flops=0, bytes_accessed=0, specs=None, vmem=12 * MIB, out_specs=None):
    return pl.pallas_call(
        kernel,
        out_shape=outs,
        in_specs=specs,
        out_specs=out_specs or jax.tree.map(lambda _: VMEM, outs),
        scratch_shapes=list(scratch),
        compiler_params=pltpu.CompilerParams(vmem_limit_bytes=vmem),
        cost_estimate=pl.CostEstimate(
            flops=flops, bytes_accessed=bytes_accessed, transcendentals=0
        ),
    )


def pack_kernel(orbitals, panel, out, states, columns, sems):
    copies = [
        pltpu.make_async_copy(source, target, sems.at[i])
        for i, (source, target) in enumerate(
            [
                (panel, columns),
                (orbitals.at[0], states.at[0]),
                (orbitals.at[1], states.at[1]),
            ]
        )
    ]
    for copy in copies:
        copy.start()
    row = lax.axis_index("row")
    place = lax.broadcasted_iota(jnp.int32, (2, GZ), 1)
    copies[0].wait()
    values = columns[...].astype(F32)
    tile = jnp.zeros((2, GZ), F32)
    for k in range(YPART):
        tile = jnp.where(place == YPART * row + k, values[:, k : k + 1], tile)
    tile = jnp.concatenate([tile, jnp.zeros((YPART - 2, GZ), F32)], axis=0).astype(BF16)
    for state in range(2):
        copies[1 + state].wait()
        for pair in range(ROWS // 2):
            target = 2 * pair + state
            begin = (PAIR * pair - REACH) % GX
            head = min(WIDE, GX - begin)
            out[target, 0:head] = states[state, begin : begin + head]
            if head < WIDE:
                out[target, head:WIDE] = states[state, : WIDE - head]
            out[target, WIDE] = tile


def after_kernel(packed, received, out):
    pass


def three_parts(value):
    high = value.astype(BF16).astype(F32)
    rest = value - high
    middle = rest.astype(BF16).astype(F32)
    return high, middle, rest - middle


def given_kernel(potential, points, projector, strength, own, near):
    for p in range(SLAB):
        own[p * GY : (p + 1) * GY, :] = potential[p]
        near[p * GY : (p + 1) * GY, :] = potential[p].astype(BF16)
    at = points[...]
    gains = jnp.concatenate(
        [jnp.full((1, GZ), strength[atom], F32) for atom in range(ATOM_DEV)], axis=0
    )
    own[SLAB_ROWS : SLAB_ROWS + 8, :] = at.astype(F32)
    own[SLAB_ROWS + 8 : SLAB_ROWS + 16, :] = projector[...]
    own[SLAB_ROWS + 16 : SLAB_ROWS + 24, :] = gains
    lane = lax.broadcasted_iota(jnp.int32, (ATOM_DEV, GZ), 1)
    high, middle, low = three_parts(gains)
    tail = [
        lax.shift_right_logical(at, 8).astype(F32),
        (at & 255).astype(F32),
        *three_parts(projector[...]),
        jnp.where(lane == 0, high, jnp.where(lane == 1, middle, low)),
    ]
    near[SLAB_ROWS:NEAR_ROWS, :] = jnp.concatenate(tail, axis=0).astype(BF16)


def densify(points, projector, dense):
    grid_row, lane = lax.shift_right_logical(points, 7), points & (GZ - 1)
    high = projector.astype(BF16).astype(F32)
    parts = (high, projector - high)
    for atom in range(ATOM_DEV):
        rows = jnp.where(
            lax.broadcasted_iota(jnp.int32, (SLAB_ROWS, GZ), 0) == grid_row[atom : atom + 1, :],
            1.0,
            0.0,
        ).astype(BF16)
        at_lane = lax.broadcasted_iota(jnp.int32, (GZ, GZ), 0) == lane[atom : atom + 1, :]
        lanes = [
            jnp.where(at_lane, part[atom : atom + 1, :], 0.0).astype(BF16) for part in parts
        ]
        dense[atom] = lax.dot_general(
            jnp.concatenate([rows] * 2, axis=1),
            jnp.concatenate(lanes, axis=1),
            (((1,), (1,)), ((), ())),
            preferred_element_type=F32,
        )


def project_kernel(own, other, near, dense, gains, built, sems):
    parity = lax.axis_index("row") & 1
    copies = []
    for slab, (pair, index) in enumerate(WINDOW):
        if pair:
            tail = jnp.where(parity == index, own[SLAB_ROWS:OWN_ROWS, :], other[SLAB_ROWS:OWN_ROWS, :])
            points = tail[0:8].astype(jnp.int32)
            projector = tail[8:16]
            gains[slab] = tail[16:24]
        else:
            tail = near[index ^ parity, SLAB_ROWS:NEAR_ROWS, :].astype(F32)
            top, bottom, high, middle, low, gain = (
                tail[ATOM_DEV * i : ATOM_DEV * (i + 1)] for i in range(6)
            )
            points = top.astype(jnp.int32) * 256 + bottom.astype(jnp.int32)
            projector = high + middle + low
            gain = gain[:, 0:1] + gain[:, 1:2] + gain[:, 2:3]
            gains[slab] = jnp.broadcast_to(gain, (ATOM_DEV, GZ))
        densify(points, projector, built.at[slab])
        copies.append(pltpu.make_async_copy(built.at[slab], dense.at[slab], sems.at[slab]))
        copies[-1].start()
    for copy in copies:
        copy.wait()


def apply(source, window, scale, potential, dense, gains, along_z, along_y, wide_z, summed_z, emit):
    count = SLAB * len(window)
    weights = []
    for s, slab in enumerate(window):
        partial = [None] * ATOM_DEV
        for p in range(SLAB):
            value = source[SLAB * (s + 1) + p]
            high = value.astype(BF16)
            low = (value - high.astype(F32)).astype(BF16)
            start = (SLAB * s + p) * GY
            wide_z[start : start + GY, 0:GZ] = high
            wide_z[start : start + GY, GZ : 2 * GZ] = low
            for atom in range(ATOM_DEV):
                weight = dense[slab, atom, p * GY : (p + 1) * GY, :]
                term = jnp.sum((weight * value).reshape(GY // 8, 8, GZ), axis=0)
                partial[atom] = term if p == 0 else partial[atom] + term
        lines = [jnp.sum(term, axis=0, keepdims=True) for term in partial]
        total = jnp.sum(jnp.concatenate(lines, axis=0), axis=1, keepdims=True)
        weights.append(total * gains[slab])
    height = count * GY
    summed_z[0:height, :] = jnp.dot(
        wide_z[0:height, :], along_z[...], preferred_element_type=F32
    )
    for i in range(0, count, 2):
        both = jnp.concatenate(
            [
                jnp.concatenate(
                    [
                        wide_z[start : start + GY, 0:GZ],
                        wide_z[start : start + GY, GZ : 2 * GZ],
                    ],
                    axis=0,
                )
                for start in (i * GY, (i + 1) * GY)
            ],
            axis=1,
        )
        turned = jnp.dot(along_y[...], both, preferred_element_type=F32)
        turned = turned[:GY] + turned[GY:]
        for j in range(2):
            plane = i + j
            s, p = divmod(plane, SLAB)
            slab = window[s]
            at = plane + SLAB
            start = plane * GY
            total = (DIAGONAL + potential(slab, p)) * source[at] + turned[:, j * GZ : (j + 1) * GZ]
            total = total + (
                summed_z[start : start + GY, 0:GZ] + summed_z[start : start + GY, GZ : 2 * GZ]
            )
            for atom in range(ATOM_DEV):
                total = (
                    total
                    + weights[s][atom : atom + 1, :] * dense[slab, atom, p * GY : (p + 1) * GY, :]
                )
            for offset in range(1, 7):
                total = total + SIDE[offset] * (source[at - offset] + source[at + offset])
            emit(plane, scale * total)


def filter_kernel(
    received, own, other, near, projectors, gains, along_z, along_y,
    out, start, first, second, last, dense, potentials, wide_z, summed_z, sems,
):
    parity = lax.axis_index("row") & 1
    copies = [
        pltpu.make_async_copy(projectors.at[slab], dense.at[slab], sems.at[slab])
        for slab in range(SLABS)
    ]
    for copy in copies:
        copy.start()
    panel = jnp.zeros((YPART, GZ), F32)
    for source in range(ROWS):
        start[:, source * YPART : (source + 1) * YPART, :] = received[source, 0:WIDE].astype(F32)
        panel = panel + received[source, WIDE].astype(F32)
    potentials[parity] = own[0:SLAB_ROWS, :]
    potentials[1 - parity] = other[0:SLAB_ROWS, :]

    def potential(slab, p):
        pair, index = WINDOW[slab]
        rows = slice(p * GY, (p + 1) * GY)
        if pair:
            return potentials[index, rows, :]
        return near[index ^ parity, rows, :].astype(F32)

    for copy in copies:
        copy.wait()
    work = (potential, dense, gains, along_z, along_y, wide_z, summed_z)

    def emit_first(plane, value):
        first[plane] = value

    def emit_second(plane, value):
        second[plane] = value - start[plane + 2 * SLAB]

    def emit_last(plane, value):
        s, p = divmod(plane, SLAB)
        last[s, p * GY : (p + 1) * GY, :] = value - first[plane + 2 * SLAB]

    apply(start, (0, 1, 2, 3, 4, 5), 1.0 / HALF_WIDTH, *work, emit_first)
    apply(first, (1, 2, 3, 4), 2.0 / HALF_WIDTH, *work, emit_second)
    apply(second, (2, 3), 2.0 / HALF_WIDTH, *work, emit_last)

    line = lax.broadcasted_iota(jnp.int32, (4, GZ), 0)
    mine = jnp.where(parity == 0, panel[0:1], panel[1:2])
    tile = jnp.where(line == 0, mine, 0.0).astype(BF16)
    for half in range(2):
        for col in range(COLS):
            member = half * COLS + col
            for k in range(PIECE):
                at = 4 * (PIECE * col + k)
                out[member, k] = last[half, at : at + 4, :].astype(BF16)
            out[member, PIECE] = tile


def rotate_kernel(received, panel_rows, out, states, wanted, rotated):
    members = 2 * COLS
    size = 4 * members
    for member in range(members):
        at = slice(4 * member, 4 * member + 4)
        for k in range(PIECE):
            states[at, k * GZ : (k + 1) * GZ] = received[member, k].astype(F32)
        tile = received[member, PIECE].astype(F32)
        wanted[at, :] = jnp.broadcast_to(tile[0:1], (4, GZ))
    order = lax.broadcasted_iota(jnp.int32, (size, 64), 0) >> 2
    state_of = 2 * (order & (COLS - 1)) + lax.shift_right_logical(order, 5)
    stored = jnp.where(panel_rows[...] == state_of, 1.0, 0.0).astype(BF16)
    spread = lax.dot_general(
        wanted[:, 0:64].astype(BF16), stored, (((1,), (1,)), ((), ())),
        preferred_element_type=F32,
    )
    same = (
        lax.broadcasted_iota(jnp.int32, (size, size), 0) & 3
    ) == (lax.broadcasted_iota(jnp.int32, (size, size), 1) & 3)
    spread = jnp.where(same, spread, 0.0).astype(BF16)
    rotated[...] = jnp.dot(spread, states[...].astype(BF16), preferred_element_type=F32)
    for col in range(COLS):
        for state in range(2):
            at = 4 * (state * COLS + col)
            for k in range(PIECE):
                out[col, state * PIECE + k] = rotated[
                    at : at + 4, k * GZ : (k + 1) * GZ
                ].astype(BF16)


def place_kernel(received, out):
    for col in range(COLS):
        for state in range(2):
            for k in range(PIECE):
                at = 4 * (PIECE * col + k)
                out[state, at : at + 4, :] = received[col, state * PIECE + k].astype(F32)


def per_device(orbitals, potential, proj_points, projector, strength, ritz_panel, panel_rows):
    shape = jax.ShapeDtypeStruct
    along_z, along_y = stencil_matrices()
    smem = pl.BlockSpec(memory_space=pltpu.SMEM)
    axes = ("row", "col")

    own, near = call(
        given_kernel,
        (shape((OWN_ROWS, GZ), F32), shape((NEAR_ROWS, GZ), BF16)),
        specs=[VMEM] * 3 + [smem],
    )(potential, proj_points, projector, strength)
    offsets = ((-2, -1, 2, 3), (-2, -3, 2, 1))
    fetched = lax.ppermute(
        near,
        axes,
        [
            ((row + offsets[row % 2][col % 4]) % ROWS * COLS + col, row * COLS + col)
            for row in range(ROWS)
            for col in range(COLS)
        ],
    )
    packed = call(
        pack_kernel,
        shape((ROWS, SENT, YPART, GZ), BF16),
        scratch=[
            pltpu.VMEM((2, GX, YPART, GZ), BF16),
            pltpu.VMEM((2, YPART), BF16),
            pltpu.SemaphoreType.DMA((3,)),
        ],
        specs=[ANY] * 2,
        vmem=60 * MIB,
        flops=1_000_000,
        bytes_accessed=1_000_000,
    )(orbitals, ritz_panel.T)
    packed = pl.pallas_call(
        after_kernel,
        out_shape=shape(packed.shape, packed.dtype),
        in_specs=[ANY] * 2,
        out_specs=ANY,
        input_output_aliases={0: 0},
    )(packed, fetched)
    regrouped = lax.all_to_all(packed, "row", split_axis=0, concat_axis=0, tiled=True)
    other = lax.ppermute(own, "row", [(i, i ^ 1) for i in range(ROWS)])
    near = lax.all_gather(
        fetched,
        "col",
        axis=0,
        axis_index_groups=[[4 * i + k for k in range(4)] for i in range(COLS // 4)],
    )
    projectors, gains = call(
        project_kernel,
        (shape((SLABS, ATOM_DEV, SLAB_ROWS, GZ), F32), shape((SLABS, ATOM_DEV, GZ), F32)),
        scratch=[
            pltpu.VMEM((SLABS, ATOM_DEV, SLAB_ROWS, GZ), F32),
            pltpu.SemaphoreType.DMA((SLABS,)),
        ],
        specs=[VMEM] * 3,
        flops=4_000_000_000,
        bytes_accessed=10_000_000,
        vmem=24 * MIB,
        out_specs=(ANY, VMEM),
    )(own, other, near)
    layered = call(
        filter_kernel,
        shape((2 * COLS, PIECE + 1, 4, GZ), BF16),
        scratch=[
            pltpu.VMEM((WIDE, GY, GZ), F32),
            pltpu.VMEM((WIDE - PAIR, GY, GZ), F32),
            pltpu.VMEM((WIDE - 2 * PAIR, GY, GZ), F32),
            pltpu.VMEM((2, SLAB_ROWS, GZ), F32),
            pltpu.VMEM((SLABS, ATOM_DEV, SLAB_ROWS, GZ), F32),
            pltpu.VMEM((2, SLAB_ROWS, GZ), F32),
            pltpu.VMEM((SLABS * SLAB_ROWS, 2 * GZ), BF16),
            pltpu.VMEM((SLABS * SLAB_ROWS, 2 * GZ), F32),
            pltpu.SemaphoreType.DMA((SLABS,)),
        ],
        specs=[VMEM] * 4 + [ANY] + [VMEM] * 3,
        vmem=40 * MIB,
    )(regrouped, own, other, near, projectors, gains, along_z, along_y)
    columns = lax.all_to_all(
        layered,
        axes,
        split_axis=0,
        concat_axis=0,
        tiled=True,
        axis_index_groups=[
            [row * COLS + col for row in (2 * i, 2 * i + 1) for col in range(COLS)]
            for i in range(ROWS // 2)
        ],
    )
    turned = call(
        rotate_kernel,
        shape((COLS, 2 * PIECE, 4, GZ), BF16),
        scratch=[
            pltpu.VMEM((8 * COLS, PIECE * GZ), F32),
            pltpu.VMEM((8 * COLS, GZ), F32),
            pltpu.VMEM((8 * COLS, PIECE * GZ), F32),
        ],
        specs=[VMEM] * 2,
    )(columns, panel_rows.reshape(1, -1))
    result = lax.all_to_all(turned, "col", split_axis=0, concat_axis=0, tiled=True)
    whole = call(place_kernel, shape((2, SLAB_ROWS, GZ), F32), specs=[VMEM])(result)
    return whole.reshape(2, SLAB, GY, GZ)


def solution(mesh):
    placed = (
        P("col", None, "row", None),
        P("row", None, None),
        P("row", None),
        P("row", None),
        P("row"),
        P("row", "col"),
        P(),
    )
    return jax.shard_map(
        per_device,
        mesh=mesh,
        in_specs=placed,
        out_specs=P("col", "row", None, None),
        check_vma=False,
    )
```

```python
import functools

import jax
import jax.numpy as jnp
import numpy as np
from jax import lax
from jax.experimental import pallas as pl
from jax.experimental.pallas import tpu as pltpu
from jax.sharding import PartitionSpec as P

F32 = jnp.float32
BF16 = jnp.bfloat16

STENCIL = (
    -5369.0 / 1800.0,
    12.0 / 7.0,
    -15.0 / 56.0,
    10.0 / 189.0,
    -1.0 / 112.0,
    2.0 / 1925.0,
    -1.0 / 16632.0,
)
CENTER = 7.0
HALF_WIDTH = 5.0

ROWS, COLS = 16, 32
SLAB, GY, GZ = 6, 64, 128
GX = ROWS * SLAB
YPART = GY // ROWS
WIDE = 3 * SLAB
ATOM_DEV = 8
SLAB_ROWS = SLAB * GY
SENT = 2 * WIDE + 1
HALF = ROWS // 2
PIECE = SLAB_ROWS // COLS // 4
OTHER_ROWS = SLAB_ROWS + 3 * ATOM_DEV

SIDE = tuple(-0.5 * c for c in STENCIL)
DIAGONAL = -0.5 * 3.0 * STENCIL[0] - CENTER

VMEM = pl.BlockSpec(memory_space=pltpu.VMEM)
MIB = 1024 * 1024


def circulant(size):
    whole = np.zeros((size, size), np.float32)
    for offset in range(1, 7):
        for i in range(size):
            whole[i, (i + offset) % size] += SIDE[offset]
            whole[i, (i - offset) % size] += SIDE[offset]
    high = whole.astype(jnp.bfloat16)
    low = (whole - high.astype(np.float32)).astype(jnp.bfloat16)
    return high, low


def stencil_matrices():
    high, low = circulant(GZ)
    along_z = np.block([[high, low], [high, low]])
    high, low = circulant(GY)
    along_y = np.block([[high, high], [low, low]])
    return jnp.asarray(along_z), jnp.asarray(along_y)


def call(kernel, outs, scratch=(), flops=0, bytes_accessed=0, specs=None, vmem=12 * MIB):
    return pl.pallas_call(
        kernel,
        out_shape=outs,
        in_specs=specs,
        out_specs=jax.tree.map(lambda _: VMEM, outs),
        scratch_shapes=list(scratch),
        compiler_params=pltpu.CompilerParams(vmem_limit_bytes=vmem),
        cost_estimate=pl.CostEstimate(
            flops=flops, bytes_accessed=bytes_accessed, transcendentals=0
        ),
    )


def pack_kernel(orbitals, panel, out, states, columns, sems):
    copies = [
        pltpu.make_async_copy(source, target, sems.at[i])
        for i, (source, target) in enumerate(
            [
                (panel, columns),
                (orbitals.at[0], states.at[0]),
                (orbitals.at[1], states.at[1]),
            ]
        )
    ]
    for copy in copies:
        copy.start()
    row = lax.axis_index("row")
    place = lax.broadcasted_iota(jnp.int32, (2, GZ), 1)
    copies[0].wait()
    values = columns[...].astype(F32)
    tile = jnp.zeros((2, GZ), F32)
    for k in range(YPART):
        tile = jnp.where(place == YPART * row + k, values[:, k : k + 1], tile)
    tile = jnp.concatenate([tile, jnp.zeros((YPART - 2, GZ), F32)], axis=0).astype(BF16)
    for state in range(2):
        copies[1 + state].wait()
        for target in range(HALF * state, HALF * state + HALF):
            for index, slab in enumerate((target, target ^ HALF)):
                begin = (SLAB * slab - SLAB) % GX
                base = index * WIDE
                head = min(WIDE, GX - begin)
                out[target, base : base + head] = states[state, begin : begin + head]
                if head < WIDE:
                    out[target, base + head : base + WIDE] = states[state, : WIDE - head]
            out[target, 2 * WIDE] = tile


def other_kernel(potential, points, projector, strength, out):
    for p in range(SLAB):
        out[p * GY : (p + 1) * GY, :] = potential[p]
    out[SLAB_ROWS : SLAB_ROWS + 8, :] = points[...].astype(F32)
    out[SLAB_ROWS + 8 : SLAB_ROWS + 16, :] = projector[...]
    for atom in range(ATOM_DEV):
        at = SLAB_ROWS + 16 + atom
        out[at : at + 1, :] = jnp.full((1, GZ), strength[atom], F32)


def densify(points, projector, dense):
    grid_row, lane = lax.shift_right_logical(points, 7), points & (GZ - 1)
    high = projector.astype(BF16).astype(F32)
    parts = (high, projector - high)
    for atom in range(ATOM_DEV):
        rows = jnp.where(
            lax.broadcasted_iota(jnp.int32, (SLAB_ROWS, GZ), 0) == grid_row[atom : atom + 1, :],
            1.0,
            0.0,
        ).astype(BF16)
        at_lane = lax.broadcasted_iota(jnp.int32, (GZ, GZ), 0) == lane[atom : atom + 1, :]
        lanes = [
            jnp.where(at_lane, part[atom : atom + 1, :], 0.0).astype(BF16) for part in parts
        ]
        dense[atom] = lax.dot_general(
            jnp.concatenate([rows] * 2, axis=1),
            jnp.concatenate(lanes, axis=1),
            (((1,), (1,)), ((), ())),
            preferred_element_type=F32,
        )


def project_kernel(points, projector, strength, dense, gains):
    densify(points[...], projector[...], dense)
    for atom in range(ATOM_DEV):
        gains[atom : atom + 1, :] = jnp.full((1, GZ), strength[atom], F32)


def other_projectors(given, dense):
    points = given[SLAB_ROWS : SLAB_ROWS + 8, :].astype(jnp.int32)
    densify(points, given[SLAB_ROWS + 8 : SLAB_ROWS + 16, :], dense)
    return given.at[SLAB_ROWS + 16 : SLAB_ROWS + 24]


def apply(planes, reach, scale, potentials, denses, gains, along_z, along_y, wide_z, summed_z, emit):
    weights = []
    for slab in range(2):
        partial = [None] * ATOM_DEV
        for p in range(SLAB):
            value = planes(slab, p)
            high = value.astype(BF16)
            low = (value - high.astype(F32)).astype(BF16)
            start = (slab * SLAB + p) * GY
            wide_z[start : start + GY, 0:GZ] = high
            wide_z[start : start + GY, GZ : 2 * GZ] = low
            for atom in range(ATOM_DEV):
                weight = denses[slab][atom, p * GY : (p + 1) * GY, :]
                term = jnp.sum((weight * value).reshape(GY // 8, 8, GZ), axis=0)
                partial[atom] = term if p == 0 else partial[atom] + term
        lines = [jnp.sum(term, axis=0, keepdims=True) for term in partial]
        total = jnp.sum(jnp.concatenate(lines, axis=0), axis=1, keepdims=True)
        weights.append(total * gains[slab][...])
    summed_z[...] = jnp.dot(wide_z[...], along_z[...], preferred_element_type=F32)
    for p in range(SLAB):
        both = jnp.concatenate(
            [
                jnp.concatenate(
                    [
                        wide_z[start : start + GY, 0:GZ],
                        wide_z[start : start + GY, GZ : 2 * GZ],
                    ],
                    axis=0,
                )
                for start in (p * GY, (SLAB + p) * GY)
            ],
            axis=1,
        )
        turned = jnp.dot(along_y[...], both, preferred_element_type=F32)
        turned = turned[:GY] + turned[GY:]
        for slab in range(2):
            start = (slab * SLAB + p) * GY
            level = DIAGONAL + potentials[slab](p)
            total = level * planes(slab, p) + turned[:, slab * GZ : (slab + 1) * GZ]
            total = total + (
                summed_z[start : start + GY, 0:GZ] + summed_z[start : start + GY, GZ : 2 * GZ]
            )
            for atom in range(ATOM_DEV):
                total = (
                    total
                    + weights[slab][atom : atom + 1, :]
                    * denses[slab][atom, p * GY : (p + 1) * GY, :]
                )
            for offset in range(1, 7):
                terms = [
                    planes(slab, k)
                    for k in (p - offset, p + offset)
                    if -reach <= k < SLAB + reach
                ]
                if terms:
                    total = total + SIDE[offset] * functools.reduce(jnp.add, terms)
            emit(slab, p, scale * total)


def potentials_of(own, other):
    return (lambda p: own[p]), (lambda p: other[p * GY : (p + 1) * GY, :])


def first_kernel(
    received, potential, other, dense, gains, along_z, along_y,
    start_out, next_out, sent_out, panel_out, slabs, other_dense, wide_z, summed_z,
):
    other_gains = other_projectors(other, other_dense)
    panel = jnp.zeros((YPART, GZ), F32)
    for source in range(ROWS):
        for slab in range(2):
            slabs[slab, :, source * YPART : (source + 1) * YPART, :] = received[
                source, slab * WIDE : (slab + 1) * WIDE
            ].astype(F32)
        panel = panel + received[source, 2 * WIDE].astype(F32)
    mine = jnp.where(lax.axis_index("row") < HALF, panel[0:1], panel[1:2])
    panel_out[...] = jnp.broadcast_to(mine, (8, GZ))
    for slab in range(2):
        start_out[slab] = slabs[slab, SLAB : 2 * SLAB]

    def emit(slab, p, value):
        next_out[slab, p] = value
        sent_out[slab, p] = value.astype(BF16)

    apply(
        lambda slab, p: slabs[slab, SLAB + p], SLAB, 1.0 / HALF_WIDTH,
        potentials_of(potential, other), (dense, other_dense), (gains, other_gains),
        along_z, along_y, wide_z, summed_z, emit,
    )


def inside_kernel(
    current, previous, potential, other, dense, gains, along_z, along_y,
    out, other_dense, wide_z, summed_z,
):
    other_gains = other_projectors(other, other_dense)

    def emit(slab, p, value):
        out[slab, p] = value - previous[slab, p]

    apply(
        lambda slab, p: current[slab, p], 0, 2.0 / HALF_WIDTH,
        potentials_of(potential, other), (dense, other_dense), (gains, other_gains),
        along_z, along_y, wide_z, summed_z, emit,
    )


def joining(partial, below, above):
    column = lax.axis_index("row") & (HALF - 1)
    lower = jnp.where(column == 0, 1, 0)
    upper = jnp.where(column == HALF - 1, 1, 0)

    def joined(slab, p):
        total = partial[slab, p]
        lower_slab = lower ^ slab
        upper_slab = upper ^ slab
        for offset in range(1, 7):
            terms = []
            if p - offset < 0:
                terms.append(below[lower_slab, SLAB + p - offset].astype(F32))
            if p + offset >= SLAB:
                terms.append(above[upper_slab, p + offset - SLAB].astype(F32))
            if terms:
                side = (2.0 / HALF_WIDTH) * SIDE[offset]
                total = total + side * functools.reduce(jnp.add, terms)
        return total

    return joined


def join_kernel(partial, below, above, next_out, sent_out):
    joined = joining(partial, below, above)
    for p in range(SLAB):
        for slab in range(2):
            value = joined(slab, p)
            next_out[slab, p] = value
            sent_out[slab, p] = value.astype(BF16)


def last_kernel(partial, below, above, panel, out, slabs):
    joined = joining(partial, below, above)
    for p in range(SLAB):
        for slab in range(2):
            slabs[slab, p * GY : (p + 1) * GY, :] = joined(slab, p)
    upper = lax.axis_index("row") // HALF
    line = lax.broadcasted_iota(jnp.int32, (4, GZ), 0)
    tile = jnp.where(line == 0, panel[0:4], 0.0).astype(BF16)
    for half in range(2):
        slab = upper ^ half
        for col in range(COLS):
            member = half * COLS + col
            for k in range(PIECE):
                at = 4 * (PIECE * col + k)
                out[member, k] = slabs[slab, at : at + 4, :].astype(BF16)
            out[member, PIECE] = tile


def rotate_kernel(received, panel_rows, out, states, wanted, rotated):
    members = 2 * COLS
    size = 4 * members
    for member in range(members):
        at = slice(4 * member, 4 * member + 4)
        for k in range(PIECE):
            states[at, k * GZ : (k + 1) * GZ] = received[member, k].astype(F32)
        tile = received[member, PIECE].astype(F32)
        wanted[at, :] = jnp.broadcast_to(tile[0:1], (4, GZ))
    order = lax.broadcasted_iota(jnp.int32, (size, 64), 0) >> 2
    state_of = 2 * (order & (COLS - 1)) + lax.shift_right_logical(order, 5)
    stored = jnp.where(panel_rows[...] == state_of, 1.0, 0.0).astype(BF16)
    spread = lax.dot_general(
        wanted[:, 0:64].astype(BF16), stored, (((1,), (1,)), ((), ())),
        preferred_element_type=F32,
    )
    same = (
        lax.broadcasted_iota(jnp.int32, (size, size), 0) & 3
    ) == (lax.broadcasted_iota(jnp.int32, (size, size), 1) & 3)
    spread = jnp.where(same, spread, 0.0).astype(BF16)
    rotated[...] = jnp.dot(spread, states[...].astype(BF16), preferred_element_type=F32)
    for col in range(COLS):
        for state in range(2):
            at = 4 * (state * COLS + col)
            for k in range(PIECE):
                out[col, state * PIECE + k] = rotated[
                    at : at + 4, k * GZ : (k + 1) * GZ
                ].astype(BF16)


def place_kernel(received, out):
    for col in range(COLS):
        for state in range(2):
            for k in range(PIECE):
                at = 4 * (PIECE * col + k)
                out[state, at : at + 4, :] = received[col, state * PIECE + k].astype(F32)


def per_device(orbitals, potential, proj_points, projector, strength, ritz_panel, panel_rows):
    shape = jax.ShapeDtypeStruct
    slabs_f32 = shape((2, SLAB, GY, GZ), F32)
    slabs_bf16 = shape((2, SLAB, GY, GZ), BF16)
    dense_gains = (shape((ATOM_DEV, SLAB_ROWS, GZ), F32), shape((ATOM_DEV, GZ), F32))
    along_z, along_y = stencil_matrices()
    smem = pl.BlockSpec(memory_space=pltpu.SMEM)
    work = [
        pltpu.VMEM((ATOM_DEV, SLAB_ROWS, GZ), F32),
        pltpu.VMEM((2 * SLAB_ROWS, 2 * GZ), BF16),
        pltpu.VMEM((2 * SLAB_ROWS, 2 * GZ), F32),
    ]
    around = [(i, i // HALF * HALF + (i + 1) % HALF) for i in range(ROWS)]

    packed = call(
        pack_kernel,
        shape((ROWS, SENT, YPART, GZ), BF16),
        scratch=[
            pltpu.VMEM((2, GX, YPART, GZ), BF16),
            pltpu.VMEM((2, YPART), BF16),
            pltpu.SemaphoreType.DMA((3,)),
        ],
        specs=[pl.BlockSpec(memory_space=pl.ANY)] * 2,
        vmem=60 * MIB,
    )(orbitals, ritz_panel.T)
    regrouped = lax.all_to_all(packed, "row", split_axis=0, concat_axis=0, tiled=True)
    given = call(
        other_kernel,
        shape((OTHER_ROWS, GZ), F32),
        specs=[VMEM] * 3 + [smem],
        flops=1_000_000,
        bytes_accessed=400_000,
    )(potential, proj_points, projector, strength)
    other = lax.ppermute(given, "row", [(i, i ^ HALF) for i in range(ROWS)])
    dense, gains = call(
        project_kernel,
        dense_gains,
        specs=[VMEM, VMEM, smem],
        flops=1_000_000_000,
        bytes_accessed=1_600_000,
    )(proj_points, projector, strength)
    fixed = (potential, other, dense, gains, along_z, along_y)
    previous, current, sent, panel = call(
        first_kernel,
        (slabs_f32, slabs_f32, slabs_bf16, shape((8, GZ), F32)),
        scratch=[pltpu.VMEM((2, WIDE, GY, GZ), F32)] + work,
        specs=[VMEM] * 7,
    )(regrouped, *fixed)
    for step in range(2):
        above = lax.ppermute(sent, "row", [(d, s) for s, d in around])
        below = lax.ppermute(sent, "row", around)
        partial = call(
            inside_kernel,
            slabs_f32,
            scratch=work,
            specs=[VMEM] * 8,
            flops=2_000_000_000,
            bytes_accessed=3_000_000,
        )(current, previous, *fixed)
        if step == 0:
            previous = current
            current, sent = call(join_kernel, (slabs_f32, slabs_bf16), specs=[VMEM] * 3)(
                partial, below, above
            )
    layered = call(
        last_kernel,
        shape((2 * COLS, PIECE + 1, 4, GZ), BF16),
        scratch=[pltpu.VMEM((2, SLAB_ROWS, GZ), F32)],
        specs=[VMEM] * 4,
    )(partial, below, above, panel)
    both = [
        [(i + HALF * half) * COLS + col for half in range(2) for col in range(COLS)]
        for i in range(HALF)
    ]
    columns = lax.all_to_all(
        layered, ("row", "col"), split_axis=0, concat_axis=0, tiled=True, axis_index_groups=both
    )
    turned = call(
        rotate_kernel,
        shape((COLS, 2 * PIECE, 4, GZ), BF16),
        scratch=[
            pltpu.VMEM((8 * COLS, PIECE * GZ), F32),
            pltpu.VMEM((8 * COLS, GZ), F32),
            pltpu.VMEM((8 * COLS, PIECE * GZ), F32),
        ],
        specs=[VMEM] * 2,
    )(columns, panel_rows.reshape(1, -1))
    result = lax.all_to_all(turned, "col", split_axis=0, concat_axis=0, tiled=True)
    whole = call(place_kernel, shape((2, SLAB_ROWS, GZ), F32), specs=[VMEM])(result)
    return whole.reshape(2, SLAB, GY, GZ)


def solution(mesh):
    placed = (
        P("col", None, "row", None),
        P("row", None, None),
        P("row", None),
        P("row", None),
        P("row"),
        P("row", "col"),
        P(),
    )
    return jax.shard_map(
        per_device,
        mesh=mesh,
        in_specs=placed,
        out_specs=P("col", "row", None, None),
        check_vma=False,
    )
```

```python
import functools

import jax
import jax.numpy as jnp
import numpy as np
from jax import lax
from jax.experimental import pallas as pl
from jax.experimental.pallas import tpu as pltpu
from jax.sharding import PartitionSpec as P

F32 = jnp.float32
BF16 = jnp.bfloat16

STENCIL = (
    -5369.0 / 1800.0,
    12.0 / 7.0,
    -15.0 / 56.0,
    10.0 / 189.0,
    -1.0 / 112.0,
    2.0 / 1925.0,
    -1.0 / 16632.0,
)
CENTER = 7.0
HALF_WIDTH = 5.0

ROWS, COLS = 16, 32
SLAB, GY, GZ = 6, 64, 128
GX = ROWS * SLAB
YPART = GY // ROWS
WIDE = 3 * SLAB
ATOM_DEV = 8
SLAB_ROWS = SLAB * GY
SENT = 2 * WIDE + 1
HALF = ROWS // 2
PIECE = SLAB_ROWS // COLS // 4
OTHER_ROWS = SLAB_ROWS + 3 * ATOM_DEV

SIDE = tuple(-0.5 * c for c in STENCIL)
DIAGONAL = -0.5 * 3.0 * STENCIL[0] - CENTER

VMEM = pl.BlockSpec(memory_space=pltpu.VMEM)
MIB = 1024 * 1024


def circulant(size):
    whole = np.zeros((size, size), np.float32)
    for offset in range(1, 7):
        for i in range(size):
            whole[i, (i + offset) % size] += SIDE[offset]
            whole[i, (i - offset) % size] += SIDE[offset]
    high = whole.astype(jnp.bfloat16)
    low = (whole - high.astype(np.float32)).astype(jnp.bfloat16)
    return high, low


def stencil_matrices():
    high, low = circulant(GZ)
    along_z = np.block([[high, low], [high, low]])
    high, low = circulant(GY)
    along_y = np.block([[high, high], [low, low]])
    return jnp.asarray(along_z), jnp.asarray(along_y)


def call(kernel, outs, scratch=(), flops=0, bytes_accessed=0, specs=None, vmem=12 * MIB):
    return pl.pallas_call(
        kernel,
        out_shape=outs,
        in_specs=specs,
        out_specs=jax.tree.map(lambda _: VMEM, outs),
        scratch_shapes=list(scratch),
        compiler_params=pltpu.CompilerParams(vmem_limit_bytes=vmem),
        cost_estimate=pl.CostEstimate(
            flops=flops, bytes_accessed=bytes_accessed, transcendentals=0
        ),
    )


def pack_kernel(orbitals, panel, out, states, columns, sems):
    copies = [
        pltpu.make_async_copy(source, target, sems.at[i])
        for i, (source, target) in enumerate(
            [
                (panel, columns),
                (orbitals.at[0], states.at[0]),
                (orbitals.at[1], states.at[1]),
            ]
        )
    ]
    for copy in copies:
        copy.start()
    row = lax.axis_index("row")
    place = lax.broadcasted_iota(jnp.int32, (2, GZ), 1)
    copies[0].wait()
    values = columns[...].astype(F32)
    tile = jnp.zeros((2, GZ), F32)
    for k in range(YPART):
        tile = jnp.where(place == YPART * row + k, values[:, k : k + 1], tile)
    tile = jnp.concatenate([tile, jnp.zeros((YPART - 2, GZ), F32)], axis=0).astype(BF16)
    for state in range(2):
        copies[1 + state].wait()
        for target in range(HALF * state, HALF * state + HALF):
            for index, slab in enumerate((target, target ^ HALF)):
                begin = (SLAB * slab - SLAB) % GX
                base = index * WIDE
                head = min(WIDE, GX - begin)
                out[target, base : base + head] = states[state, begin : begin + head]
                if head < WIDE:
                    out[target, base + head : base + WIDE] = states[state, : WIDE - head]
            out[target, 2 * WIDE] = tile


def other_kernel(potential, points, projector, strength, out):
    for p in range(SLAB):
        out[p * GY : (p + 1) * GY, :] = potential[p]
    out[SLAB_ROWS : SLAB_ROWS + 8, :] = points[...].astype(F32)
    out[SLAB_ROWS + 8 : SLAB_ROWS + 16, :] = projector[...]
    for atom in range(ATOM_DEV):
        at = SLAB_ROWS + 16 + atom
        out[at : at + 1, :] = jnp.full((1, GZ), strength[atom], F32)


def densify(points, projector, dense):
    grid_row, lane = lax.shift_right_logical(points, 7), points & (GZ - 1)
    high = projector.astype(BF16).astype(F32)
    parts = (high, projector - high)
    for atom in range(ATOM_DEV):
        rows = jnp.where(
            lax.broadcasted_iota(jnp.int32, (SLAB_ROWS, GZ), 0) == grid_row[atom : atom + 1, :],
            1.0,
            0.0,
        ).astype(BF16)
        at_lane = lax.broadcasted_iota(jnp.int32, (GZ, GZ), 0) == lane[atom : atom + 1, :]
        lanes = [
            jnp.where(at_lane, part[atom : atom + 1, :], 0.0).astype(BF16) for part in parts
        ]
        dense[atom] = lax.dot_general(
            jnp.concatenate([rows] * 2, axis=1),
            jnp.concatenate(lanes, axis=1),
            (((1,), (1,)), ((), ())),
            preferred_element_type=F32,
        )


def project_kernel(points, projector, strength, dense, gains):
    densify(points[...], projector[...], dense)
    for atom in range(ATOM_DEV):
        gains[atom : atom + 1, :] = jnp.full((1, GZ), strength[atom], F32)


def other_projectors(given, dense):
    points = given[SLAB_ROWS : SLAB_ROWS + 8, :].astype(jnp.int32)
    densify(points, given[SLAB_ROWS + 8 : SLAB_ROWS + 16, :], dense)
    return given.at[SLAB_ROWS + 16 : SLAB_ROWS + 24]


def apply(planes, reach, scale, potentials, denses, gains, along_z, along_y, wide_z, summed_z, emit):
    weights = []
    for slab in range(2):
        partial = [None] * ATOM_DEV
        for p in range(SLAB):
            value = planes(slab, p)
            high = value.astype(BF16)
            low = (value - high.astype(F32)).astype(BF16)
            start = (slab * SLAB + p) * GY
            wide_z[start : start + GY, 0:GZ] = high
            wide_z[start : start + GY, GZ : 2 * GZ] = low
            for atom in range(ATOM_DEV):
                weight = denses[slab][atom, p * GY : (p + 1) * GY, :]
                term = jnp.sum((weight * value).reshape(GY // 8, 8, GZ), axis=0)
                partial[atom] = term if p == 0 else partial[atom] + term
        lines = [jnp.sum(term, axis=0, keepdims=True) for term in partial]
        total = jnp.sum(jnp.concatenate(lines, axis=0), axis=1, keepdims=True)
        weights.append(total * gains[slab][...])
    summed_z[...] = jnp.dot(wide_z[...], along_z[...], preferred_element_type=F32)
    for p in range(SLAB):
        both = jnp.concatenate(
            [
                jnp.concatenate(
                    [
                        wide_z[start : start + GY, 0:GZ],
                        wide_z[start : start + GY, GZ : 2 * GZ],
                    ],
                    axis=0,
                )
                for start in (p * GY, (SLAB + p) * GY)
            ],
            axis=1,
        )
        turned = jnp.dot(along_y[...], both, preferred_element_type=F32)
        turned = turned[:GY] + turned[GY:]
        for slab in range(2):
            start = (slab * SLAB + p) * GY
            level = DIAGONAL + potentials[slab](p)
            total = level * planes(slab, p) + turned[:, slab * GZ : (slab + 1) * GZ]
            total = total + (
                summed_z[start : start + GY, 0:GZ] + summed_z[start : start + GY, GZ : 2 * GZ]
            )
            for atom in range(ATOM_DEV):
                total = (
                    total
                    + weights[slab][atom : atom + 1, :]
                    * denses[slab][atom, p * GY : (p + 1) * GY, :]
                )
            for offset in range(1, 7):
                terms = [
                    planes(slab, k)
                    for k in (p - offset, p + offset)
                    if -reach <= k < SLAB + reach
                ]
                if terms:
                    total = total + SIDE[offset] * functools.reduce(jnp.add, terms)
            emit(slab, p, scale * total)


def potentials_of(own, other):
    return (lambda p: own[p]), (lambda p: other[p * GY : (p + 1) * GY, :])


def first_kernel(
    received, potential, other, dense, gains, along_z, along_y,
    start_out, next_out, sent_out, panel_out, slabs, other_dense, wide_z, summed_z,
):
    other_gains = other_projectors(other, other_dense)
    panel = jnp.zeros((YPART, GZ), F32)
    for source in range(ROWS):
        for slab in range(2):
            slabs[slab, :, source * YPART : (source + 1) * YPART, :] = received[
                source, slab * WIDE : (slab + 1) * WIDE
            ].astype(F32)
        panel = panel + received[source, 2 * WIDE].astype(F32)
    mine = jnp.where(lax.axis_index("row") < HALF, panel[0:1], panel[1:2])
    panel_out[...] = jnp.broadcast_to(mine, (8, GZ))
    for slab in range(2):
        start_out[slab] = slabs[slab, SLAB : 2 * SLAB]

    def emit(slab, p, value):
        next_out[slab, p] = value
        sent_out[slab, p] = value.astype(BF16)

    apply(
        lambda slab, p: slabs[slab, SLAB + p], SLAB, 1.0 / HALF_WIDTH,
        potentials_of(potential, other), (dense, other_dense), (gains, other_gains),
        along_z, along_y, wide_z, summed_z, emit,
    )


def inside_kernel(
    current, previous, potential, other, dense, gains, along_z, along_y,
    out, other_dense, wide_z, summed_z,
):
    other_gains = other_projectors(other, other_dense)

    def emit(slab, p, value):
        out[slab, p] = value - previous[slab, p]

    apply(
        lambda slab, p: current[slab, p], 0, 2.0 / HALF_WIDTH,
        potentials_of(potential, other), (dense, other_dense), (gains, other_gains),
        along_z, along_y, wide_z, summed_z, emit,
    )


def joining(partial, below, above):
    column = lax.axis_index("row") & (HALF - 1)
    lower = jnp.where(column == 0, 1, 0)
    upper = jnp.where(column == HALF - 1, 1, 0)

    def joined(slab, p):
        total = partial[slab, p]
        lower_slab = lower ^ slab
        upper_slab = upper ^ slab
        for offset in range(1, 7):
            terms = []
            if p - offset < 0:
                terms.append(below[lower_slab, SLAB + p - offset].astype(F32))
            if p + offset >= SLAB:
                terms.append(above[upper_slab, p + offset - SLAB].astype(F32))
            if terms:
                side = (2.0 / HALF_WIDTH) * SIDE[offset]
                total = total + side * functools.reduce(jnp.add, terms)
        return total

    return joined


def join_kernel(partial, above, below, next_out, sent_out):
    joined = joining(partial, below, above)
    for p in range(SLAB):
        for slab in range(2):
            value = joined(slab, p)
            next_out[slab, p] = value
            sent_out[slab, p] = value.astype(BF16)


def last_kernel(partial, above, below, panel, out, slabs):
    joined = joining(partial, below, above)
    for p in range(SLAB):
        for slab in range(2):
            slabs[slab, p * GY : (p + 1) * GY, :] = joined(slab, p)
    upper = lax.axis_index("row") // HALF
    line = lax.broadcasted_iota(jnp.int32, (4, GZ), 0)
    tile = jnp.where(line == 0, panel[0:4], 0.0).astype(BF16)
    for half in range(2):
        slab = upper ^ half
        for col in range(COLS):
            member = half * COLS + col
            for k in range(PIECE):
                at = 4 * (PIECE * col + k)
                out[member, k] = slabs[slab, at : at + 4, :].astype(BF16)
            out[member, PIECE] = tile


def rotate_kernel(received, panel_rows, out, states, wanted, rotated):
    members = 2 * COLS
    size = 4 * members
    for member in range(members):
        at = slice(4 * member, 4 * member + 4)
        for k in range(PIECE):
            states[at, k * GZ : (k + 1) * GZ] = received[member, k].astype(F32)
        tile = received[member, PIECE].astype(F32)
        wanted[at, :] = jnp.broadcast_to(tile[0:1], (4, GZ))
    order = lax.broadcasted_iota(jnp.int32, (size, 64), 0) >> 2
    state_of = 2 * (order & (COLS - 1)) + lax.shift_right_logical(order, 5)
    stored = jnp.where(panel_rows[...] == state_of, 1.0, 0.0).astype(BF16)
    spread = lax.dot_general(
        wanted[:, 0:64].astype(BF16), stored, (((1,), (1,)), ((), ())),
        preferred_element_type=F32,
    )
    same = (
        lax.broadcasted_iota(jnp.int32, (size, size), 0) & 3
    ) == (lax.broadcasted_iota(jnp.int32, (size, size), 1) & 3)
    spread = jnp.where(same, spread, 0.0).astype(BF16)
    rotated[...] = jnp.dot(spread, states[...].astype(BF16), preferred_element_type=F32)
    for col in range(COLS):
        for state in range(2):
            at = 4 * (state * COLS + col)
            for k in range(PIECE):
                out[col, state * PIECE + k] = rotated[
                    at : at + 4, k * GZ : (k + 1) * GZ
                ].astype(BF16)


def place_kernel(received, out):
    for col in range(COLS):
        for state in range(2):
            for k in range(PIECE):
                at = 4 * (PIECE * col + k)
                out[state, at : at + 4, :] = received[col, state * PIECE + k].astype(F32)


def per_device(orbitals, potential, proj_points, projector, strength, ritz_panel, panel_rows):
    shape = jax.ShapeDtypeStruct
    slabs_f32 = shape((2, SLAB, GY, GZ), F32)
    slabs_bf16 = shape((2, SLAB, GY, GZ), BF16)
    dense_gains = (shape((ATOM_DEV, SLAB_ROWS, GZ), F32), shape((ATOM_DEV, GZ), F32))
    along_z, along_y = stencil_matrices()
    smem = pl.BlockSpec(memory_space=pltpu.SMEM)
    work = [
        pltpu.VMEM((ATOM_DEV, SLAB_ROWS, GZ), F32),
        pltpu.VMEM((2 * SLAB_ROWS, 2 * GZ), BF16),
        pltpu.VMEM((2 * SLAB_ROWS, 2 * GZ), F32),
    ]
    around = [(i, i // HALF * HALF + (i + 1) % HALF) for i in range(ROWS)]

    packed = call(
        pack_kernel,
        shape((ROWS, SENT, YPART, GZ), BF16),
        scratch=[
            pltpu.VMEM((2, GX, YPART, GZ), BF16),
            pltpu.VMEM((2, YPART), BF16),
            pltpu.SemaphoreType.DMA((3,)),
        ],
        specs=[pl.BlockSpec(memory_space=pl.ANY)] * 2,
        vmem=60 * MIB,
    )(orbitals, ritz_panel.T)
    regrouped = lax.all_to_all(packed, "row", split_axis=0, concat_axis=0, tiled=True)
    given = call(
        other_kernel,
        shape((OTHER_ROWS, GZ), F32),
        specs=[VMEM] * 3 + [smem],
        flops=1_000_000,
        bytes_accessed=400_000,
    )(potential, proj_points, projector, strength)
    other = lax.ppermute(given, "row", [(i, i ^ HALF) for i in range(ROWS)])
    dense, gains = call(
        project_kernel,
        dense_gains,
        specs=[VMEM, VMEM, smem],
        flops=1_000_000_000,
        bytes_accessed=1_600_000,
    )(proj_points, projector, strength)
    fixed = (potential, other, dense, gains, along_z, along_y)
    previous, current, sent, panel = call(
        first_kernel,
        (slabs_f32, slabs_f32, slabs_bf16, shape((8, GZ), F32)),
        scratch=[pltpu.VMEM((2, WIDE, GY, GZ), F32)] + work,
        specs=[VMEM] * 7,
    )(regrouped, *fixed)
    for step in range(2):
        above = lax.ppermute(sent, "row", [(d, s) for s, d in around])
        below = lax.ppermute(sent, "row", around)
        partial = call(
            inside_kernel,
            slabs_f32,
            scratch=work,
            specs=[VMEM] * 8,
            flops=2_000_000_000,
            bytes_accessed=3_000_000,
        )(current, previous, *fixed)
        if step == 0:
            previous = current
            current, sent = call(join_kernel, (slabs_f32, slabs_bf16), specs=[VMEM] * 3)(
                partial, above, below
            )
    layered = call(
        last_kernel,
        shape((2 * COLS, PIECE + 1, 4, GZ), BF16),
        scratch=[pltpu.VMEM((2, SLAB_ROWS, GZ), F32)],
        specs=[VMEM] * 4,
    )(partial, above, below, panel)
    both = [
        [(i + HALF * half) * COLS + col for half in range(2) for col in range(COLS)]
        for i in range(HALF)
    ]
    columns = lax.all_to_all(
        layered, ("row", "col"), split_axis=0, concat_axis=0, tiled=True, axis_index_groups=both
    )
    turned = call(
        rotate_kernel,
        shape((COLS, 2 * PIECE, 4, GZ), BF16),
        scratch=[
            pltpu.VMEM((8 * COLS, PIECE * GZ), F32),
            pltpu.VMEM((8 * COLS, GZ), F32),
            pltpu.VMEM((8 * COLS, PIECE * GZ), F32),
        ],
        specs=[VMEM] * 2,
    )(columns, panel_rows.reshape(1, -1))
    result = lax.all_to_all(turned, "col", split_axis=0, concat_axis=0, tiled=True)
    whole = call(place_kernel, shape((2, SLAB_ROWS, GZ), F32), specs=[VMEM])(result)
    return whole.reshape(2, SLAB, GY, GZ)


def solution(mesh):
    placed = (
        P("col", None, "row", None),
        P("row", None, None),
        P("row", None),
        P("row", None),
        P("row"),
        P("row", "col"),
        P(),
    )
    return jax.shard_map(
        per_device,
        mesh=mesh,
        in_specs=placed,
        out_specs=P("col", "row", None, None),
        check_vma=False,
    )
```

```python
import functools

import jax
import jax.numpy as jnp
import numpy as np
from jax import lax
from jax.experimental import pallas as pl
from jax.experimental.pallas import tpu as pltpu
from jax.sharding import PartitionSpec as P

F32 = jnp.float32
BF16 = jnp.bfloat16

STENCIL = (
    -5369.0 / 1800.0,
    12.0 / 7.0,
    -15.0 / 56.0,
    10.0 / 189.0,
    -1.0 / 112.0,
    2.0 / 1925.0,
    -1.0 / 16632.0,
)
CENTER = 7.0
HALF_WIDTH = 5.0

ROWS, COLS = 16, 32
SLAB, GY, GZ = 6, 64, 128
GX = ROWS * SLAB
YPART = GY // ROWS
WIDE = 3 * SLAB
ATOM_DEV = 8
SLAB_ROWS = SLAB * GY
SENT = 2 * WIDE + 1
HALF = ROWS // 2
PIECE = SLAB_ROWS // COLS // 4
OTHER_ROWS = SLAB_ROWS + 3 * ATOM_DEV

SIDE = tuple(-0.5 * c for c in STENCIL)
DIAGONAL = -0.5 * 3.0 * STENCIL[0] - CENTER

VMEM = pl.BlockSpec(memory_space=pltpu.VMEM)
MIB = 1024 * 1024


def circulant(size):
    whole = np.zeros((size, size), np.float32)
    for offset in range(1, 7):
        for i in range(size):
            whole[i, (i + offset) % size] += SIDE[offset]
            whole[i, (i - offset) % size] += SIDE[offset]
    high = whole.astype(jnp.bfloat16)
    low = (whole - high.astype(np.float32)).astype(jnp.bfloat16)
    return high, low


def stencil_matrices():
    high, low = circulant(GZ)
    along_z = np.block([[high, low], [high, low]])
    high, low = circulant(GY)
    along_y = np.block([[high, high], [low, low]])
    return jnp.asarray(along_z), jnp.asarray(along_y)


def call(kernel, outs, scratch=(), flops=0, bytes_accessed=0, specs=None, vmem=12 * MIB):
    return pl.pallas_call(
        kernel,
        out_shape=outs,
        in_specs=specs,
        out_specs=jax.tree.map(lambda _: VMEM, outs),
        scratch_shapes=list(scratch),
        compiler_params=pltpu.CompilerParams(vmem_limit_bytes=vmem),
        cost_estimate=pl.CostEstimate(
            flops=flops, bytes_accessed=bytes_accessed, transcendentals=0
        ),
    )


def pack_kernel(orbitals, panel, out, states, columns, sems):
    copies = [
        pltpu.make_async_copy(source, target, sems.at[i])
        for i, (source, target) in enumerate(
            [
                (panel, columns),
                (orbitals.at[0], states.at[0]),
                (orbitals.at[1], states.at[1]),
            ]
        )
    ]
    for copy in copies:
        copy.start()
    row = lax.axis_index("row")
    place = lax.broadcasted_iota(jnp.int32, (2, GZ), 1)
    copies[0].wait()
    values = columns[...].astype(F32)
    tile = jnp.zeros((2, GZ), F32)
    for k in range(YPART):
        tile = jnp.where(place == YPART * row + k, values[:, k : k + 1], tile)
    tile = jnp.concatenate([tile, jnp.zeros((YPART - 2, GZ), F32)], axis=0).astype(BF16)
    for state in range(2):
        copies[1 + state].wait()
        for target in range(HALF * state, HALF * state + HALF):
            for index, slab in enumerate((target, target ^ HALF)):
                begin = (SLAB * slab - SLAB) % GX
                base = index * WIDE
                head = min(WIDE, GX - begin)
                out[target, base : base + head] = states[state, begin : begin + head]
                if head < WIDE:
                    out[target, base + head : base + WIDE] = states[state, : WIDE - head]
            out[target, 2 * WIDE] = tile


def other_kernel(potential, points, projector, strength, out):
    for p in range(SLAB):
        out[p * GY : (p + 1) * GY, :] = potential[p]
    out[SLAB_ROWS : SLAB_ROWS + 8, :] = points[...].astype(F32)
    out[SLAB_ROWS + 8 : SLAB_ROWS + 16, :] = projector[...]
    for atom in range(ATOM_DEV):
        at = SLAB_ROWS + 16 + atom
        out[at : at + 1, :] = jnp.full((1, GZ), strength[atom], F32)


def densify(points, projector, dense):
    grid_row, lane = lax.shift_right_logical(points, 7), points & (GZ - 1)
    high = projector.astype(BF16).astype(F32)
    parts = (high, projector - high)
    for atom in range(ATOM_DEV):
        rows = jnp.where(
            lax.broadcasted_iota(jnp.int32, (SLAB_ROWS, GZ), 0) == grid_row[atom : atom + 1, :],
            1.0,
            0.0,
        ).astype(BF16)
        at_lane = lax.broadcasted_iota(jnp.int32, (GZ, GZ), 0) == lane[atom : atom + 1, :]
        lanes = [
            jnp.where(at_lane, part[atom : atom + 1, :], 0.0).astype(BF16) for part in parts
        ]
        dense[atom] = lax.dot_general(
            jnp.concatenate([rows] * 2, axis=1),
            jnp.concatenate(lanes, axis=1),
            (((1,), (1,)), ((), ())),
            preferred_element_type=F32,
        )


def project_kernel(points, projector, strength, dense, gains):
    densify(points[...], projector[...], dense)
    for atom in range(ATOM_DEV):
        gains[atom : atom + 1, :] = jnp.full((1, GZ), strength[atom], F32)


def other_projectors(given, dense):
    points = given[SLAB_ROWS : SLAB_ROWS + 8, :].astype(jnp.int32)
    densify(points, given[SLAB_ROWS + 8 : SLAB_ROWS + 16, :], dense)
    return given.at[SLAB_ROWS + 16 : SLAB_ROWS + 24]


def apply(planes, reach, scale, potentials, denses, gains, along_z, along_y, wide_z, summed_z, emit):
    weights = []
    for slab in range(2):
        partial = [None] * ATOM_DEV
        for p in range(SLAB):
            value = planes(slab, p)
            high = value.astype(BF16)
            low = (value - high.astype(F32)).astype(BF16)
            start = (slab * SLAB + p) * GY
            wide_z[start : start + GY, 0:GZ] = high
            wide_z[start : start + GY, GZ : 2 * GZ] = low
            for atom in range(ATOM_DEV):
                weight = denses[slab][atom, p * GY : (p + 1) * GY, :]
                term = jnp.sum((weight * value).reshape(GY // 8, 8, GZ), axis=0)
                partial[atom] = term if p == 0 else partial[atom] + term
        lines = [jnp.sum(term, axis=0, keepdims=True) for term in partial]
        total = jnp.sum(jnp.concatenate(lines, axis=0), axis=1, keepdims=True)
        weights.append(total * gains[slab][...])
    summed_z[...] = jnp.dot(wide_z[...], along_z[...], preferred_element_type=F32)
    for p in range(SLAB):
        both = jnp.concatenate(
            [
                jnp.concatenate(
                    [
                        wide_z[start : start + GY, 0:GZ],
                        wide_z[start : start + GY, GZ : 2 * GZ],
                    ],
                    axis=0,
                )
                for start in (p * GY, (SLAB + p) * GY)
            ],
            axis=1,
        )
        turned = jnp.dot(along_y[...], both, preferred_element_type=F32)
        turned = turned[:GY] + turned[GY:]
        for slab in range(2):
            start = (slab * SLAB + p) * GY
            level = DIAGONAL + potentials[slab](p)
            total = level * planes(slab, p) + turned[:, slab * GZ : (slab + 1) * GZ]
            total = total + (
                summed_z[start : start + GY, 0:GZ] + summed_z[start : start + GY, GZ : 2 * GZ]
            )
            for atom in range(ATOM_DEV):
                total = (
                    total
                    + weights[slab][atom : atom + 1, :]
                    * denses[slab][atom, p * GY : (p + 1) * GY, :]
                )
            for offset in range(1, 7):
                terms = [
                    planes(slab, k)
                    for k in (p - offset, p + offset)
                    if -reach <= k < SLAB + reach
                ]
                if terms:
                    total = total + SIDE[offset] * functools.reduce(jnp.add, terms)
            emit(slab, p, scale * total)


def potentials_of(own, other):
    return (lambda p: own[p]), (lambda p: other[p * GY : (p + 1) * GY, :])


def first_kernel(
    received, potential, other, dense, gains, along_z, along_y,
    start_out, next_out, sent_out, panel_out, slabs, other_dense, wide_z, summed_z,
):
    other_gains = other_projectors(other, other_dense)
    panel = jnp.zeros((YPART, GZ), F32)
    for source in range(ROWS):
        for slab in range(2):
            slabs[slab, :, source * YPART : (source + 1) * YPART, :] = received[
                source, slab * WIDE : (slab + 1) * WIDE
            ].astype(F32)
        panel = panel + received[source, 2 * WIDE].astype(F32)
    mine = jnp.where(lax.axis_index("row") < HALF, panel[0:1], panel[1:2])
    panel_out[...] = jnp.broadcast_to(mine, (8, GZ))
    for slab in range(2):
        start_out[slab] = slabs[slab, SLAB : 2 * SLAB]

    def emit(slab, p, value):
        next_out[slab, p] = value
        sent_out[slab, p] = value.astype(BF16)

    apply(
        lambda slab, p: slabs[slab, SLAB + p], SLAB, 1.0 / HALF_WIDTH,
        potentials_of(potential, other), (dense, other_dense), (gains, other_gains),
        along_z, along_y, wide_z, summed_z, emit,
    )


def inside_kernel(
    current, previous, potential, other, dense, gains, along_z, along_y,
    out, other_dense, wide_z, summed_z,
):
    other_gains = other_projectors(other, other_dense)

    def emit(slab, p, value):
        out[slab, p] = value - previous[slab, p]

    apply(
        lambda slab, p: current[slab, p], 0, 2.0 / HALF_WIDTH,
        potentials_of(potential, other), (dense, other_dense), (gains, other_gains),
        along_z, along_y, wide_z, summed_z, emit,
    )


def joining(partial, below, above):
    column = lax.axis_index("row") & (HALF - 1)
    lower = jnp.where(column == 0, 1, 0)
    upper = jnp.where(column == HALF - 1, 1, 0)

    def joined(slab, p):
        total = partial[slab, p]
        lower_slab = lower ^ slab
        upper_slab = upper ^ slab
        for offset in range(1, 7):
            terms = []
            if p - offset < 0:
                terms.append(below[lower_slab, SLAB + p - offset].astype(F32))
            if p + offset >= SLAB:
                terms.append(above[upper_slab, p + offset - SLAB].astype(F32))
            if terms:
                side = (2.0 / HALF_WIDTH) * SIDE[offset]
                total = total + side * functools.reduce(jnp.add, terms)
        return total

    return joined


def by_parity(body, first, second):
    even = (lax.axis_index("row") & 1) == 0
    pl.when(even)(lambda: body(second, first))
    pl.when(jnp.logical_not(even))(lambda: body(first, second))


def join_kernel(partial, first, second, next_out, sent_out):
    def body(below, above):
        joined = joining(partial, below, above)
        for p in range(SLAB):
            for slab in range(2):
                value = joined(slab, p)
                next_out[slab, p] = value
                sent_out[slab, p] = value.astype(BF16)

    by_parity(body, first, second)


def last_kernel(partial, first, second, panel, out, slabs):
    def body(below, above):
        joined = joining(partial, below, above)
        for p in range(SLAB):
            for slab in range(2):
                slabs[slab, p * GY : (p + 1) * GY, :] = joined(slab, p)

    by_parity(body, first, second)
    upper = lax.axis_index("row") // HALF
    line = lax.broadcasted_iota(jnp.int32, (4, GZ), 0)
    tile = jnp.where(line == 0, panel[0:4], 0.0).astype(BF16)
    for half in range(2):
        slab = upper ^ half
        for col in range(COLS):
            member = half * COLS + col
            for k in range(PIECE):
                at = 4 * (PIECE * col + k)
                out[member, k] = slabs[slab, at : at + 4, :].astype(BF16)
            out[member, PIECE] = tile


def rotate_kernel(received, panel_rows, out, states, wanted, rotated):
    members = 2 * COLS
    size = 4 * members
    for member in range(members):
        at = slice(4 * member, 4 * member + 4)
        for k in range(PIECE):
            states[at, k * GZ : (k + 1) * GZ] = received[member, k].astype(F32)
        tile = received[member, PIECE].astype(F32)
        wanted[at, :] = jnp.broadcast_to(tile[0:1], (4, GZ))
    order = lax.broadcasted_iota(jnp.int32, (size, 64), 0) >> 2
    state_of = 2 * (order & (COLS - 1)) + lax.shift_right_logical(order, 5)
    stored = jnp.where(panel_rows[...] == state_of, 1.0, 0.0).astype(BF16)
    spread = lax.dot_general(
        wanted[:, 0:64].astype(BF16), stored, (((1,), (1,)), ((), ())),
        preferred_element_type=F32,
    )
    same = (
        lax.broadcasted_iota(jnp.int32, (size, size), 0) & 3
    ) == (lax.broadcasted_iota(jnp.int32, (size, size), 1) & 3)
    spread = jnp.where(same, spread, 0.0).astype(BF16)
    rotated[...] = jnp.dot(spread, states[...].astype(BF16), preferred_element_type=F32)
    for col in range(COLS):
        for state in range(2):
            at = 4 * (state * COLS + col)
            for k in range(PIECE):
                out[col, state * PIECE + k] = rotated[
                    at : at + 4, k * GZ : (k + 1) * GZ
                ].astype(BF16)


def place_kernel(received, out):
    for col in range(COLS):
        for state in range(2):
            for k in range(PIECE):
                at = 4 * (PIECE * col + k)
                out[state, at : at + 4, :] = received[col, state * PIECE + k].astype(F32)


def per_device(orbitals, potential, proj_points, projector, strength, ritz_panel, panel_rows):
    shape = jax.ShapeDtypeStruct
    slabs_f32 = shape((2, SLAB, GY, GZ), F32)
    slabs_bf16 = shape((2, SLAB, GY, GZ), BF16)
    dense_gains = (shape((ATOM_DEV, SLAB_ROWS, GZ), F32), shape((ATOM_DEV, GZ), F32))
    along_z, along_y = stencil_matrices()
    smem = pl.BlockSpec(memory_space=pltpu.SMEM)
    work = [
        pltpu.VMEM((ATOM_DEV, SLAB_ROWS, GZ), F32),
        pltpu.VMEM((2 * SLAB_ROWS, 2 * GZ), BF16),
        pltpu.VMEM((2 * SLAB_ROWS, 2 * GZ), F32),
    ]
    around = [(i, i // HALF * HALF + (i + 1) % HALF) for i in range(ROWS)]

    packed = call(
        pack_kernel,
        shape((ROWS, SENT, YPART, GZ), BF16),
        scratch=[
            pltpu.VMEM((2, GX, YPART, GZ), BF16),
            pltpu.VMEM((2, YPART), BF16),
            pltpu.SemaphoreType.DMA((3,)),
        ],
        specs=[pl.BlockSpec(memory_space=pl.ANY)] * 2,
        vmem=60 * MIB,
    )(orbitals, ritz_panel.T)
    regrouped = lax.all_to_all(packed, "row", split_axis=0, concat_axis=0, tiled=True)
    given = call(
        other_kernel,
        shape((OTHER_ROWS, GZ), F32),
        specs=[VMEM] * 3 + [smem],
        flops=1_000_000,
        bytes_accessed=400_000,
    )(potential, proj_points, projector, strength)
    other = lax.ppermute(given, "row", [(i, i ^ HALF) for i in range(ROWS)])
    dense, gains = call(
        project_kernel,
        dense_gains,
        specs=[VMEM, VMEM, smem],
        flops=1_000_000_000,
        bytes_accessed=1_600_000,
    )(proj_points, projector, strength)
    fixed = (potential, other, dense, gains, along_z, along_y)
    previous, current, sent, panel = call(
        first_kernel,
        (slabs_f32, slabs_f32, slabs_bf16, shape((8, GZ), F32)),
        scratch=[pltpu.VMEM((2, WIDE, GY, GZ), F32)] + work,
        specs=[VMEM] * 7,
    )(regrouped, *fixed)
    for step in range(2):
        first = lax.ppermute(sent, "row", [(i, i ^ 1) for i in range(ROWS)])
        second = lax.ppermute(
            sent, "row", [pair for s, d in around if s % 2 for pair in ((s, d), (d, s))]
        )
        partial = call(
            inside_kernel,
            slabs_f32,
            scratch=work,
            specs=[VMEM] * 8,
            flops=2_000_000_000,
            bytes_accessed=3_000_000,
        )(current, previous, *fixed)
        if step == 0:
            previous = current
            current, sent = call(join_kernel, (slabs_f32, slabs_bf16), specs=[VMEM] * 3)(
                partial, first, second
            )
    layered = call(
        last_kernel,
        shape((2 * COLS, PIECE + 1, 4, GZ), BF16),
        scratch=[pltpu.VMEM((2, SLAB_ROWS, GZ), F32)],
        specs=[VMEM] * 4,
    )(partial, first, second, panel)
    both = [
        [(i + HALF * half) * COLS + col for half in range(2) for col in range(COLS)]
        for i in range(HALF)
    ]
    columns = lax.all_to_all(
        layered, ("row", "col"), split_axis=0, concat_axis=0, tiled=True, axis_index_groups=both
    )
    turned = call(
        rotate_kernel,
        shape((COLS, 2 * PIECE, 4, GZ), BF16),
        scratch=[
            pltpu.VMEM((8 * COLS, PIECE * GZ), F32),
            pltpu.VMEM((8 * COLS, GZ), F32),
            pltpu.VMEM((8 * COLS, PIECE * GZ), F32),
        ],
        specs=[VMEM] * 2,
    )(columns, panel_rows.reshape(1, -1))
    result = lax.all_to_all(turned, "col", split_axis=0, concat_axis=0, tiled=True)
    whole = call(place_kernel, shape((2, SLAB_ROWS, GZ), F32), specs=[VMEM])(result)
    return whole.reshape(2, SLAB, GY, GZ)


def solution(mesh):
    placed = (
        P("col", None, "row", None),
        P("row", None, None),
        P("row", None),
        P("row", None),
        P("row"),
        P("row", "col"),
        P(),
    )
    return jax.shard_map(
        per_device,
        mesh=mesh,
        in_specs=placed,
        out_specs=P("col", "row", None, None),
        check_vma=False,
    )
```

```python
import functools

import jax
import jax.numpy as jnp
import numpy as np
from jax import lax
from jax.experimental import pallas as pl
from jax.experimental.pallas import tpu as pltpu
from jax.sharding import PartitionSpec as P

F32 = jnp.float32
BF16 = jnp.bfloat16

STENCIL = (
    -5369.0 / 1800.0,
    12.0 / 7.0,
    -15.0 / 56.0,
    10.0 / 189.0,
    -1.0 / 112.0,
    2.0 / 1925.0,
    -1.0 / 16632.0,
)
CENTER = 7.0
HALF_WIDTH = 5.0

ROWS, COLS = 16, 32
SLAB, GY, GZ = 6, 64, 128
GX = ROWS * SLAB
YPART = GY // ROWS
WIDE = 3 * SLAB
ATOM_DEV = 8
SLAB_ROWS = SLAB * GY
SENT = 2 * WIDE + 1
HALF = ROWS // 2
PIECE = SLAB_ROWS // COLS // 4
OTHER_ROWS = SLAB_ROWS + 3 * ATOM_DEV

SIDE = tuple(-0.5 * c for c in STENCIL)
DIAGONAL = -0.5 * 3.0 * STENCIL[0] - CENTER

VMEM = pl.BlockSpec(memory_space=pltpu.VMEM)
MIB = 1024 * 1024


def circulant(size):
    whole = np.zeros((size, size), np.float32)
    for offset in range(1, 7):
        for i in range(size):
            whole[i, (i + offset) % size] += SIDE[offset]
            whole[i, (i - offset) % size] += SIDE[offset]
    high = whole.astype(jnp.bfloat16)
    low = (whole - high.astype(np.float32)).astype(jnp.bfloat16)
    return high, low


def stencil_matrices():
    high, low = circulant(GZ)
    along_z = np.block([[high, low], [high, low]])
    high, low = circulant(GY)
    along_y = np.block([[high, high], [low, low]])
    return jnp.asarray(along_z), jnp.asarray(along_y)


def call(kernel, outs, scratch=(), flops=0, bytes_accessed=0, specs=None, vmem=12 * MIB):
    return pl.pallas_call(
        kernel,
        out_shape=outs,
        in_specs=specs,
        out_specs=jax.tree.map(lambda _: VMEM, outs),
        scratch_shapes=list(scratch),
        compiler_params=pltpu.CompilerParams(vmem_limit_bytes=vmem),
        cost_estimate=pl.CostEstimate(
            flops=flops, bytes_accessed=bytes_accessed, transcendentals=0
        ),
    )


def pack_kernel(orbitals, panel, out, states, columns, sems):
    copies = [
        pltpu.make_async_copy(source, target, sems.at[i])
        for i, (source, target) in enumerate(
            [
                (panel, columns),
                (orbitals.at[0], states.at[0]),
                (orbitals.at[1], states.at[1]),
            ]
        )
    ]
    for copy in copies:
        copy.start()
    row = lax.axis_index("row")
    place = lax.broadcasted_iota(jnp.int32, (2, GZ), 1)
    copies[0].wait()
    values = columns[...].astype(F32)
    tile = jnp.zeros((2, GZ), F32)
    for k in range(YPART):
        tile = jnp.where(place == YPART * row + k, values[:, k : k + 1], tile)
    tile = jnp.concatenate([tile, jnp.zeros((YPART - 2, GZ), F32)], axis=0).astype(BF16)
    for state in range(2):
        copies[1 + state].wait()
        for target in range(HALF * state, HALF * state + HALF):
            for index, slab in enumerate((target, target ^ HALF)):
                begin = (SLAB * slab - SLAB) % GX
                base = index * WIDE
                head = min(WIDE, GX - begin)
                out[target, base : base + head] = states[state, begin : begin + head]
                if head < WIDE:
                    out[target, base + head : base + WIDE] = states[state, : WIDE - head]
            out[target, 2 * WIDE] = tile


def other_kernel(potential, points, projector, strength, out):
    for p in range(SLAB):
        out[p * GY : (p + 1) * GY, :] = potential[p]
    out[SLAB_ROWS : SLAB_ROWS + 8, :] = points[...].astype(F32)
    out[SLAB_ROWS + 8 : SLAB_ROWS + 16, :] = projector[...]
    for atom in range(ATOM_DEV):
        at = SLAB_ROWS + 16 + atom
        out[at : at + 1, :] = jnp.full((1, GZ), strength[atom], F32)


def densify(points, projector, dense):
    grid_row, lane = lax.shift_right_logical(points, 7), points & (GZ - 1)
    high = projector.astype(BF16).astype(F32)
    parts = (high, projector - high)
    for atom in range(ATOM_DEV):
        rows = jnp.where(
            lax.broadcasted_iota(jnp.int32, (SLAB_ROWS, GZ), 0) == grid_row[atom : atom + 1, :],
            1.0,
            0.0,
        ).astype(BF16)
        at_lane = lax.broadcasted_iota(jnp.int32, (GZ, GZ), 0) == lane[atom : atom + 1, :]
        lanes = [
            jnp.where(at_lane, part[atom : atom + 1, :], 0.0).astype(BF16) for part in parts
        ]
        dense[atom] = lax.dot_general(
            jnp.concatenate([rows] * 2, axis=1),
            jnp.concatenate(lanes, axis=1),
            (((1,), (1,)), ((), ())),
            preferred_element_type=F32,
        )


def project_kernel(points, projector, strength, dense, gains):
    densify(points[...], projector[...], dense)
    for atom in range(ATOM_DEV):
        gains[atom : atom + 1, :] = jnp.full((1, GZ), strength[atom], F32)


def other_projectors(given, dense):
    points = given[SLAB_ROWS : SLAB_ROWS + 8, :].astype(jnp.int32)
    densify(points, given[SLAB_ROWS + 8 : SLAB_ROWS + 16, :], dense)
    return given.at[SLAB_ROWS + 16 : SLAB_ROWS + 24]


def apply(planes, reach, scale, potentials, denses, gains, along_z, along_y, wide_z, summed_z, emit):
    weights = []
    for slab in range(2):
        partial = [None] * ATOM_DEV
        for p in range(SLAB):
            value = planes(slab, p)
            high = value.astype(BF16)
            low = (value - high.astype(F32)).astype(BF16)
            start = (slab * SLAB + p) * GY
            wide_z[start : start + GY, 0:GZ] = high
            wide_z[start : start + GY, GZ : 2 * GZ] = low
            for atom in range(ATOM_DEV):
                weight = denses[slab][atom, p * GY : (p + 1) * GY, :]
                term = jnp.sum((weight * value).reshape(GY // 8, 8, GZ), axis=0)
                partial[atom] = term if p == 0 else partial[atom] + term
        lines = [jnp.sum(term, axis=0, keepdims=True) for term in partial]
        total = jnp.sum(jnp.concatenate(lines, axis=0), axis=1, keepdims=True)
        weights.append(total * gains[slab][...])
    summed_z[...] = jnp.dot(wide_z[...], along_z[...], preferred_element_type=F32)
    for p in range(SLAB):
        both = jnp.concatenate(
            [
                jnp.concatenate(
                    [
                        wide_z[start : start + GY, 0:GZ],
                        wide_z[start : start + GY, GZ : 2 * GZ],
                    ],
                    axis=0,
                )
                for start in (p * GY, (SLAB + p) * GY)
            ],
            axis=1,
        )
        turned = jnp.dot(along_y[...], both, preferred_element_type=F32)
        turned = turned[:GY] + turned[GY:]
        for slab in range(2):
            start = (slab * SLAB + p) * GY
            level = DIAGONAL + potentials[slab](p)
            total = level * planes(slab, p) + turned[:, slab * GZ : (slab + 1) * GZ]
            total = total + (
                summed_z[start : start + GY, 0:GZ] + summed_z[start : start + GY, GZ : 2 * GZ]
            )
            for atom in range(ATOM_DEV):
                total = (
                    total
                    + weights[slab][atom : atom + 1, :]
                    * denses[slab][atom, p * GY : (p + 1) * GY, :]
                )
            for offset in range(1, 7):
                terms = [
                    planes(slab, k)
                    for k in (p - offset, p + offset)
                    if -reach <= k < SLAB + reach
                ]
                if terms:
                    total = total + SIDE[offset] * functools.reduce(jnp.add, terms)
            emit(slab, p, scale * total)


def potentials_of(own, other):
    return (lambda p: own[p]), (lambda p: other[p * GY : (p + 1) * GY, :])


def first_kernel(
    received, potential, other, dense, gains, along_z, along_y,
    start_out, next_out, sent_out, panel_out, slabs, other_dense, wide_z, summed_z,
):
    other_gains = other_projectors(other, other_dense)
    panel = jnp.zeros((YPART, GZ), F32)
    for source in range(ROWS):
        for slab in range(2):
            slabs[slab, :, source * YPART : (source + 1) * YPART, :] = received[
                source, slab * WIDE : (slab + 1) * WIDE
            ].astype(F32)
        panel = panel + received[source, 2 * WIDE].astype(F32)
    mine = jnp.where(lax.axis_index("row") < HALF, panel[0:1], panel[1:2])
    panel_out[...] = jnp.broadcast_to(mine, (8, GZ))
    for slab in range(2):
        start_out[slab] = slabs[slab, SLAB : 2 * SLAB]

    def emit(slab, p, value):
        next_out[slab, p] = value
        sent_out[slab, p] = value.astype(BF16)

    apply(
        lambda slab, p: slabs[slab, SLAB + p], SLAB, 1.0 / HALF_WIDTH,
        potentials_of(potential, other), (dense, other_dense), (gains, other_gains),
        along_z, along_y, wide_z, summed_z, emit,
    )


def inside_kernel(
    current, previous, potential, other, dense, gains, along_z, along_y,
    out, other_dense, wide_z, summed_z,
):
    other_gains = other_projectors(other, other_dense)

    def emit(slab, p, value):
        out[slab, p] = value - previous[slab, p]

    apply(
        lambda slab, p: current[slab, p], 0, 2.0 / HALF_WIDTH,
        potentials_of(potential, other), (dense, other_dense), (gains, other_gains),
        along_z, along_y, wide_z, summed_z, emit,
    )


def joining(partial, below, above):
    column = lax.axis_index("row") & (HALF - 1)
    lower = jnp.where(column == 0, 1, 0)
    upper = jnp.where(column == HALF - 1, 1, 0)

    def joined(slab, p):
        total = partial[slab, p]
        lower_slab = lower ^ slab
        upper_slab = upper ^ slab
        for offset in range(1, 7):
            terms = []
            if p - offset < 0:
                terms.append(below[lower_slab, SLAB + p - offset].astype(F32))
            if p + offset >= SLAB:
                terms.append(above[upper_slab, p + offset - SLAB].astype(F32))
            if terms:
                side = (2.0 / HALF_WIDTH) * SIDE[offset]
                total = total + side * functools.reduce(jnp.add, terms)
        return total

    return joined


def by_parity(body, first, second):
    even = (lax.axis_index("row") & 1) == 0
    pl.when(even)(lambda: body(second, first))
    pl.when(jnp.logical_not(even))(lambda: body(first, second))


def join_kernel(partial, first, second, next_out, sent_out):
    def body(below, above):
        joined = joining(partial, below, above)
        for p in range(SLAB):
            for slab in range(2):
                value = joined(slab, p)
                next_out[slab, p] = value
                sent_out[slab, p] = value.astype(BF16)

    by_parity(body, first, second)


def last_kernel(partial, first, second, panel, out, slabs):
    def body(below, above):
        joined = joining(partial, below, above)
        for p in range(SLAB):
            for slab in range(2):
                slabs[slab, p * GY : (p + 1) * GY, :] = joined(slab, p)

    by_parity(body, first, second)
    upper = lax.axis_index("row") // HALF
    line = lax.broadcasted_iota(jnp.int32, (2, GZ), 0)
    tile = jnp.where(line == 0, panel[0:2], 0.0).astype(BF16)
    for half in range(2):
        slab = upper ^ half
        for col in range(COLS):
            member = half * COLS + col
            for k in range(2 * PIECE):
                at = 2 * (2 * PIECE * col + k)
                out[member, k] = slabs[slab, at : at + 2, :].astype(BF16)
            out[member, 2 * PIECE] = tile


def rotate_kernel(received, panel_rows, out, states, wanted, rotated):
    members = 2 * COLS
    size = 4 * members
    for member in range(members):
        at = slice(4 * member, 4 * member + 4)
        for k in range(2 * PIECE):
            half = 4 * member + 2 * (k % 2)
            states[half : half + 2, k // 2 * GZ : (k // 2 + 1) * GZ] = received[member, k].astype(
                F32
            )
        tile = received[member, 2 * PIECE].astype(F32)
        wanted[at, :] = jnp.broadcast_to(tile[0:1], (4, GZ))
    order = lax.broadcasted_iota(jnp.int32, (size, 64), 0) >> 2
    state_of = 2 * (order & (COLS - 1)) + lax.shift_right_logical(order, 5)
    stored = jnp.where(panel_rows[...] == state_of, 1.0, 0.0).astype(BF16)
    spread = lax.dot_general(
        wanted[:, 0:64].astype(BF16), stored, (((1,), (1,)), ((), ())),
        preferred_element_type=F32,
    )
    same = (
        lax.broadcasted_iota(jnp.int32, (size, size), 0) & 3
    ) == (lax.broadcasted_iota(jnp.int32, (size, size), 1) & 3)
    spread = jnp.where(same, spread, 0.0).astype(BF16)
    rotated[...] = jnp.dot(spread, states[...].astype(BF16), preferred_element_type=F32)
    for col in range(COLS):
        for state in range(2):
            at = 4 * (state * COLS + col)
            for k in range(PIECE):
                out[col, state * PIECE + k] = rotated[
                    at : at + 4, k * GZ : (k + 1) * GZ
                ].astype(BF16)


def place_kernel(received, out):
    for col in range(COLS):
        for state in range(2):
            for k in range(PIECE):
                at = 4 * (PIECE * col + k)
                out[state, at : at + 4, :] = received[col, state * PIECE + k].astype(F32)


def per_device(orbitals, potential, proj_points, projector, strength, ritz_panel, panel_rows):
    shape = jax.ShapeDtypeStruct
    slabs_f32 = shape((2, SLAB, GY, GZ), F32)
    slabs_bf16 = shape((2, SLAB, GY, GZ), BF16)
    dense_gains = (shape((ATOM_DEV, SLAB_ROWS, GZ), F32), shape((ATOM_DEV, GZ), F32))
    along_z, along_y = stencil_matrices()
    smem = pl.BlockSpec(memory_space=pltpu.SMEM)
    work = [
        pltpu.VMEM((ATOM_DEV, SLAB_ROWS, GZ), F32),
        pltpu.VMEM((2 * SLAB_ROWS, 2 * GZ), BF16),
        pltpu.VMEM((2 * SLAB_ROWS, 2 * GZ), F32),
    ]
    around = [(i, i // HALF * HALF + (i + 1) % HALF) for i in range(ROWS)]

    packed = call(
        pack_kernel,
        shape((ROWS, SENT, YPART, GZ), BF16),
        scratch=[
            pltpu.VMEM((2, GX, YPART, GZ), BF16),
            pltpu.VMEM((2, YPART), BF16),
            pltpu.SemaphoreType.DMA((3,)),
        ],
        specs=[pl.BlockSpec(memory_space=pl.ANY)] * 2,
        vmem=60 * MIB,
    )(orbitals, ritz_panel.T)
    regrouped = lax.all_to_all(packed, "row", split_axis=0, concat_axis=0, tiled=True)
    given = call(
        other_kernel,
        shape((OTHER_ROWS, GZ), F32),
        specs=[VMEM] * 3 + [smem],
        flops=1_000_000,
        bytes_accessed=400_000,
    )(potential, proj_points, projector, strength)
    other = lax.ppermute(given, "row", [(i, i ^ HALF) for i in range(ROWS)])
    dense, gains = call(
        project_kernel,
        dense_gains,
        specs=[VMEM, VMEM, smem],
        flops=1_000_000_000,
        bytes_accessed=1_600_000,
    )(proj_points, projector, strength)
    fixed = (potential, other, dense, gains, along_z, along_y)
    previous, current, sent, panel = call(
        first_kernel,
        (slabs_f32, slabs_f32, slabs_bf16, shape((8, GZ), F32)),
        scratch=[pltpu.VMEM((2, WIDE, GY, GZ), F32)] + work,
        specs=[VMEM] * 7,
    )(regrouped, *fixed)
    for step in range(2):
        first = lax.ppermute(sent, "row", [(i, i ^ 1) for i in range(ROWS)])
        second = lax.ppermute(
            sent, "row", [pair for s, d in around if s % 2 for pair in ((s, d), (d, s))]
        )
        partial = call(
            inside_kernel,
            slabs_f32,
            scratch=work,
            specs=[VMEM] * 8,
            flops=2_000_000_000,
            bytes_accessed=3_000_000,
        )(current, previous, *fixed)
        if step == 0:
            previous = current
            current, sent = call(join_kernel, (slabs_f32, slabs_bf16), specs=[VMEM] * 3)(
                partial, first, second
            )
    layered = call(
        last_kernel,
        shape((2 * COLS, 2 * PIECE + 1, 2, GZ), BF16),
        scratch=[pltpu.VMEM((2, SLAB_ROWS, GZ), F32)],
        specs=[VMEM] * 4,
    )(partial, first, second, panel)
    both = [
        [(i + HALF * half) * COLS + col for half in range(2) for col in range(COLS)]
        for i in range(HALF)
    ]
    columns = lax.all_to_all(
        layered, ("row", "col"), split_axis=0, concat_axis=0, tiled=True, axis_index_groups=both
    )
    turned = call(
        rotate_kernel,
        shape((COLS, 2 * PIECE, 4, GZ), BF16),
        scratch=[
            pltpu.VMEM((8 * COLS, PIECE * GZ), F32),
            pltpu.VMEM((8 * COLS, GZ), F32),
            pltpu.VMEM((8 * COLS, PIECE * GZ), F32),
        ],
        specs=[VMEM] * 2,
    )(columns, panel_rows.reshape(1, -1))
    result = lax.all_to_all(turned, "col", split_axis=0, concat_axis=0, tiled=True)
    whole = call(place_kernel, shape((2, SLAB_ROWS, GZ), F32), specs=[VMEM])(result)
    return whole.reshape(2, SLAB, GY, GZ)


def solution(mesh):
    placed = (
        P("col", None, "row", None),
        P("row", None, None),
        P("row", None),
        P("row", None),
        P("row"),
        P("row", "col"),
        P(),
    )
    return jax.shard_map(
        per_device,
        mesh=mesh,
        in_specs=placed,
        out_specs=P("col", "row", None, None),
        check_vma=False,
    )
```

```python
import functools

import jax
import jax.numpy as jnp
import numpy as np
from jax import lax
from jax.experimental import pallas as pl
from jax.experimental.pallas import tpu as pltpu
from jax.sharding import PartitionSpec as P

F32 = jnp.float32
BF16 = jnp.bfloat16

STENCIL = (
    -5369.0 / 1800.0,
    12.0 / 7.0,
    -15.0 / 56.0,
    10.0 / 189.0,
    -1.0 / 112.0,
    2.0 / 1925.0,
    -1.0 / 16632.0,
)
CENTER = 7.0
HALF_WIDTH = 5.0

ROWS, COLS = 16, 32
SLAB, GY, GZ = 6, 64, 128
GX = ROWS * SLAB
YPART = GY // ROWS
WIDE = 3 * SLAB
ATOM_DEV = 8
SLAB_ROWS = SLAB * GY
SENT = 2 * WIDE + 1
HALF = ROWS // 2
EARLY = 4
PIECE = SLAB_ROWS // COLS // 4
OTHER_ROWS = SLAB_ROWS + 3 * ATOM_DEV

SIDE = tuple(-0.5 * c for c in STENCIL)
DIAGONAL = -0.5 * 3.0 * STENCIL[0] - CENTER

VMEM = pl.BlockSpec(memory_space=pltpu.VMEM)
MIB = 1024 * 1024


def circulant(size):
    whole = np.zeros((size, size), np.float32)
    for offset in range(1, 7):
        for i in range(size):
            whole[i, (i + offset) % size] += SIDE[offset]
            whole[i, (i - offset) % size] += SIDE[offset]
    high = whole.astype(jnp.bfloat16)
    low = (whole - high.astype(np.float32)).astype(jnp.bfloat16)
    return high, low


def stencil_matrices():
    high, low = circulant(GZ)
    along_z = np.block([[high, low], [high, low]])
    high, low = circulant(GY)
    along_y = np.block([[high, high], [low, low]])
    return jnp.asarray(along_z), jnp.asarray(along_y)


def call(kernel, outs, scratch=(), flops=0, bytes_accessed=0, specs=None, vmem=12 * MIB):
    return pl.pallas_call(
        kernel,
        out_shape=outs,
        in_specs=specs,
        out_specs=jax.tree.map(lambda _: VMEM, outs),
        scratch_shapes=list(scratch),
        compiler_params=pltpu.CompilerParams(vmem_limit_bytes=vmem),
        cost_estimate=pl.CostEstimate(
            flops=flops, bytes_accessed=bytes_accessed, transcendentals=0
        ),
    )


def pack_kernel(orbitals, panel, out, states, columns, sems):
    copies = [
        pltpu.make_async_copy(source, target, sems.at[i])
        for i, (source, target) in enumerate(
            [
                (panel, columns),
                (orbitals.at[0], states.at[0]),
                (orbitals.at[1], states.at[1]),
            ]
        )
    ]
    for copy in copies:
        copy.start()
    row = lax.axis_index("row")
    place = lax.broadcasted_iota(jnp.int32, (2, GZ), 1)
    copies[0].wait()
    values = columns[...].astype(F32)
    tile = jnp.zeros((2, GZ), F32)
    for k in range(YPART):
        tile = jnp.where(place == YPART * row + k, values[:, k : k + 1], tile)
    tile = jnp.concatenate([tile, jnp.zeros((YPART - 2, GZ), F32)], axis=0).astype(BF16)
    for state in range(2):
        copies[1 + state].wait()
        for target in range(HALF * state, HALF * state + HALF):
            for index, slab in enumerate((target, target ^ HALF)):
                begin = (SLAB * slab - SLAB) % GX
                base = index * WIDE
                head = min(WIDE, GX - begin)
                out[target, base : base + head] = states[state, begin : begin + head]
                if head < WIDE:
                    out[target, base + head : base + WIDE] = states[state, : WIDE - head]
            out[target, 2 * WIDE] = tile


def other_kernel(potential, points, projector, strength, out):
    for p in range(SLAB):
        out[p * GY : (p + 1) * GY, :] = potential[p]
    out[SLAB_ROWS : SLAB_ROWS + 8, :] = points[...].astype(F32)
    out[SLAB_ROWS + 8 : SLAB_ROWS + 16, :] = projector[...]
    for atom in range(ATOM_DEV):
        at = SLAB_ROWS + 16 + atom
        out[at : at + 1, :] = jnp.full((1, GZ), strength[atom], F32)


def densify(points, projector, dense, atoms=range(ATOM_DEV)):
    grid_row, lane = lax.shift_right_logical(points, 7), points & (GZ - 1)
    high = projector.astype(BF16).astype(F32)
    parts = (high, projector - high)
    for atom in atoms:
        rows = jnp.where(
            lax.broadcasted_iota(jnp.int32, (SLAB_ROWS, GZ), 0) == grid_row[atom : atom + 1, :],
            1.0,
            0.0,
        ).astype(BF16)
        at_lane = lax.broadcasted_iota(jnp.int32, (GZ, GZ), 0) == lane[atom : atom + 1, :]
        lanes = [
            jnp.where(at_lane, part[atom : atom + 1, :], 0.0).astype(BF16) for part in parts
        ]
        dense[atom - atoms[0]] = lax.dot_general(
            jnp.concatenate([rows] * 2, axis=1),
            jnp.concatenate(lanes, axis=1),
            (((1,), (1,)), ((), ())),
            preferred_element_type=F32,
        )


def project_kernel(points, projector, strength, dense, gains):
    densify(points[...], projector[...], dense)
    for atom in range(ATOM_DEV):
        gains[atom : atom + 1, :] = jnp.full((1, GZ), strength[atom], F32)


def project_other_kernel(given, dense):
    points = given[SLAB_ROWS : SLAB_ROWS + 8, :].astype(jnp.int32)
    densify(points, given[SLAB_ROWS + 8 : SLAB_ROWS + 16, :], dense, range(EARLY))


def projectors_of(dense, gains, given, early, late):
    points = given[SLAB_ROWS : SLAB_ROWS + 8, :].astype(jnp.int32)
    densify(points, given[SLAB_ROWS + 8 : SLAB_ROWS + 16, :], late, range(EARLY, ATOM_DEV))

    def own(atom, rows):
        return dense[atom, rows, :]

    def other(atom, rows):
        return early[atom, rows, :] if atom < EARLY else late[atom - EARLY, rows, :]

    return (own, other), (gains, given.at[SLAB_ROWS + 16 : SLAB_ROWS + 24])


def apply(
    planes, reach, scale, exact, potentials, denses, gains, along_z, along_y, wide_z, summed_z, emit
):
    deep = GZ if exact else 2 * GZ
    weights = []
    for slab in range(2):
        partial = [None] * ATOM_DEV
        for p in range(SLAB):
            value = planes(slab, p)
            high = value.astype(BF16)
            start = (slab * SLAB + p) * GY
            wide_z[start : start + GY, 0:GZ] = high
            if not exact:
                low = (value - high.astype(F32)).astype(BF16)
                wide_z[start : start + GY, GZ : 2 * GZ] = low
            for atom in range(ATOM_DEV):
                weight = denses[slab](atom, slice(p * GY, (p + 1) * GY))
                term = jnp.sum((weight * value).reshape(GY // 8, 8, GZ), axis=0)
                partial[atom] = term if p == 0 else partial[atom] + term
        lines = [jnp.sum(term, axis=0, keepdims=True) for term in partial]
        total = jnp.sum(jnp.concatenate(lines, axis=0), axis=1, keepdims=True)
        weights.append(total * gains[slab][...])
    summed_z[...] = jnp.dot(
        wide_z[:, 0:deep], along_z[0:deep, :], preferred_element_type=F32
    )
    for p in range(SLAB):
        both = jnp.concatenate(
            [
                jnp.concatenate(
                    [
                        wide_z[start : start + GY, at : at + GZ]
                        for at in range(0, deep, GZ)
                    ],
                    axis=0,
                )
                for start in (p * GY, (SLAB + p) * GY)
            ],
            axis=1,
        )
        turned = jnp.dot(along_y[:, 0 : deep // 2], both, preferred_element_type=F32)
        turned = turned[:GY] + turned[GY:]
        for slab in range(2):
            start = (slab * SLAB + p) * GY
            level = DIAGONAL + potentials[slab](p)
            total = level * planes(slab, p) + turned[:, slab * GZ : (slab + 1) * GZ]
            total = total + (
                summed_z[start : start + GY, 0:GZ] + summed_z[start : start + GY, GZ : 2 * GZ]
            )
            for atom in range(ATOM_DEV):
                total = (
                    total
                    + weights[slab][atom : atom + 1, :]
                    * denses[slab](atom, slice(p * GY, (p + 1) * GY))
                )
            for offset in range(1, 7):
                terms = [
                    planes(slab, k)
                    for k in (p - offset, p + offset)
                    if -reach <= k < SLAB + reach
                ]
                if terms:
                    total = total + SIDE[offset] * functools.reduce(jnp.add, terms)
            emit(slab, p, scale * total)


def potentials_of(own, other):
    return (lambda p: own[p]), (lambda p: other[p * GY : (p + 1) * GY, :])


def first_kernel(
    received, potential, other, dense, gains, early, along_z, along_y,
    start_out, next_out, sent_out, panel_out, slabs, late, wide_z, summed_z,
):
    denses, all_gains = projectors_of(dense, gains, other, early, late)
    panel = jnp.zeros((YPART, GZ), F32)
    for source in range(ROWS):
        for slab in range(2):
            slabs[slab, :, source * YPART : (source + 1) * YPART, :] = received[
                source, slab * WIDE : (slab + 1) * WIDE
            ].astype(F32)
        panel = panel + received[source, 2 * WIDE].astype(F32)
    mine = jnp.where(lax.axis_index("row") < HALF, panel[0:1], panel[1:2])
    panel_out[...] = jnp.broadcast_to(mine, (8, GZ))
    for slab in range(2):
        start_out[slab] = slabs[slab, SLAB : 2 * SLAB]

    def emit(slab, p, value):
        next_out[slab, p] = value
        sent_out[slab, p] = value.astype(BF16)

    apply(
        lambda slab, p: slabs[slab, SLAB + p], SLAB, 1.0 / HALF_WIDTH, True,
        potentials_of(potential, other), denses, all_gains,
        along_z, along_y, wide_z, summed_z, emit,
    )


def inside_kernel(
    current, previous, potential, other, dense, gains, early, along_z, along_y,
    out, late, wide_z, summed_z,
):
    denses, all_gains = projectors_of(dense, gains, other, early, late)

    def emit(slab, p, value):
        out[slab, p] = value - previous[slab, p]

    apply(
        lambda slab, p: current[slab, p], 0, 2.0 / HALF_WIDTH, False,
        potentials_of(potential, other), denses, all_gains,
        along_z, along_y, wide_z, summed_z, emit,
    )


def joining(partial, below, above):
    column = lax.axis_index("row") & (HALF - 1)
    lower = jnp.where(column == 0, 1, 0)
    upper = jnp.where(column == HALF - 1, 1, 0)

    def joined(slab, p):
        total = partial[slab, p]
        lower_slab = lower ^ slab
        upper_slab = upper ^ slab
        for offset in range(1, 7):
            terms = []
            if p - offset < 0:
                terms.append(below[lower_slab, SLAB + p - offset].astype(F32))
            if p + offset >= SLAB:
                terms.append(above[upper_slab, p + offset - SLAB].astype(F32))
            if terms:
                side = (2.0 / HALF_WIDTH) * SIDE[offset]
                total = total + side * functools.reduce(jnp.add, terms)
        return total

    return joined


def by_parity(body, first, second):
    even = (lax.axis_index("row") & 1) == 0
    pl.when(even)(lambda: body(second, first))
    pl.when(jnp.logical_not(even))(lambda: body(first, second))


def join_kernel(partial, first, second, next_out, sent_out):
    def body(below, above):
        joined = joining(partial, below, above)
        for p in range(SLAB):
            for slab in range(2):
                value = joined(slab, p)
                next_out[slab, p] = value
                sent_out[slab, p] = value.astype(BF16)

    by_parity(body, first, second)


def last_kernel(partial, first, second, panel, out, slabs):
    def body(below, above):
        joined = joining(partial, below, above)
        for p in range(SLAB):
            for slab in range(2):
                slabs[slab, p * GY : (p + 1) * GY, :] = joined(slab, p)

    by_parity(body, first, second)
    upper = lax.axis_index("row") // HALF
    line = lax.broadcasted_iota(jnp.int32, (2, GZ), 0)
    tile = jnp.where(line == 0, panel[0:2], 0.0).astype(BF16)
    for half in range(2):
        slab = upper ^ half
        for col in range(COLS):
            member = half * COLS + col
            for k in range(2 * PIECE):
                at = 2 * (2 * PIECE * col + k)
                out[member, k] = slabs[slab, at : at + 2, :].astype(BF16)
            out[member, 2 * PIECE] = tile


def rotate_kernel(received, panel_rows, out, states, wanted, rotated):
    members = 2 * COLS
    size = 4 * members
    for member in range(members):
        at = slice(4 * member, 4 * member + 4)
        for k in range(2 * PIECE):
            half = 4 * member + 2 * (k % 2)
            states[half : half + 2, k // 2 * GZ : (k // 2 + 1) * GZ] = received[member, k].astype(
                F32
            )
        tile = received[member, 2 * PIECE].astype(F32)
        wanted[at, :] = jnp.broadcast_to(tile[0:1], (4, GZ))
    order = lax.broadcasted_iota(jnp.int32, (size, 64), 0) >> 2
    state_of = 2 * (order & (COLS - 1)) + lax.shift_right_logical(order, 5)
    stored = jnp.where(panel_rows[...] == state_of, 1.0, 0.0).astype(BF16)
    spread = lax.dot_general(
        wanted[:, 0:64].astype(BF16), stored, (((1,), (1,)), ((), ())),
        preferred_element_type=F32,
    )
    same = (
        lax.broadcasted_iota(jnp.int32, (size, size), 0) & 3
    ) == (lax.broadcasted_iota(jnp.int32, (size, size), 1) & 3)
    spread = jnp.where(same, spread, 0.0).astype(BF16)
    rotated[...] = jnp.dot(spread, states[...].astype(BF16), preferred_element_type=F32)
    for col in range(COLS):
        for state in range(2):
            at = 4 * (state * COLS + col)
            for k in range(PIECE):
                out[col, state * PIECE + k] = rotated[
                    at : at + 4, k * GZ : (k + 1) * GZ
                ].astype(BF16)


def place_kernel(received, out):
    for col in range(COLS):
        for state in range(2):
            for k in range(PIECE):
                at = 4 * (PIECE * col + k)
                out[state, at : at + 4, :] = received[col, state * PIECE + k].astype(F32)


def per_device(orbitals, potential, proj_points, projector, strength, ritz_panel, panel_rows):
    shape = jax.ShapeDtypeStruct
    slabs_f32 = shape((2, SLAB, GY, GZ), F32)
    slabs_bf16 = shape((2, SLAB, GY, GZ), BF16)
    dense_gains = (shape((ATOM_DEV, SLAB_ROWS, GZ), F32), shape((ATOM_DEV, GZ), F32))
    along_z, along_y = stencil_matrices()
    smem = pl.BlockSpec(memory_space=pltpu.SMEM)
    work = [
        pltpu.VMEM((ATOM_DEV - EARLY, SLAB_ROWS, GZ), F32),
        pltpu.VMEM((2 * SLAB_ROWS, 2 * GZ), BF16),
        pltpu.VMEM((2 * SLAB_ROWS, 2 * GZ), F32),
    ]
    around = [(i, i // HALF * HALF + (i + 1) % HALF) for i in range(ROWS)]

    packed = call(
        pack_kernel,
        shape((ROWS, SENT, YPART, GZ), BF16),
        scratch=[
            pltpu.VMEM((2, GX, YPART, GZ), BF16),
            pltpu.VMEM((2, YPART), BF16),
            pltpu.SemaphoreType.DMA((3,)),
        ],
        specs=[pl.BlockSpec(memory_space=pl.ANY)] * 2,
        vmem=60 * MIB,
    )(orbitals, ritz_panel.T)
    regrouped = lax.all_to_all(packed, "row", split_axis=0, concat_axis=0, tiled=True)
    given = call(
        other_kernel,
        shape((OTHER_ROWS, GZ), F32),
        specs=[VMEM] * 3 + [smem],
        flops=1_000_000,
        bytes_accessed=400_000,
    )(potential, proj_points, projector, strength)
    other = lax.ppermute(given, "row", [(i, i ^ HALF) for i in range(ROWS)])
    dense, gains = call(
        project_kernel,
        dense_gains,
        specs=[VMEM, VMEM, smem],
        flops=1_000_000_000,
        bytes_accessed=1_600_000,
    )(proj_points, projector, strength)
    early = call(
        project_other_kernel,
        shape((EARLY, SLAB_ROWS, GZ), F32),
        specs=[VMEM],
        flops=500_000_000,
        bytes_accessed=800_000,
    )(other)
    fixed = (potential, other, dense, gains, early, along_z, along_y)
    previous, current, sent, panel = call(
        first_kernel,
        (slabs_f32, slabs_f32, slabs_bf16, shape((8, GZ), F32)),
        scratch=[pltpu.VMEM((2, WIDE, GY, GZ), F32)] + work,
        specs=[VMEM] * 8,
    )(regrouped, *fixed)
    for step in range(2):
        first = lax.ppermute(sent, "row", [(i, i ^ 1) for i in range(ROWS)])
        second = lax.ppermute(
            sent, "row", [pair for s, d in around if s % 2 for pair in ((s, d), (d, s))]
        )
        partial = call(
            inside_kernel,
            slabs_f32,
            scratch=work,
            specs=[VMEM] * 9,
            flops=2_000_000_000,
            bytes_accessed=3_000_000,
        )(current, previous, *fixed)
        if step == 0:
            previous = current
            current, sent = call(join_kernel, (slabs_f32, slabs_bf16), specs=[VMEM] * 3)(
                partial, first, second
            )
    layered = call(
        last_kernel,
        shape((2 * COLS, 2 * PIECE + 1, 2, GZ), BF16),
        scratch=[pltpu.VMEM((2, SLAB_ROWS, GZ), F32)],
        specs=[VMEM] * 4,
    )(partial, first, second, panel)
    both = [
        [(i + HALF * half) * COLS + col for half in range(2) for col in range(COLS)]
        for i in range(HALF)
    ]
    columns = lax.all_to_all(
        layered, ("row", "col"), split_axis=0, concat_axis=0, tiled=True, axis_index_groups=both
    )
    turned = call(
        rotate_kernel,
        shape((COLS, 2 * PIECE, 4, GZ), BF16),
        scratch=[
            pltpu.VMEM((8 * COLS, PIECE * GZ), F32),
            pltpu.VMEM((8 * COLS, GZ), F32),
            pltpu.VMEM((8 * COLS, PIECE * GZ), F32),
        ],
        specs=[VMEM] * 2,
    )(columns, panel_rows.reshape(1, -1))
    result = lax.all_to_all(turned, "col", split_axis=0, concat_axis=0, tiled=True)
    whole = call(place_kernel, shape((2, SLAB_ROWS, GZ), F32), specs=[VMEM])(result)
    return whole.reshape(2, SLAB, GY, GZ)


def solution(mesh):
    placed = (
        P("col", None, "row", None),
        P("row", None, None),
        P("row", None),
        P("row", None),
        P("row"),
        P("row", "col"),
        P(),
    )
    return jax.shard_map(
        per_device,
        mesh=mesh,
        in_specs=placed,
        out_specs=P("col", "row", None, None),
        check_vma=False,
    )
```
